512 devices in a mesh: lat: 16 (over z_lo, y), lon: 32 (over z_hi, x, core).
Axes of the slice: x: 4, y: 4, z: 16 (z_hi: 4, z_lo: 4; z = z_hi * 4 + z_lo), core: 2. Of those that a mesh axis runs over, the one named last changes fastest.
Arguments:
- tracers: float32 [2, 24, 512, 4096], P(None, None, 'lat', 'lon'), may hold values from -6 to 6
- velocity: float32 [2, 24, 512, 4096], P(None, None, 'lat', 'lon'), may hold values from -6 to 6
- diffusivity: float32 [512, 4096], P('lat', 'lon'), may hold values from 0.05 to 5
- ocean_levels: int32 [512, 4096], P('lat', 'lon'), may hold values from 0 to 24, as said below
- surface_height: float32 [512, 4096], P('lat', 'lon'), may hold values from -6 to 6
- transport: float32 [2, 512, 4096], P(None, 'lat', 'lon'), may hold values from -6 to 6
- atm_flux: float32 [16, 4, 16384], P('lat', None, 'lon'), may hold values from -6 to 6
- send_rows: int32 [16, 32, 32, 64], P('lat', 'lon'), may hold values from 0 to 511
- src_owner: int32 [4, 512, 4096], P(None, 'lat', 'lon'), may hold values from 0 to 31
- src_slot: int32 [4, 512, 4096], P(None, 'lat', 'lon'), may hold values from 0 to 63
- xgrid_weights: float32 [4, 512, 4096], P(None, 'lat', 'lon'), may hold values from 0.1 to 1
- xgrid_count: int32 [512, 4096], P('lat', 'lon'), may hold values from 1 to 4
Outputs:
- tracers_out: float32 [2, 24, 512, 4096], P(None, None, 'lat', 'lon')
- height_out: float32 [512, 4096], P('lat', 'lon')
- transport_out: float32 [2, 512, 4096], P(None, 'lat', 'lon')
The draws below stay inside these ranges and needn't reach their ends.
Inputs may be any that keep to these rules, and one draw needn't show every extreme that they name: `ocean_levels`: 0 marks a land column.
All inputs are finite; a program needn't handle non-finite values.
Results may differ from the reference program's by a relative error of at most 0.0001.
Values sent between devices are 32-bit elements; how exact they have to be, the bound alone decides.
No kernel may reach another device: no remote copies, remote signals or barrier semaphores. Data moves between devices by JAX's collectives and lax.ppermute only.
A program may use at most 64 MiB of HBM per device.

```python
import math
import jax
import jax.numpy as jnp

CY = 32
CX = 128
LEV = 24
SUBSTEPS = 6
NFLUX = 4
KX = 4
SLOTS = 64
ATM_DEV = 512
NY = 512
NX = 4096
ATMS = 16384
N_LAT = 16
N_LON = 32


def draw_ocean_levels(key, part):
    key = jax.random.fold_in(key, 7)
    tile_key, roll_key, depth_key = jax.random.split(key, 3)
    land_share = jax.random.randint(tile_key, (NY // CY, NX // CX), 0, 90)
    land_cells = jnp.repeat(jnp.repeat(land_share, CY, axis=0), CX, axis=1)
    rolled = jax.random.randint(roll_key, (NY, NX), 0, 100)
    depth_cells = jax.random.randint(depth_key, (NY, NX), 1, LEV + 1)
    return jnp.where(rolled < land_cells, 0, depth_cells).astype(jnp.int32)


def plant(result, own_key, least, top_value):
    spot = [jax.random.randint(jax.random.fold_in(own_key, axis), (), 0, length) for axis, length in enumerate(result.shape)]
    longest = result.shape.index(max(result.shape))
    neighbour = spot[:longest] + [(spot[longest] + 1) % result.shape[longest]] + spot[longest + 1:]
    return result.at[tuple(spot)].set(least).at[tuple(neighbour)].set(top_value)


def level_of(own_key, dims, cuts, least, largest):
    loudness = 1.0
    for axis_at, shards_of in cuts:
        heights = jax.random.uniform(jax.random.fold_in(jax.random.fold_in(own_key, 6), axis_at), (shards_of,), jnp.float32, least / len(cuts), largest / len(cuts))
        loudness = loudness * jnp.repeat(jnp.exp(heights), dims[axis_at] // shards_of).reshape((-1,) + (1,) * (len(dims) - 1 - axis_at))
    return loudness


def noise(rng, shape, width, limit, cuts=(), kind=jnp.bfloat16):
    factor_of = level_of(rng, shape, cuts, -0.22, 0.18) if cuts else 1.0
    array = jax.random.normal(rng, shape, jnp.float32) * width * factor_of
    return jnp.minimum(jnp.maximum(array, -limit), limit).astype(kind)


def setup_inputs(seed: int = 0) -> dict:
    keys = jax.random.split(jax.random.key(seed), 13)
    return {
        "tracers": noise(keys[0], (2, LEV, NY, NX), 1.0, 6.0, ((2, 16), (3, 32)), jnp.float32),
        "velocity": noise(keys[1], (2, LEV, NY, NX), 1.0, 6.0, ((2, 16), (3, 32)), jnp.float32),
        "diffusivity": jnp.clip(jnp.exp(math.log(5.0) - 4.6051702 * jax.random.uniform(keys[2], (NY, NX), jnp.float32) ** level_of(keys[2], (NY, NX), ((0, 16), (1, 32)), -0.2, 0.2)), 0.05, 5.0),
        "ocean_levels": draw_ocean_levels(jax.random.fold_in(keys[12], 71), 0),
        "surface_height": noise(keys[4], (NY, NX), 1.0, 6.0, ((0, 16), (1, 32)), jnp.float32),
        "transport": noise(keys[5], (2, NY, NX), 1.0, 6.0, ((1, 16), (2, 32)), jnp.float32),
        "atm_flux": noise(keys[6], (N_LAT, NFLUX, ATMS), 1.0, 6.0, ((0, 16), (2, 32)), jnp.float32),
        "send_rows": plant(jax.random.randint(keys[7], (N_LAT, N_LON, N_LON, SLOTS), 0, ATM_DEV), jax.random.fold_in(keys[7], 1), 0, ATM_DEV - 1).astype(jnp.int32),
        "src_owner": plant(jax.random.randint(keys[8], (KX, NY, NX), 0, N_LON), jax.random.fold_in(keys[8], 1), 0, N_LON - 1).astype(jnp.int32),
        "src_slot": plant(jax.random.randint(keys[9], (KX, NY, NX), 0, SLOTS), jax.random.fold_in(keys[9], 1), 0, SLOTS - 1).astype(jnp.int32),
        "xgrid_weights": jnp.clip(0.1 + 0.9 * jax.random.uniform(keys[10], (KX, NY, NX), jnp.float32) ** level_of(keys[10], (KX, NY, NX), ((1, 16), (2, 32)), -0.2, 0.2), 0.1, 1.0),
        "xgrid_count": plant(jax.random.randint(keys[11], (NY, NX), 1, KX + 1), jax.random.fold_in(keys[11], 1), 1, KX).astype(jnp.int32),
    }


adv_rate = 0.1
heat_gain = 0.5
salt_gain = 0.5
wave_div = 0.5
wave_grad = 0.8
fresh_gain = 0.2
wind_gain = 0.2


def ocean_wetness(ocean_levels, depth_count):
    layer_ids = jnp.arange(depth_count, dtype=jnp.int32)[:, None, None]
    return (layer_ids < ocean_levels[None]).astype(jnp.float32)


def vertical_solve(forced, diffusivity, wetness):
    depth_count = forced.shape[1]
    couple = [diffusivity * wetness[layer + 1] for layer in range(depth_count - 1)]
    zero_plane = jnp.zeros_like(diffusivity)
    uppers = []
    rights = []
    for layer in range(depth_count):
        below_k = couple[layer] if layer < depth_count - 1 else zero_plane
        above_k = couple[layer - 1] if layer > 0 else zero_plane
        diag_val = 1.0 + above_k + below_k
        if layer == 0:
            pivot = diag_val
            right_val = forced[:, 0] / pivot
        else:
            pivot = diag_val + above_k * uppers[-1]
            right_val = (forced[:, layer] + above_k * rights[-1]) / pivot
        uppers.append(-below_k / pivot)
        rights.append(right_val)
    solved = [rights[-1]]
    for layer in range(depth_count - 2, -1, -1):
        solved.append(rights[layer] - uppers[layer] * solved[-1])
    return jnp.stack(solved[::-1], axis=1)


def remap(atm_flux, send_rows, src_owner, src_slot, xgrid_weights, xgrid_count):
    lat_block = (jnp.arange(NY, dtype=jnp.int32) // CY)[None, :, None]
    lon_block = (jnp.arange(NX, dtype=jnp.int32) // CX)[None, None, :]
    local_row = send_rows[lat_block, src_owner, lon_block, src_slot]
    column = src_owner * ATM_DEV + local_row
    entry_ids = jnp.arange(KX, dtype=jnp.int32)[:, None, None]
    used = (entry_ids < xgrid_count[None]).astype(jnp.float32) * xgrid_weights
    results = []
    for flux_id in range(NFLUX):
        values = atm_flux[:, flux_id, :][lat_block, column]
        results.append(jnp.sum(values * used, axis=0))
    return jnp.stack(results)


def reference(tracers, velocity, diffusivity, ocean_levels, surface_height, transport, atm_flux, send_rows, src_owner, src_slot, xgrid_weights, xgrid_count):
    depth_count = tracers.shape[1]
    wetness = ocean_wetness(ocean_levels, depth_count)
    fluxes = remap(atm_flux, send_rows, src_owner, src_slot, xgrid_weights, xgrid_count)
    east_vals = jnp.roll(tracers, -1, axis=3)
    east_wet = jnp.roll(wetness, -1, axis=2)
    north_vals = jnp.concatenate([tracers[:, :, 1:], tracers[:, :, -1:, ::-1]], axis=2)
    north_wet = jnp.concatenate([wetness[:, 1:], wetness[:, -1:, ::-1]], axis=1)
    east_flux = velocity[0] * ((tracers + east_vals) * 0.5) * (wetness * east_wet)
    north_flux = velocity[1] * ((tracers + north_vals) * 0.5) * (wetness * north_wet)
    west_flux = jnp.roll(east_flux, 1, axis=3)
    south_flux = jnp.concatenate([jnp.zeros_like(north_flux[:, :, :1]), north_flux[:, :, :-1]], axis=2)
    advected = tracers - adv_rate * ((east_flux - west_flux) + (north_flux - south_flux))
    surface = jnp.stack([heat_gain * fluxes[0], -salt_gain * fluxes[1]]) * wetness[0]
    forced = advected.at[:, 0].add(surface)
    tracers_out = vertical_solve(forced, diffusivity, wetness)
    ocean_top = wetness[0]
    depth_frac = ocean_levels.astype(jnp.float32) / depth_count
    height = surface_height
    east_tr = transport[0]
    north_tr = transport[1]
    for substep in range(SUBSTEPS):
        west_tr = jnp.roll(east_tr, 1, axis=1)
        south_tr = jnp.concatenate([jnp.zeros_like(north_tr[:1]), north_tr[:-1]], axis=0)
        spread = (east_tr - west_tr) + (north_tr - south_tr)
        height = (height - wave_div * spread + fresh_gain * fluxes[1]) * ocean_top
        east_h = jnp.roll(height, -1, axis=1)
        north_h = jnp.concatenate([height[1:], height[-1:, ::-1]], axis=0)
        east_tr = (east_tr - wave_grad * depth_frac * (east_h - height) + wind_gain * fluxes[2]) * ocean_top
        north_tr = (north_tr - wave_grad * depth_frac * (north_h - height) + wind_gain * fluxes[3]) * ocean_top
    return tracers_out, height, jnp.stack([east_tr, north_tr])
```

```python
import jax
import jax.numpy as jnp
from jax import lax
from jax.experimental import pallas as pl
from jax.experimental.pallas import tpu as pltpu
from jax.sharding import PartitionSpec as P

SUBSTEPS = 6
HALO = 8
FIELDS = 7
HEIGHT, EAST, NORTH, LEVELS, FRESH, WIND_E, WIND_N = range(FIELDS)
ROW_T = FIELDS * HALO
WEST_T = FIELDS * HALO + 1
EAST_T = FIELDS * HALO

adv_rate = 0.1
heat_gain = 0.5
salt_gain = 0.5
wave_div = 0.5
wave_grad = 0.8
fresh_gain = 0.2
wind_gain = 0.2

F32 = jnp.float32


def lanes(shape):
    return lax.broadcasted_iota(jnp.int32, shape, len(shape) - 1)


def rows_of(shape):
    return lax.broadcasted_iota(jnp.int32, shape, len(shape) - 2)


def turn(x, by, axis):
    size = x.shape[axis]
    by = by % size
    return x if by == 0 else pltpu.roll(x, by, axis)


def is_even(axis):
    return lax.rem(lax.axis_index(axis), 2) == 0


def is_top():
    return lax.axis_index("lat") == lax.axis_size("lat") - 1


def pick_kernel(atm_ref, rows_ref, out_ref):
    rows = rows_ref[0, 0]
    both = jnp.concatenate([rows, rows], axis=1)
    lane = both & 127
    part = both >> 7
    low = lanes(both.shape) < 64
    for pair in range(2):
        acc = None
        for k in range(atm_ref.shape[2] // 128):
            got = []
            for f in (2 * pair, 2 * pair + 1):
                row = jnp.broadcast_to(atm_ref[0, f : f + 1, k * 128 : (k + 1) * 128], both.shape)
                got.append(jnp.take_along_axis(row, lane, axis=1))
            value = jnp.where(low, got[0], got[1])
            acc = value if k == 0 else jnp.where(part == k, value, acc)
        out_ref[:, 0, pair * 128 : (pair + 1) * 128] = acc


def remap_kernel(
    table_ref, owner_ref, slot_ref, weight_ref, count_ref, level_ref, height_ref, transport_ref,
    t_low_ref, t_high_ref, v_high_ref, flux_ref, first_ref, second_ref, t_south_ref, tab, pack,
):
    received = table_ref[:, 0, :]
    half = received.shape[0] // 2
    low = lanes((half, 128)) < 64
    for pair in range(2):
        part = received[:, pair * 128 : (pair + 1) * 128]
        lo, hi = part[:half], part[half:]
        tab[2 * pair] = jnp.where(low, lo, turn(hi, 64, 1))
        tab[2 * pair + 1] = jnp.where(low, turn(lo, 64, 1), hi)
    count = count_ref[...]
    total = [jnp.zeros(count.shape, F32) for _ in range(4)]
    for k in range(owner_ref.shape[0]):
        owner = owner_ref[k]
        lane = slot_ref[k] + 64 * (owner >= half).astype(jnp.int32)
        row = jnp.where(owner >= half, owner - half, owner)
        acc = [None] * 4
        for r in range(half):
            here = row == r
            for f in range(4):
                source = jnp.broadcast_to(tab[f, r : r + 1, :], lane.shape)
                value = jnp.take_along_axis(source, lane, axis=1)
                acc[f] = value if r == 0 else jnp.where(here, value, acc[f])
        used = jnp.where(count > k, weight_ref[k], 0.0)
        total = [t + a * used for t, a in zip(total, acc)]
    for f in range(4):
        flux_ref[f] = total[f]

    even = is_even("lat")
    top = height_ref.shape[0] - HALO
    level_f = level_ref[...].astype(F32)
    for side, out in ((top, pack.at[0]), (0, pack.at[1])):
        rows = slice(side, side + HALO)
        out[HEIGHT * HALO : HEIGHT * HALO + HALO] = height_ref[rows]
        out[EAST * HALO : EAST * HALO + HALO] = transport_ref[0, rows]
        out[NORTH * HALO : NORTH * HALO + HALO] = transport_ref[1, rows]
        out[LEVELS * HALO : LEVELS * HALO + HALO] = level_f[rows]
        for i, f in ((FRESH, 1), (WIND_E, 2), (WIND_N, 3)):
            out[i * HALO : i * HALO + HALO] = total[f][rows]
    depth = t_low_ref.shape[1]
    for c in range(2):
        for l in range(depth):
            at = ROW_T + c * depth + l
            pack[0, at : at + 1] = t_high_ref[c, l, HALO - 1 : HALO]
            pack[1, at : at + 1] = t_low_ref[c, l, 0:1]
    for l in range(depth):
        at = ROW_T + 2 * depth + l
        pack[0, at : at + 1] = v_high_ref[0, l, HALO - 1 : HALO]
    pack[1, ROW_T + 2 * depth :] = jnp.zeros((depth, 128), F32)
    north_going, south_going = pack[0], pack[1]
    first_ref[...] = jnp.where(even, north_going, south_going)
    second_ref[...] = jnp.where(even, south_going, north_going)
    t_south_ref[...] = south_going[ROW_T : ROW_T + 2 * depth]


def column_kernel(t_ref, u_ref, level_ref, diff_ref, west_ref, east_ref, inv_ref):
    depth = t_ref.shape[1]
    shape = t_ref.shape[2:]
    lane = lanes(shape)
    west = jnp.zeros(shape, F32)
    east = jnp.zeros(shape, F32)
    for c in range(2):
        for l in range(depth):
            f = c * depth + l
            moved = turn(t_ref[c, l], WEST_T + f, 1)
            west = jnp.where(lane == WEST_T + f, moved, west)
            east = jnp.where(lane == EAST_T + f, moved, east)
    for l in range(depth):
        at = EAST_T + 2 * depth + l
        east = jnp.where(lane == at, turn(u_ref[0, l], at + 1, 1), east)
    west_ref[...] = west
    east_ref[...] = east
    level = level_ref[...]
    diff = diff_ref[...]
    above = jnp.zeros(shape, F32)
    inv = None
    for l in range(depth):
        below = jnp.where(level > l + 1, diff, 0.0) if l < depth - 1 else jnp.zeros(shape, F32)
        pivot = 1.0 + above + below
        if l > 0:
            pivot = pivot - above * above * inv
        inv = 1.0 / pivot
        inv_ref[l] = inv
        above = below


def edge_kernel(
    first_ref, second_ref, height_ref, transport_ref, level_ref, flux_ref, west_ref, east_ref,
    one_ref, two_ref, north_ref, south_ref,
):
    even = is_even("lat")
    a, b = first_ref[...], second_ref[...]
    north = jnp.where(even, a, b)
    south_ref[...] = jnp.where(even, b, a)
    south = south_ref[...]
    mirrored = jnp.take_along_axis(north, 127 - lanes(north.shape), axis=1)
    north = jnp.where(is_top(), mirrored, north)
    north_ref[...] = north
    own = (
        height_ref[...],
        transport_ref[0],
        transport_ref[1],
        level_ref[...].astype(F32),
        flux_ref[1],
        flux_ref[2],
        flux_ref[3],
    )
    pad = jnp.zeros((HALO, 128), F32)
    west = jnp.concatenate([pad, west_ref[...], pad], axis=0)
    east = jnp.concatenate([pad, east_ref[...], pad], axis=0)
    lane = lanes(west.shape)
    for i in range(FIELDS):
        rows = slice(i * HALO, (i + 1) * HALO)
        whole = jnp.concatenate([south[rows], own[i], north[rows]], axis=0)
        here = (lane >= i * HALO) & (lane < (i + 1) * HALO)
        west = jnp.where(here, turn(whole, i * HALO, 1), west)
        east = jnp.where(here, turn(whole, (i + 1) * HALO, 1), east)
    even = is_even("lon")
    one_ref[...] = jnp.where(even, east, west)
    two_ref[...] = jnp.where(even, west, east)


def step_kernel(
    one_ref, two_ref, north_ref, south_ref, height_ref, transport_ref, level_ref, flux_ref,
    west_ref, t_south_ref, inv_ref, diff_ref, t_ref, v_ref,
    t_out, height_out, transport_out, south_flux,
):
    top = is_top()
    even = is_even("lon")
    one, two = one_ref[...], two_ref[...]
    from_east = jnp.where(even, one, two)
    from_west = jnp.where(even, two, one)
    north, south = north_ref[...], south_ref[...]
    level = level_ref[...]
    level_f = level.astype(F32)
    rows, cols = level.shape
    lane = lanes(from_east.shape)
    own = (
        height_ref[...], transport_ref[0], transport_ref[1], level_f,
        flux_ref[1], flux_ref[2], flux_ref[3],
    )
    ext = []
    for i in range(FIELDS):
        at = slice(i * HALO, (i + 1) * HALO)
        whole = jnp.concatenate([south[at], own[i], north[at]], axis=0)
        rim = jnp.where(
            lane < HALO,
            turn(from_east, -i * HALO, 1),
            jnp.where(lane >= cols - HALO, turn(from_west, cols - (i + 1) * HALO, 1), 0.0),
        )
        ext.append(jnp.concatenate([whole, rim], axis=1))

    depth = t_ref.shape[1]

    def coefficients(f):
        wet = (f[LEVELS] > 0.0).astype(F32)
        return (
            wet,
            wave_grad * (f[LEVELS] / depth),
            fresh_gain * f[FRESH] * wet,
            wind_gain * f[WIND_E] * wet,
            wind_gain * f[WIND_N] * wet,
        )

    mine = [x for x in ext]
    fold = [x[HALO + rows :] for x in ext]
    wet, grad, fresh, wind_e, wind_n = coefficients(mine)
    p_wet, p_grad, p_fresh, p_wind_e, p_wind_n = coefficients(fold)
    h, e, n = mine[HEIGHT], mine[EAST], mine[NORTH]
    p_h, p_e, p_n = fold[HEIGHT], fold[EAST], fold[NORTH]
    row = rows_of(h.shape)
    last = HALO + rows - 1
    across = (row == last) & top
    p_last = rows_of(p_h.shape) == HALO - 1
    for _ in range(SUBSTEPS):
        h = (h - wave_div * ((e - turn(e, 1, 1)) + (n - turn(n, 1, 0)))) * wet + fresh
        p_h = (p_h - wave_div * ((p_e - turn(p_e, -1, 1)) + (p_n - turn(p_n, 1, 0)))) * p_wet + p_fresh
        h_n = jnp.where(across, jnp.broadcast_to(p_h[HALO - 1 :], h.shape), turn(h, -1, 0))
        p_h_n = jnp.where(p_last, jnp.broadcast_to(h[last : last + 1], p_h.shape), turn(p_h, -1, 0))
        e = (e - grad * (turn(h, -1, 1) - h)) * wet + wind_e
        n = (n - grad * (h_n - h)) * wet + wind_n
        p_e = (p_e - p_grad * (turn(p_h, 1, 1) - p_h)) * p_wet + p_wind_e
        p_n = (p_n - p_grad * (p_h_n - p_h)) * p_wet + p_wind_n
    inside = slice(HALO, HALO + rows)
    height_out[...] = h[inside, :cols]
    transport_out[0] = e[inside, :cols]
    transport_out[1] = n[inside, :cols]

    ext_level = ext[LEVELS]
    level_e = turn(ext_level, -1, 1)[inside, :cols]
    level_w = turn(ext_level, 1, 1)[inside, :cols]
    first = LEVELS * HALO
    level_n_row = jnp.where(top, north[first + HALO - 1 : first + HALO], north[first : first + 1])
    level_s_row = south[first + HALO - 1 : first + HALO]
    shape = (rows, cols)
    lane = lanes(shape)
    row = rows_of(shape)
    level_n = jnp.where(row == rows - 1, jnp.broadcast_to(level_n_row, shape), turn(level_f, -1, 0))
    face_e = jnp.minimum(level_f, level_e)
    face_n = jnp.minimum(level_f, level_n)
    face_s = jnp.minimum(level_f[0:1], level_s_row)
    t_w = from_west[inside]
    t_0 = turn(west_ref[...], EAST_T - WEST_T, 1)
    start_u = EAST_T + 2 * depth
    u_w = jnp.where(lane < EAST_T + depth, turn(t_w, EAST_T - start_u, 1), turn(t_w, EAST_T + depth - start_u, 1))
    layer = jnp.where(lane < EAST_T + depth, lane - EAST_T, lane - EAST_T - depth).astype(F32)
    face_w = jnp.broadcast_to(jnp.minimum(level_f, level_w)[:, 0:1], shape)
    west_flux = jnp.where(layer < face_w, u_w * ((t_w + t_0) * 0.5), 0.0)
    t_e = from_east[inside]
    for c in range(2):
        planes = slice(ROW_T + c * depth, ROW_T + (c + 1) * depth)
        flux = south[ROW_T + 2 * depth : ROW_T + 3 * depth] * (
            (south[planes] + t_south_ref[c * depth : (c + 1) * depth]) * 0.5
        )
        deep = rows_of(flux.shape).astype(F32) < face_s
        south_flux[c * depth : (c + 1) * depth] = jnp.where(deep, flux, 0.0)

    diff = diff_ref[...]
    wet_0 = (level > 0).astype(F32)
    source = (heat_gain * flux_ref[0] * wet_0, -salt_gain * flux_ref[1] * wet_0)
    right = [None, None]
    for l in range(depth):
        mask_e = face_e > l
        mask_n = face_n > l
        u_l, v_l = v_ref[0, l], v_ref[1, l]
        above = jnp.where(level > l, diff, 0.0)
        inv = inv_ref[l]
        for c in range(2):
            f = c * depth + l
            t = t_ref[c, l]
            east = jnp.where(lane == cols - 1, turn(t_e, cols - 1 - (WEST_T + f), 1), turn(t, -1, 1))
            flux_e = jnp.where(mask_e, u_l * ((t + east) * 0.5), 0.0)
            flux_w = jnp.where(lane == 0, turn(west_flux, -(EAST_T + f), 1), turn(flux_e, 1, 1))
            north_row = jnp.broadcast_to(north_ref[ROW_T + f : ROW_T + f + 1], shape)
            up = jnp.where(row == rows - 1, north_row, turn(t, -1, 0))
            flux_n = jnp.where(mask_n, v_l * ((t + up) * 0.5), 0.0)
            south_row = jnp.broadcast_to(south_flux[f : f + 1], shape)
            flux_s = jnp.where(row == 0, south_row, turn(flux_n, 1, 0))
            forced = t - adv_rate * ((flux_e - flux_w) + (flux_n - flux_s))
            if l == 0:
                forced = forced + source[c]
                right[c] = forced * inv
            else:
                right[c] = (forced + above * right[c]) * inv
            t_out[c, l] = right[c]
    for l in range(depth - 2, -1, -1):
        below = jnp.where(level > l + 1, diff, 0.0) * inv_ref[l]
        for c in range(2):
            right[c] = t_out[c, l] + below * right[c]
            t_out[c, l] = right[c]


def vmem(count):
    return [pl.BlockSpec(memory_space=pltpu.VMEM)] * count


def params():
    return pltpu.CompilerParams(vmem_limit_bytes=48 * 1024 * 1024)


def shape_of(*shape):
    return jax.ShapeDtypeStruct(shape, F32)


def lat_pairs(n_lat, n_lon):
    def at(i, j):
        return i * n_lon + j

    first, second = [], []
    for j in range(n_lon):
        for i in range(0, n_lat, 2):
            first += [(at(i, j), at(i + 1, j)), (at(i + 1, j), at(i, j))]
        for i in range(1, n_lat - 1, 2):
            second += [(at(i, j), at(i + 1, j)), (at(i + 1, j), at(i, j))]
        second.append((at(n_lat - 1, j), at(n_lat - 1, n_lon - 1 - j)))
    return first, second


def lon_pairs(n_lon):
    first, second = [], []
    for j in range(0, n_lon, 2):
        first += [(j, j + 1), (j + 1, j)]
        k, m = j + 1, (j + 2) % n_lon
        second += [(k, m), (m, k)]
    return first, second


def per_device(
    tracers,
    velocity,
    diffusivity,
    ocean_levels,
    surface_height,
    transport,
    atm_flux,
    send_rows,
    src_owner,
    src_slot,
    xgrid_weights,
    xgrid_count,
):
    n_lat, n_lon = lax.axis_size("lat"), lax.axis_size("lon")
    depth, rows, cols = tracers.shape[1:]
    slots = send_rows.shape[3]
    picked = pl.pallas_call(
        pick_kernel,
        out_shape=shape_of(n_lon, 1, 4 * slots),
        in_specs=vmem(2),
        out_specs=vmem(1)[0],
        compiler_params=params(),
        name="pick",
    )(atm_flux, send_rows)
    table = lax.all_to_all(picked, "lon", split_axis=0, concat_axis=0, tiled=True)

    eight = lambda pick: pl.BlockSpec((2, depth, HALO, cols), lambda i, p=pick: (0, 0, p, 0))
    last = rows // HALO - 1
    lat_rows = ROW_T + 3 * depth
    flux, first, second, t_south = pl.pallas_call(
        remap_kernel,
        grid=(1,),
        out_shape=(
            shape_of(4, rows, cols),
            shape_of(lat_rows, cols),
            shape_of(lat_rows, cols),
            shape_of(2 * depth, cols),
        ),
        in_specs=vmem(8)
        + [
            eight(0),
            eight(last),
            pl.BlockSpec((1, depth, HALO, cols), lambda i: (1, 0, last, 0)),
        ],
        out_specs=vmem(4),
        scratch_shapes=[
            pltpu.VMEM((4, n_lon // 2, 128), F32),
            pltpu.VMEM((2, lat_rows, cols), F32),
        ],
        compiler_params=params(),
        name="remap",
    )(
        table, src_owner, src_slot, xgrid_weights, xgrid_count, ocean_levels, surface_height, transport,
        tracers, tracers, velocity,
    )
    pairs = lat_pairs(n_lat, n_lon)
    first = lax.ppermute(first, ("lat", "lon"), pairs[0])
    second = lax.ppermute(second, ("lat", "lon"), pairs[1])

    west, east, inv = pl.pallas_call(
        column_kernel,
        grid=(1,),
        out_shape=(shape_of(rows, cols), shape_of(rows, cols), shape_of(depth, rows, cols)),
        in_specs=[
            pl.BlockSpec((2, depth, rows, cols), lambda i: (0, 0, 0, 0)),
            pl.BlockSpec((1, depth, rows, cols), lambda i: (0, 0, 0, 0)),
        ]
        + vmem(2),
        out_specs=vmem(3),
        compiler_params=params(),
        cost_estimate=pl.CostEstimate(flops=2000000, bytes_accessed=2000000, transcendentals=0),
        name="columns",
    )(tracers, velocity, ocean_levels, diffusivity)

    one, two, north, south = pl.pallas_call(
        edge_kernel,
        out_shape=(
            shape_of(rows + 2 * HALO, cols),
            shape_of(rows + 2 * HALO, cols),
            shape_of(lat_rows, cols),
            shape_of(lat_rows, cols),
        ),
        in_specs=vmem(8),
        out_specs=vmem(4),
        compiler_params=params(),
        name="edges",
    )(first, second, surface_height, transport, ocean_levels, flux, west, east)
    pairs = lon_pairs(n_lon)
    one = lax.ppermute(one, "lon", pairs[0])
    two = lax.ppermute(two, "lon", pairs[1])

    return pl.pallas_call(
        step_kernel,
        out_shape=(shape_of(2, depth, rows, cols), shape_of(rows, cols), shape_of(2, rows, cols)),
        in_specs=vmem(14),
        out_specs=tuple(vmem(3)),
        scratch_shapes=[pltpu.VMEM((2 * depth, cols), F32)],
        compiler_params=params(),
        name="step",
    )(
        one, two, north, south, surface_height, transport, ocean_levels, flux,
        west, t_south, inv, diffusivity, tracers, velocity,
    )


def solution(mesh):
    return jax.shard_map(
        per_device,
        mesh=mesh,
        in_specs=(
            P(None, None, "lat", "lon"),
            P(None, None, "lat", "lon"),
            P("lat", "lon"),
            P("lat", "lon"),
            P("lat", "lon"),
            P(None, "lat", "lon"),
            P("lat", None, "lon"),
            P("lat", "lon", None, None),
            P(None, "lat", "lon"),
            P(None, "lat", "lon"),
            P(None, "lat", "lon"),
            P("lat", "lon"),
        ),
        out_specs=(P(None, None, "lat", "lon"), P("lat", "lon"), P(None, "lat", "lon")),
        check_vma=False,
    )
```

```python
import jax
import jax.numpy as jnp
from jax import lax
from jax.experimental import pallas as pl
from jax.experimental.pallas import tpu as pltpu
from jax.sharding import PartitionSpec as P

SUBSTEPS = 6
HALO = 8
FIELDS = 7
HEIGHT, EAST, NORTH, LEVELS, FRESH, WIND_E, WIND_N = range(FIELDS)
ROW_RIM = FIELDS * HALO
ROW_T = ROW_RIM + HALO
OWNER, SLOT, USED = 32, 64, 96

adv_rate = 0.1
heat_gain = 0.5
salt_gain = 0.5
wave_div = 0.5
wave_grad = 0.8
fresh_gain = 0.2
wind_gain = 0.2

F32 = jnp.float32


def lanes(shape):
    return lax.broadcasted_iota(jnp.int32, shape, len(shape) - 1)


def rows_of(shape):
    return lax.broadcasted_iota(jnp.int32, shape, len(shape) - 2)


def turn(x, by, axis):
    size = x.shape[axis]
    by = by % size
    return x if by == 0 else pltpu.roll(x, by, axis)


def is_even(axis):
    return lax.rem(lax.axis_index(axis), 2) == 0


def is_top():
    return lax.axis_index("lat") == lax.axis_size("lat") - 1


def pick_kernel(atm_hbm, rows_hbm, out_ref, atm_ref, rows_ref, sems):
    copies = [
        pltpu.make_async_copy(atm_hbm, atm_ref, sems.at[0]),
        pltpu.make_async_copy(rows_hbm, rows_ref, sems.at[1]),
    ]
    for copy in copies:
        copy.start()
    for copy in copies:
        copy.wait()
    rows = rows_ref[0, 0]
    both = jnp.concatenate([rows, rows], axis=1)
    lane = both & 127
    part = both >> 7
    low = lanes(both.shape) < 64
    values = []
    for f in range(4):
        acc = None
        for k in range(atm_ref.shape[2] // 128):
            row = jnp.broadcast_to(atm_ref[0, f : f + 1, k * 128 : (k + 1) * 128], both.shape)
            value = jnp.take_along_axis(row, lane, axis=1)
            acc = value if k == 0 else jnp.where(part == k, value, acc)
        values.append(acc)
    out_ref[:, 0, 0:128] = jnp.where(low, values[0], values[1])
    out_ref[:, 0, 128:256] = jnp.where(low, values[2], values[3])
    for f in range(1, 4):
        at = 128 + f * 128
        out_ref[:, 0, at : at + 128] = jnp.where(low, turn(values[f], -1, 0), turn(values[f], 1, 0))


def edge_kernel(
    picked_ref, t_ref, v_ref, level_ref, diff_ref, height_ref, transport_ref, owner_ref, slot_ref,
    weight_ref, count_ref, one_ref, two_ref, t_0_ref, rows_ref, inv_ref, pick_row_ref, pick_lane_ref, used_ref,
):
    depth = t_ref.shape[1]
    shape = t_ref.shape[2:]
    rows, cols = shape
    lane = lanes(shape)
    level = level_ref[...]
    half = lax.axis_size("lon") // 2
    count = count_ref[...]
    for k in range(owner_ref.shape[0]):
        owner = owner_ref[k]
        high = owner >= half
        pick_row_ref[k] = jnp.where(high, owner - half, owner)
        pick_lane_ref[k] = jnp.where(high, slot_ref[k] + 64, slot_ref[k])
        used_ref[k] = jnp.where(count > k, weight_ref[k], 0.0)
    fields = [height_ref[...], transport_ref[0], transport_ref[1], level.astype(F32)]
    fields += [owner_ref[k].astype(F32) for k in range(4)]
    fields += [slot_ref[k].astype(F32) for k in range(4)]
    fields += [used_ref[k] for k in range(4)]
    west = jnp.zeros(shape, F32)
    east = jnp.zeros(shape, F32)
    for g, field in enumerate(fields):
        here = (lane >= g * HALO) & (lane < (g + 1) * HALO)
        west = jnp.where(here, turn(field, g * HALO, 1), west)
        east = jnp.where(here, turn(field, (g + 1) * HALO, 1), east)
    west_t = jnp.zeros(shape, F32)
    east_t = jnp.zeros(shape, F32)
    for c in range(2):
        for l in range(depth):
            f = c * depth + l
            moved = turn(t_ref[c, l], f + 1, 1)
            west_t = jnp.where(lane == f + 1, moved, west_t)
            east_t = jnp.where(lane == f, moved, east_t)
    for l in range(depth):
        at = 2 * depth + l
        east_t = jnp.where(lane == at, turn(v_ref[0, l], at + 1, 1), east_t)
    even = is_even("lon")
    one_ref[:rows] = jnp.where(even, east, west)
    two_ref[:rows] = jnp.where(even, west, east)
    one_ref[rows:] = jnp.where(even, east_t, west_t)
    two_ref[rows:] = jnp.where(even, west_t, east_t)
    t_0_ref[...] = turn(west_t, -1, 1)
    for c in range(2):
        for l in range(depth):
            at = c * depth + l
            rows_ref[0, at : at + 1] = t_ref[c, l, rows - 1 : rows]
            rows_ref[1, at : at + 1] = t_ref[c, l, 0:1]
    for l in range(depth):
        at = 2 * depth + l
        rows_ref[0, at : at + 1] = v_ref[1, l, rows - 1 : rows]
    rows_ref[1, 2 * depth :] = jnp.zeros((depth, cols), F32)
    diff = diff_ref[...]
    above = jnp.zeros(shape, F32)
    inv = None
    for l in range(depth):
        below = jnp.where(level > l + 1, diff, 0.0) if l < depth - 1 else jnp.zeros(shape, F32)
        pivot = 1.0 + above + below
        if l > 0:
            pivot = pivot - above * above * inv
        inv = 1.0 / pivot
        inv_ref[l] = inv
        above = below


def remap_kernel(
    table_ref, one_ref, two_ref, pick_row_ref, pick_lane_ref, used_ref, rows_ref, level_ref, height_ref,
    transport_ref, flux_ref, rim_ref, first_ref, second_ref, tab, side, pack,
):
    n_lon = table_ref.shape[0]
    half = n_lon // 2
    rows, cols = height_ref.shape
    low = lanes((half, 128)) < 64
    for pair in range(2):
        part = table_ref[:, 0, pair * 128 : (pair + 1) * 128]
        lo, hi = part[:half], part[half:]
        tab[2 * pair] = jnp.where(low, lo, turn(hi, 64, 1))
        tab[2 * pair + 1] = jnp.where(low, turn(lo, 64, 1), hi)
    total = [jnp.zeros((rows, cols), F32) for _ in range(4)]
    for k in range(used_ref.shape[0]):
        lane = pick_lane_ref[k]
        row = pick_row_ref[k]
        acc = [None] * 4
        for r in range(half):
            here = row == r
            for f in range(4):
                source = jnp.broadcast_to(tab[f, r : r + 1, :], lane.shape)
                value = jnp.take_along_axis(source, lane, axis=1)
                acc[f] = value if r == 0 else jnp.where(here, value, acc[f])
        used = used_ref[k]
        total = [t + a * used for t, a in zip(total, acc)]
    for f in range(4):
        flux_ref[f] = total[f]

    even = is_even("lon")
    one, two = one_ref[:rows], two_ref[:rows]
    east = jnp.where(even, one, two)
    west = jnp.where(even, two, one)
    lane = lanes(east.shape)
    from_east = lane < 64
    valid = (lane >= 32) & (lane < 96)
    owner = jnp.where(valid, jnp.where(from_east, east, turn(west, 32, 1)), 0.0).astype(jnp.int32)
    slot = jnp.where(valid, jnp.where(from_east, turn(east, -32, 1), west), 0.0).astype(jnp.int32)
    used = jnp.where(valid, jnp.where(from_east, turn(east, -64, 1), turn(west, -32, 1)), 0.0)
    slot = jnp.where(from_east, slot, slot + 64)
    for f in range(3):
        side[f] = table_ref[:, 0, 256 + f * 128 : 384 + f * 128]
    acc = [None] * 3
    for r in range(n_lon):
        here = owner == r
        for f in range(3):
            source = jnp.broadcast_to(side[f, r : r + 1, :], slot.shape)
            value = jnp.take_along_axis(source, slot, axis=1)
            acc[f] = value if r == 0 else jnp.where(here, value, acc[f])
    rim = []
    inner, outer = lane < HALO, lane >= cols - HALO
    for g in range(4):
        rim.append((turn(east, -g * HALO, 1), turn(west, cols - (g + 1) * HALO, 1)))
    for f in range(3):
        v = acc[f] * used
        v = v + turn(v, -16, 1)
        v = v + turn(v, -8, 1)
        rim.append((turn(v, -32, 1), turn(v, 56, 1)))
    rim = [jnp.where(inner, e, jnp.where(outer, w, 0.0)) for e, w in rim]
    for i in range(FIELDS):
        rim_ref[i] = rim[i]

    level_f = level_ref[...].astype(F32)
    own = (
        height_ref[...], transport_ref[0], transport_ref[1], level_f, total[1], total[2], total[3],
    )
    lane = lanes((HALO, cols))
    for s, at in ((0, rows - HALO), (1, 0)):
        cut = slice(at, at + HALO)
        rims = jnp.zeros((HALO, cols), F32)
        for i in range(FIELDS):
            pack[s, i * HALO : (i + 1) * HALO] = own[i][cut]
            start = 2 * HALO * i
            here = (lane >= start) & (lane < start + 2 * HALO)
            rims = jnp.where(here, turn(rim[i][cut], start + HALO, 1), rims)
        pack[s, ROW_RIM:ROW_T] = rims
        pack[s, ROW_T:] = rows_ref[s]
    even = is_even("lat")
    north_going, south_going = pack[0], pack[1]
    first_ref[...] = jnp.where(even, north_going, south_going)
    second_ref[...] = jnp.where(even, south_going, north_going)


def step_kernel(
    one_ref, two_ref, first_ref, second_ref, height_ref, transport_ref, level_ref, flux_ref, rim_ref,
    t_0_ref, rows_ref, inv_ref, diff_ref, t_ref, v_ref,
    t_out, height_out, transport_out, north_ref, south_flux,
):
    top = is_top()
    level = level_ref[...]
    level_f = level.astype(F32)
    rows, cols = level.shape
    depth = t_ref.shape[1]
    even = is_even("lat")
    a, b = first_ref[...], second_ref[...]
    south = jnp.where(even, b, a)
    north = jnp.where(even, a, b)
    mirrored = jnp.take_along_axis(north, 127 - lanes(north.shape), axis=1)
    north = jnp.where(top, mirrored, north)
    north_ref[...] = north
    even = is_even("lon")
    one, two = one_ref[rows:], two_ref[rows:]
    t_e = jnp.where(even, one, two)
    t_w = jnp.where(even, two, one)
    own = (
        height_ref[...], transport_ref[0], transport_ref[1], level_f,
        flux_ref[1], flux_ref[2], flux_ref[3],
    )
    ext = []
    lane = lanes((HALO, cols))
    side = (lane < HALO) | (lane >= cols - HALO)
    for i in range(FIELDS):
        at = slice(i * HALO, (i + 1) * HALO)
        whole = jnp.concatenate([south[at], own[i], north[at]], axis=0)
        start = jnp.where(top, cols - 2 * HALO * (FIELDS - i) - HALO, cols - 2 * HALO * i - HALO)
        north_rim = jnp.where(side, pltpu.roll(north[ROW_RIM:ROW_T], start, 1), 0.0)
        south_rim = jnp.where(side, turn(south[ROW_RIM:ROW_T], -(2 * HALO * i + HALO), 1), 0.0)
        rim = jnp.concatenate([south_rim, rim_ref[i], north_rim], axis=0)
        ext.append(jnp.concatenate([whole, rim], axis=1))


    def coefficients(f):
        wet = (f[LEVELS] > 0.0).astype(F32)
        return (
            wet,
            wave_grad * (f[LEVELS] / depth),
            fresh_gain * f[FRESH] * wet,
            wind_gain * f[WIND_E] * wet,
            wind_gain * f[WIND_N] * wet,
        )

    mine = [x for x in ext]
    fold = [x[HALO + rows :] for x in ext]
    wet, grad, fresh, wind_e, wind_n = coefficients(mine)
    p_wet, p_grad, p_fresh, p_wind_e, p_wind_n = coefficients(fold)
    h, e, n = mine[HEIGHT], mine[EAST], mine[NORTH]
    p_h, p_e, p_n = fold[HEIGHT], fold[EAST], fold[NORTH]
    row = rows_of(h.shape)
    last = HALO + rows - 1
    across = (row == last) & top
    p_last = rows_of(p_h.shape) == HALO - 1
    for _ in range(SUBSTEPS):
        h = (h - wave_div * ((e - turn(e, 1, 1)) + (n - turn(n, 1, 0)))) * wet + fresh
        p_h = (p_h - wave_div * ((p_e - turn(p_e, -1, 1)) + (p_n - turn(p_n, 1, 0)))) * p_wet + p_fresh
        h_n = jnp.where(across, jnp.broadcast_to(p_h[HALO - 1 :], h.shape), turn(h, -1, 0))
        p_h_n = jnp.where(p_last, jnp.broadcast_to(h[last : last + 1], p_h.shape), turn(p_h, -1, 0))
        e = (e - grad * (turn(h, -1, 1) - h)) * wet + wind_e
        n = (n - grad * (h_n - h)) * wet + wind_n
        p_e = (p_e - p_grad * (turn(p_h, 1, 1) - p_h)) * p_wet + p_wind_e
        p_n = (p_n - p_grad * (p_h_n - p_h)) * p_wet + p_wind_n
    inside = slice(HALO, HALO + rows)
    height_out[...] = h[inside, :cols]
    transport_out[0] = e[inside, :cols]
    transport_out[1] = n[inside, :cols]

    ext_level = ext[LEVELS]
    level_e = turn(ext_level, -1, 1)[inside, :cols]
    level_w = turn(ext_level, 1, 1)[inside, :cols]
    first = LEVELS * HALO
    level_n_row = jnp.where(top, north[first + HALO - 1 : first + HALO], north[first : first + 1])
    level_s_row = south[first + HALO - 1 : first + HALO]
    shape = (rows, cols)
    lane = lanes(shape)
    row = rows_of(shape)
    level_n = jnp.where(row == rows - 1, jnp.broadcast_to(level_n_row, shape), turn(level_f, -1, 0))
    face_e = jnp.minimum(level_f, level_e)
    face_n = jnp.minimum(level_f, level_n)
    face_s = jnp.minimum(level_f[0:1], level_s_row)
    t_0 = t_0_ref[...]
    u_w = jnp.where(lane < depth, turn(t_w, -2 * depth, 1), turn(t_w, -depth, 1))
    layer = jnp.where(lane < depth, lane, lane - depth).astype(F32)
    face_w = jnp.broadcast_to(jnp.minimum(level_f, level_w)[:, 0:1], shape)
    west_flux = jnp.where(layer < face_w, u_w * ((t_w + t_0) * 0.5), 0.0)
    for c in range(2):
        planes = slice(ROW_T + c * depth, ROW_T + (c + 1) * depth)
        flux = south[ROW_T + 2 * depth : ROW_T + 3 * depth] * (
            (south[planes] + rows_ref[1, c * depth : (c + 1) * depth]) * 0.5
        )
        deep = rows_of(flux.shape).astype(F32) < face_s
        south_flux[c * depth : (c + 1) * depth] = jnp.where(deep, flux, 0.0)

    diff = diff_ref[...]
    wet_0 = (level > 0).astype(F32)
    source = (heat_gain * flux_ref[0] * wet_0, -salt_gain * flux_ref[1] * wet_0)
    right = [None, None]
    for l in range(depth):
        mask_e = face_e > l
        mask_n = face_n > l
        u_l, v_l = v_ref[0, l], v_ref[1, l]
        above = jnp.where(level > l, diff, 0.0)
        inv = inv_ref[l]
        for c in range(2):
            f = c * depth + l
            t = t_ref[c, l]
            east = jnp.where(lane == cols - 1, turn(t_e, cols - 2 - f, 1), turn(t, -1, 1))
            flux_e = jnp.where(mask_e, u_l * ((t + east) * 0.5), 0.0)
            flux_w = jnp.where(lane == 0, turn(west_flux, -f, 1), turn(flux_e, 1, 1))
            north_row = jnp.broadcast_to(north_ref[ROW_T + f : ROW_T + f + 1], shape)
            up = jnp.where(row == rows - 1, north_row, turn(t, -1, 0))
            flux_n = jnp.where(mask_n, v_l * ((t + up) * 0.5), 0.0)
            south_row = jnp.broadcast_to(south_flux[f : f + 1], shape)
            flux_s = jnp.where(row == 0, south_row, turn(flux_n, 1, 0))
            forced = t - adv_rate * ((flux_e - flux_w) + (flux_n - flux_s))
            if l == 0:
                forced = forced + source[c]
                right[c] = forced * inv
            else:
                right[c] = (forced + above * right[c]) * inv
            t_out[c, l] = right[c]
    for l in range(depth - 2, -1, -1):
        below = jnp.where(level > l + 1, diff, 0.0) * inv_ref[l]
        for c in range(2):
            right[c] = t_out[c, l] + below * right[c]
            t_out[c, l] = right[c]


def vmem(count):
    return [pl.BlockSpec(memory_space=pltpu.VMEM)] * count


def params():
    return pltpu.CompilerParams(vmem_limit_bytes=24 * 1024 * 1024)


def shape_of(*shape):
    return jax.ShapeDtypeStruct(shape, F32)


def lat_pairs(n_lat, n_lon):
    def at(i, j):
        return i * n_lon + j

    first, second = [], []
    for j in range(n_lon):
        for i in range(0, n_lat, 2):
            first += [(at(i, j), at(i + 1, j)), (at(i + 1, j), at(i, j))]
        for i in range(1, n_lat - 1, 2):
            second += [(at(i, j), at(i + 1, j)), (at(i + 1, j), at(i, j))]
        second.append((at(n_lat - 1, j), at(n_lat - 1, n_lon - 1 - j)))
    return first, second


def lon_pairs(n_lon):
    first, second = [], []
    for j in range(0, n_lon, 2):
        first += [(j, j + 1), (j + 1, j)]
        k, m = j + 1, (j + 2) % n_lon
        second += [(k, m), (m, k)]
    return first, second


def per_device(
    tracers,
    velocity,
    diffusivity,
    ocean_levels,
    surface_height,
    transport,
    atm_flux,
    send_rows,
    src_owner,
    src_slot,
    xgrid_weights,
    xgrid_count,
):
    n_lat, n_lon = lax.axis_size("lat"), lax.axis_size("lon")
    depth, rows, cols = tracers.shape[1:]
    slots = send_rows.shape[3]
    picked = pl.pallas_call(
        pick_kernel,
        out_shape=shape_of(n_lon, 1, 10 * slots),
        in_specs=[pl.BlockSpec(memory_space=pl.ANY)] * 2,
        out_specs=vmem(1)[0],
        scratch_shapes=[
            pltpu.VMEM(atm_flux.shape, F32),
            pltpu.VMEM(send_rows.shape, jnp.int32),
            pltpu.SemaphoreType.DMA((2,)),
        ],
        compiler_params=params(),
        name="pick",
    )(atm_flux, send_rows)
    table = lax.all_to_all(picked, "lon", split_axis=0, concat_axis=0, tiled=True)

    block = (rows, cols)
    lat_rows = ROW_T + 3 * depth
    one, two, t_0, edge_rows, inv, pick_row, pick_lane, used = pl.pallas_call(
        edge_kernel,
        out_shape=(
            shape_of(2 * rows, cols),
            shape_of(2 * rows, cols),
            shape_of(*block),
            shape_of(2, 3 * depth, cols),
            shape_of(depth, *block),
            jax.ShapeDtypeStruct((4, *block), jnp.int32),
            jax.ShapeDtypeStruct((4, *block), jnp.int32),
            shape_of(4, *block),
        ),
        in_specs=[pl.BlockSpec(memory_space=pl.ANY)] + vmem(10),
        out_specs=vmem(8),
        compiler_params=params(),
        cost_estimate=pl.CostEstimate(flops=2000000, bytes_accessed=2000000, transcendentals=0),
        name="edges",
    )(
        picked, tracers, velocity, ocean_levels, diffusivity, surface_height, transport, src_owner, src_slot,
        xgrid_weights, xgrid_count,
    )
    pairs = lon_pairs(n_lon)
    two = lax.ppermute(two, "lon", pairs[1])
    one = lax.ppermute(one, "lon", pairs[0])

    flux, rim, first, second = pl.pallas_call(
        remap_kernel,
        out_shape=(
            shape_of(4, *block),
            shape_of(FIELDS, *block),
            shape_of(lat_rows, cols),
            shape_of(lat_rows, cols),
        ),
        in_specs=vmem(10),
        out_specs=vmem(4),
        scratch_shapes=[
            pltpu.VMEM((4, n_lon // 2, 128), F32),
            pltpu.VMEM((3, n_lon, 128), F32),
            pltpu.VMEM((2, lat_rows, cols), F32),
        ],
        compiler_params=params(),
        name="remap",
    )(
        table, one, two, pick_row, pick_lane, used, edge_rows, ocean_levels, surface_height, transport,
    )
    pairs = lat_pairs(n_lat, n_lon)
    second = lax.ppermute(second, ("lat", "lon"), pairs[1])
    first = lax.ppermute(first, ("lat", "lon"), pairs[0])

    return pl.pallas_call(
        step_kernel,
        out_shape=(shape_of(2, depth, rows, cols), shape_of(rows, cols), shape_of(2, rows, cols)),
        in_specs=vmem(15),
        out_specs=tuple(vmem(3)),
        scratch_shapes=[pltpu.VMEM((lat_rows, cols), F32), pltpu.VMEM((2 * depth, cols), F32)],
        compiler_params=params(),
        name="step",
    )(
        one, two, first, second, surface_height, transport, ocean_levels, flux, rim,
        t_0, edge_rows, inv, diffusivity, tracers, velocity,
    )


def solution(mesh):
    return jax.shard_map(
        per_device,
        mesh=mesh,
        in_specs=(
            P(None, None, "lat", "lon"),
            P(None, None, "lat", "lon"),
            P("lat", "lon"),
            P("lat", "lon"),
            P("lat", "lon"),
            P(None, "lat", "lon"),
            P("lat", None, "lon"),
            P("lat", "lon", None, None),
            P(None, "lat", "lon"),
            P(None, "lat", "lon"),
            P(None, "lat", "lon"),
            P("lat", "lon"),
        ),
        out_specs=(P(None, None, "lat", "lon"), P("lat", "lon"), P(None, "lat", "lon")),
        check_vma=False,
    )
```

```python
import jax
import jax.numpy as jnp
from jax import lax
from jax.experimental import pallas as pl
from jax.experimental.pallas import tpu as pltpu
from jax.sharding import PartitionSpec as P

SUBSTEPS = 6
HALO = 8
FIELDS = 7
HEIGHT, EAST, NORTH, LEVELS, FRESH, WIND_E, WIND_N = range(FIELDS)
ROW_RIM = FIELDS * HALO
ROW_T = ROW_RIM + HALO
LISTS = 256
OWNER, SLOT, USED = 32, 64, 96

adv_rate = 0.1
heat_gain = 0.5
salt_gain = 0.5
wave_div = 0.5
wave_grad = 0.8
fresh_gain = 0.2
wind_gain = 0.2

F32 = jnp.float32


def lanes(shape):
    return lax.broadcasted_iota(jnp.int32, shape, len(shape) - 1)


def rows_of(shape):
    return lax.broadcasted_iota(jnp.int32, shape, len(shape) - 2)


def turn(x, by, axis):
    size = x.shape[axis]
    by = by % size
    return x if by == 0 else pltpu.roll(x, by, axis)


def is_even(axis):
    return lax.rem(lax.axis_index(axis), 2) == 0


def is_top():
    return lax.axis_index("lat") == lax.axis_size("lat") - 1


def pick_kernel(atm_hbm, rows_hbm, out_ref, atm_ref, rows_ref, sems):
    copies = [
        pltpu.make_async_copy(atm_hbm, atm_ref, sems.at[0]),
        pltpu.make_async_copy(rows_hbm, rows_ref, sems.at[1]),
    ]
    for copy in copies:
        copy.start()
    for copy in copies:
        copy.wait()
    rows = rows_ref[0, 0]
    both = jnp.concatenate([rows, rows], axis=1)
    lane = both & 127
    part = both >> 7
    low = lanes(both.shape) < 64
    values = []
    for f in range(4):
        acc = None
        for k in range(atm_ref.shape[2] // 128):
            row = jnp.broadcast_to(atm_ref[0, f : f + 1, k * 128 : (k + 1) * 128], both.shape)
            value = jnp.take_along_axis(row, lane, axis=1)
            acc = value if k == 0 else jnp.where(part == k, value, acc)
        values.append(acc)
    out_ref[:, 0, 0:128] = jnp.where(low, values[0], values[1])
    out_ref[:, 0, 128:256] = jnp.where(low, values[2], values[3])
    for f in range(1, 4):
        at = 128 + f * 128
        out_ref[:, 0, at : at + 128] = jnp.where(low, turn(values[f], -1, 0), turn(values[f], 1, 0))


def edge_kernel(
    picked_ref, t_hbm, v_hbm, level_ref, height_ref, transport_ref, owner_ref, slot_ref, weight_ref, count_ref,
    two_ref, one_ref, t_0_ref, rows_ref, pick_row_ref, pick_lane_ref, used_ref, t_ref, v_ref, sems,
):
    copies = [
        pltpu.make_async_copy(t_hbm.at[0], t_ref.at[0], sems.at[0]),
        pltpu.make_async_copy(v_hbm.at[0], v_ref.at[0], sems.at[1]),
        pltpu.make_async_copy(t_hbm.at[1], t_ref.at[1], sems.at[2]),
        pltpu.make_async_copy(v_hbm.at[1], v_ref.at[1], sems.at[3]),
    ]
    for copy in copies:
        copy.start()
    depth = t_ref.shape[1]
    shape = t_ref.shape[2:]
    rows, cols = shape
    lane = lanes(shape)
    level = level_ref[...]
    half = lax.axis_size("lon") // 2
    count = count_ref[...]
    for k in range(owner_ref.shape[0]):
        owner = owner_ref[k]
        high = owner >= half
        pick_row_ref[k] = jnp.where(high, owner - half, owner)
        pick_lane_ref[k] = jnp.where(high, slot_ref[k] + 64, slot_ref[k])
        used_ref[k] = jnp.where(count > k, weight_ref[k], 0.0)
    fields = [height_ref[...], transport_ref[0], transport_ref[1], level.astype(F32)]
    fields += [owner_ref[k].astype(F32) for k in range(4)]
    fields += [slot_ref[k].astype(F32) for k in range(4)]
    fields += [used_ref[k] for k in range(4)]
    west = jnp.zeros(shape, F32)
    east = jnp.zeros(shape, F32)
    for g, field in enumerate(fields):
        here = (lane >= g * HALO) & (lane < (g + 1) * HALO)
        west = jnp.where(here, turn(field, g * HALO, 1), west)
        east = jnp.where(here, turn(field, (g + 1) * HALO, 1), east)
    west_t = jnp.zeros(shape, F32)
    east_t = jnp.zeros(shape, F32)
    for c in range(2):
        copies[2 * c].wait()
        for l in range(depth):
            f = c * depth + l
            moved = turn(t_ref[c, l], f + 1, 1)
            west_t = jnp.where(lane == f + 1, moved, west_t)
            east_t = jnp.where(lane == f, moved, east_t)
    copies[1].wait()
    for l in range(depth):
        at = 2 * depth + l
        east_t = jnp.where(lane == at, turn(v_ref[0, l], at + 1, 1), east_t)
    even = is_even("lon")
    one_ref[:rows] = jnp.where(even, east, west)
    two_ref[:rows] = jnp.where(even, west, east)
    one_ref[rows:] = jnp.where(even, east_t, west_t)
    two_ref[rows:] = jnp.where(even, west_t, east_t)
    t_0_ref[...] = turn(west_t, -1, 1)
    for c in range(2):
        for l in range(depth):
            at = c * depth + l
            rows_ref[0, at : at + 1] = t_ref[c, l, rows - 1 : rows]
            rows_ref[1, at : at + 1] = t_ref[c, l, 0:1]
    copies[3].wait()
    for l in range(depth):
        at = 2 * depth + l
        rows_ref[0, at : at + 1] = v_ref[1, l, rows - 1 : rows]
    rows_ref[1, 2 * depth :] = jnp.zeros((depth, cols), F32)

def own_lookup(tab, row_ref, lane_ref, used_ref, cut, fields):
    total = {f: None for f in fields}
    for k in range(used_ref.shape[0]):
        lane = lane_ref[k, cut]
        row = row_ref[k, cut]
        acc = {}
        for r in range(tab.shape[1]):
            here = row == r
            for f in fields:
                source = jnp.broadcast_to(tab[f, r : r + 1, :], lane.shape)
                value = jnp.take_along_axis(source, lane, axis=1)
                acc[f] = value if r == 0 else jnp.where(here, value, acc[f])
        used = used_ref[k, cut]
        for f in fields:
            total[f] = acc[f] * used if k == 0 else total[f] + acc[f] * used
    return total


def rim_of(east, west, by_east, by_west):
    lane = lanes(east.shape)
    outer = jnp.where(lane >= 128 - HALO, turn(west, by_west, 1), 0.0)
    return jnp.where(lane < HALO, turn(east, by_east, 1), outer)


def from_lon(one_ref, two_ref, cut):
    even = is_even("lon")
    one, two = one_ref[cut], two_ref[cut]
    return jnp.where(even, one, two), jnp.where(even, two, one)


def state_rims(east, west):
    return [rim_of(east, west, -g * HALO, 128 - (g + 1) * HALO) for g in range(4)]


def side_lookup(side, east, west):
    lane = lanes(east.shape)
    from_east = lane < 64
    valid = (lane >= 32) & (lane < 96)
    owner = jnp.where(valid, jnp.where(from_east, east, turn(west, 32, 1)), 0.0).astype(jnp.int32)
    slot = jnp.where(valid, jnp.where(from_east, turn(east, -32, 1), west), 0.0).astype(jnp.int32)
    used = jnp.where(valid, jnp.where(from_east, turn(east, -64, 1), turn(west, -32, 1)), 0.0)
    slot = jnp.where(from_east, slot, slot + 64)
    acc = [None] * 3
    for r in range(side.shape[1]):
        here = owner == r
        for f in range(3):
            source = jnp.broadcast_to(side[f, r : r + 1, :], slot.shape)
            value = jnp.take_along_axis(source, slot, axis=1)
            acc[f] = value if r == 0 else jnp.where(here, value, acc[f])
    rims = []
    for f in range(3):
        v = acc[f] * used
        v = v + turn(v, -16, 1)
        v = v + turn(v, -8, 1)
        rims.append(rim_of(v, v, -32, 56))
    return rims


def rim_lookup_kernel(
    table_ref, two_ref, one_ref, pick_row_ref, pick_lane_ref, used_ref, rows_ref, level_ref, height_ref,
    transport_ref, after_ref, second_ref, first_ref, flux_ref, rim_ref, tab, side, pack,
):
    n_lon = table_ref.shape[0]
    half = n_lon // 2
    rows, cols = height_ref.shape
    low = lanes((half, 128)) < 64
    for pair in range(2):
        part = table_ref[:, 0, pair * 128 : (pair + 1) * 128]
        lo, hi = part[:half], part[half:]
        tab[2 * pair] = jnp.where(low, lo, turn(hi, 64, 1))
        tab[2 * pair + 1] = jnp.where(low, turn(lo, 64, 1), hi)
    for f in range(3):
        side[f] = table_ref[:, 0, LISTS + f * 128 : LISTS + (f + 1) * 128]
    lane = lanes((HALO, cols))
    for s, at in ((0, rows - HALO), (1, 0)):
        cut = slice(at, at + HALO)
        found = own_lookup(tab, pick_row_ref, pick_lane_ref, used_ref, cut, (1, 2, 3))
        east, west = from_lon(one_ref, two_ref, cut)
        rims = side_lookup(side, east, west)
        for f in range(3):
            flux_ref[s, f] = found[f + 1]
            rim_ref[s, f] = rims[f]
        rims = state_rims(east, west) + rims
        own = [
            height_ref[cut], transport_ref[0, cut], transport_ref[1, cut], level_ref[cut].astype(F32),
            found[1], found[2], found[3],
        ]
        packed = jnp.zeros((HALO, cols), F32)
        for i in range(FIELDS):
            pack[s, i * HALO : (i + 1) * HALO] = own[i]
            start = 2 * HALO * i
            here = (lane >= start) & (lane < start + 2 * HALO)
            packed = jnp.where(here, turn(rims[i], start + HALO, 1), packed)
        pack[s, ROW_RIM:ROW_T] = packed
        pack[s, ROW_T:] = rows_ref[s]
    even = is_even("lat")
    north_going, south_going = pack[0], pack[1]
    second_ref[...] = jnp.where(even, south_going, north_going)
    first_ref[...] = jnp.where(even, north_going, south_going)


def lookup_kernel(
    edge_flux_ref, edge_rim_ref, tab, side, two_ref, one_ref, pick_row_ref, pick_lane_ref, used_ref,
    flux_ref, rim_ref,
):
    rows = used_ref.shape[1]
    for at in range(0, rows, HALO):
        cut = slice(at, at + HALO)
        inner = 0 < at < rows - HALO
        found = own_lookup(tab, pick_row_ref, pick_lane_ref, used_ref, cut, (0, 1, 2, 3) if inner else (0,))
        s = 1 if at == 0 else 0
        flux_ref[0, cut] = found[0]
        for f in range(1, 4):
            flux_ref[f, cut] = found[f] if inner else edge_flux_ref[s, f - 1]
        east, west = from_lon(one_ref, two_ref, cut)
        rims = state_rims(east, west)
        if inner:
            rims += side_lookup(side, east, west)
        else:
            rims += [edge_rim_ref[s, f] for f in range(3)]
        for i in range(FIELDS):
            rim_ref[i, cut] = rims[i]


def tracer_kernel(
    two_ref, one_ref, t_0_ref, level_ref, diff_ref, t_ref, v_ref, x_ref, unit_ref, inv_rows_ref, gain_ref,
):
    depth, rows, cols = t_ref.shape[1:]
    shape = (rows, cols)
    east, west = from_lon(one_ref, two_ref, slice(0, rows))
    t_e, t_w = from_lon(one_ref, two_ref, slice(rows, 2 * rows))
    level = level_ref[...]
    level_f = level.astype(F32)
    lane = lanes(shape)
    row = rows_of(shape)
    first = LEVELS * HALO
    last = cols - 1
    level_e = jnp.where(lane == last, turn(east, last - first, 1), turn(level_f, -1, 1))
    level_n = turn(level_f, -1, 0)
    face_e = jnp.minimum(level_f, level_e)
    face_n = jnp.where(row == rows - 1, 0.0, jnp.minimum(level_f, level_n))
    t_0 = t_0_ref[...]
    u_w = jnp.where(lane < depth, turn(t_w, -2 * depth, 1), turn(t_w, -depth, 1))
    layer = jnp.where(lane < depth, lane, lane - depth).astype(F32)
    level_w = west[:, first + HALO - 1 : first + HALO]
    face_w = jnp.broadcast_to(jnp.minimum(level_f[:, 0:1], level_w), shape)
    west_flux = jnp.where(layer < face_w, u_w * ((t_w + t_0) * 0.5), 0.0)
    diff = diff_ref[...]
    above = jnp.zeros(shape, F32)
    inv = None
    right = [None, None, None]
    for l in range(depth):
        below = jnp.where(level > l + 1, diff, 0.0) if l < depth - 1 else jnp.zeros(shape, F32)
        pivot = 1.0 + above + below
        if l > 0:
            pivot = pivot - above * above * inv
        inv = 1.0 / pivot
        inv_rows_ref[0, l : l + 1] = inv[rows - 1 : rows]
        inv_rows_ref[1, l : l + 1] = inv[0:1]
        gain_ref[l] = below * inv
        mask_e = face_e > l
        mask_n = face_n > l
        u_l, v_l = v_ref[0, l] * 0.5, v_ref[1, l] * 0.5
        for c in range(2):
            f = c * depth + l
            t = t_ref[c, l]
            t_east = jnp.where(lane == last, turn(t_e, last - 1 - f, 1), turn(t, -1, 1))
            flux_e = jnp.where(mask_e, u_l * (t + t_east), 0.0)
            flux_w = jnp.where(lane == 0, turn(west_flux, -f, 1), turn(flux_e, 1, 1))
            flux_n = jnp.where(mask_n, v_l * (t + turn(t, -1, 0)), 0.0)
            flux_s = turn(flux_n, 1, 0)
            forced = t - adv_rate * ((flux_e - flux_w) + (flux_n - flux_s))
            right[c] = forced * inv if l == 0 else (forced + above * right[c]) * inv
            x_ref[c, l] = right[c]
        right[2] = inv if l == 0 else above * right[2] * inv
        unit_ref[l] = right[2]
        above = below
    for l in range(depth - 2, -1, -1):
        gain = gain_ref[l]
        for c in range(2):
            right[c] = x_ref[c, l] + gain * right[c]
            x_ref[c, l] = right[c]
        right[2] = unit_ref[l] + gain * right[2]
        unit_ref[l] = right[2]


def step_kernel(
    second_ref, first_ref, height_ref, transport_ref, level_ref, diff_ref, flux_ref, rim_ref, rows_ref, inv_rows_ref,
    x_ref, unit_ref, t_out, height_out, transport_out, north_ref, shift, fixed, sems,
):
    top = is_top()
    level = level_ref[...]
    level_f = level.astype(F32)
    rows, cols = level.shape
    depth = x_ref.shape[1]
    even = is_even("lat")
    a, b = first_ref[...], second_ref[...]
    south = jnp.where(even, b, a)
    north = jnp.where(even, a, b)
    mirrored = jnp.take_along_axis(north, 127 - lanes(north.shape), axis=1)
    north = jnp.where(top, mirrored, north)
    north_ref[...] = north

    first = LEVELS * HALO
    level_n = jnp.where(top, north[first + HALO - 1 : first + HALO], north[first : first + 1])
    level_s = south[first + HALO - 1 : first + HALO]
    sides = ((north, level_n, rows - 1, -adv_rate), (south, level_s, 0, adv_rate))
    chains = []
    for s, (message, level_out, at, gain) in enumerate(sides):
        level_in = level_f[at : at + 1]
        face = jnp.minimum(level_in, level_out)
        speed = rows_ref[0, 2 * depth :] if s == 0 else message[ROW_T + 2 * depth :]
        for c in range(2):
            planes = slice(c * depth, (c + 1) * depth)
            outside = message[ROW_T + c * depth : ROW_T + (c + 1) * depth]
            flux = speed * ((outside + rows_ref[s, planes]) * 0.5)
            deep = rows_of(flux.shape).astype(F32) < face
            shift[s, planes] = jnp.where(deep, gain * flux, 0.0)
            chains.append((s, c, level_in, diff_ref[at : at + 1]))
    right = [None] * 4
    for l in range(depth):
        for i, (s, c, level_in, diff_in) in enumerate(chains):
            at = c * depth + l
            inv = inv_rows_ref[s, l : l + 1]
            value = shift[s, at : at + 1]
            if l > 0:
                value = value + jnp.where(level_in > l, diff_in, 0.0) * right[i]
            right[i] = value * inv
            shift[s, at : at + 1] = right[i]
    for l in range(depth - 2, -1, -1):
        for i, (s, c, level_in, diff_in) in enumerate(chains):
            at = c * depth + l
            inv = inv_rows_ref[s, l : l + 1]
            below = jnp.where(level_in > l + 1, diff_in, 0.0) * inv
            right[i] = shift[s, at : at + 1] + below * right[i]
            shift[s, at : at + 1] = right[i]
    wet_0 = (level > 0).astype(F32)
    source = (heat_gain * flux_ref[0] * wet_0, -salt_gain * flux_ref[1] * wet_0)
    row = rows_of((HALO, cols))
    lo, hi = slice(0, HALO), slice(rows - HALO, rows)
    mid = slice(HALO, rows - HALO)
    copies = []
    for c in range(2):
        for l in range(depth):
            at = c * depth + l
            x = x_ref[c, l] + unit_ref[l] * source[c]
            add_s = jnp.broadcast_to(shift[1, at : at + 1], (HALO, cols))
            add_n = jnp.broadcast_to(shift[0, at : at + 1], (HALO, cols))
            fixed[c, l, lo] = x[lo] + jnp.where(row == 0, add_s, 0.0)
            fixed[c, l, mid] = x[mid]
            fixed[c, l, hi] = x[hi] + jnp.where(row == HALO - 1, add_n, 0.0)
        copies.append(pltpu.make_async_copy(fixed.at[c], t_out.at[c], sems.at[c]))
        copies[c].start()

    own = (
        height_ref[...], transport_ref[0], transport_ref[1], level_f,
        flux_ref[1], flux_ref[2], flux_ref[3],
    )
    ext = []
    lane = lanes((HALO, cols))
    side = (lane < HALO) | (lane >= cols - HALO)
    for i in range(FIELDS):
        at = slice(i * HALO, (i + 1) * HALO)
        whole = jnp.concatenate([south[at], own[i], north[at]], axis=0)
        start = jnp.where(top, cols - 2 * HALO * (FIELDS - i) - HALO, cols - 2 * HALO * i - HALO)
        north_rim = jnp.where(side, pltpu.roll(north[ROW_RIM:ROW_T], start, 1), 0.0)
        south_rim = jnp.where(side, turn(south[ROW_RIM:ROW_T], -(2 * HALO * i + HALO), 1), 0.0)
        rim = jnp.concatenate([south_rim, rim_ref[i], north_rim], axis=0)
        ext.append(jnp.concatenate([whole, rim], axis=1))


    def coefficients(f):
        wet = (f[LEVELS] > 0.0).astype(F32)
        return (
            wet,
            wave_grad * (f[LEVELS] / depth),
            fresh_gain * f[FRESH] * wet,
            wind_gain * f[WIND_E] * wet,
            wind_gain * f[WIND_N] * wet,
        )

    mine = [x for x in ext]
    fold = [x[HALO + rows :] for x in ext]
    wet, grad, fresh, wind_e, wind_n = coefficients(mine)
    p_wet, p_grad, p_fresh, p_wind_e, p_wind_n = coefficients(fold)
    h, e, n = mine[HEIGHT], mine[EAST], mine[NORTH]
    p_h, p_e, p_n = fold[HEIGHT], fold[EAST], fold[NORTH]
    row = rows_of(h.shape)
    last = HALO + rows - 1
    across = (row == last) & top
    p_last = rows_of(p_h.shape) == HALO - 1
    for _ in range(SUBSTEPS):
        h = (h - wave_div * ((e - turn(e, 1, 1)) + (n - turn(n, 1, 0)))) * wet + fresh
        p_h = (p_h - wave_div * ((p_e - turn(p_e, -1, 1)) + (p_n - turn(p_n, 1, 0)))) * p_wet + p_fresh
        h_n = jnp.where(across, jnp.broadcast_to(p_h[HALO - 1 :], h.shape), turn(h, -1, 0))
        p_h_n = jnp.where(p_last, jnp.broadcast_to(h[last : last + 1], p_h.shape), turn(p_h, -1, 0))
        e = (e - grad * (turn(h, -1, 1) - h)) * wet + wind_e
        n = (n - grad * (h_n - h)) * wet + wind_n
        p_e = (p_e - p_grad * (turn(p_h, 1, 1) - p_h)) * p_wet + p_wind_e
        p_n = (p_n - p_grad * (p_h_n - p_h)) * p_wet + p_wind_n
    inside = slice(HALO, HALO + rows)
    height_out[...] = h[inside, :cols]
    transport_out[0] = e[inside, :cols]
    transport_out[1] = n[inside, :cols]

    for copy in copies:
        copy.wait()


def vmem(count):
    return [pl.BlockSpec(memory_space=pltpu.VMEM)] * count


def params(mib=24):
    return pltpu.CompilerParams(vmem_limit_bytes=mib * 1024 * 1024)


def work(mb):
    return pl.CostEstimate(flops=mb * 1000000, bytes_accessed=mb * 1000000, transcendentals=0)


def in_hbm(x):
    return pltpu.with_memory_space_constraint(x, pltpu.HBM)


def shape_of(*shape):
    return jax.ShapeDtypeStruct(shape, F32)


def lat_pairs(n_lat, n_lon):
    def at(i, j):
        return i * n_lon + j

    first, second = [], []
    for j in range(n_lon):
        for i in range(0, n_lat, 2):
            first += [(at(i, j), at(i + 1, j)), (at(i + 1, j), at(i, j))]
        for i in range(1, n_lat - 1, 2):
            second += [(at(i, j), at(i + 1, j)), (at(i + 1, j), at(i, j))]
        second.append((at(n_lat - 1, j), at(n_lat - 1, n_lon - 1 - j)))
    return first, second


def lon_pairs(n_lon):
    first, second = [], []
    for j in range(0, n_lon, 2):
        first += [(j, j + 1), (j + 1, j)]
        k, m = j + 1, (j + 2) % n_lon
        second += [(k, m), (m, k)]
    return first, second


def per_device(
    tracers,
    velocity,
    diffusivity,
    ocean_levels,
    surface_height,
    transport,
    atm_flux,
    send_rows,
    src_owner,
    src_slot,
    xgrid_weights,
    xgrid_count,
):
    n_lat, n_lon = lax.axis_size("lat"), lax.axis_size("lon")
    depth, rows, cols = tracers.shape[1:]
    slots = send_rows.shape[3]
    picked = pl.pallas_call(
        pick_kernel,
        out_shape=shape_of(n_lon, 1, 10 * slots),
        in_specs=[pl.BlockSpec(memory_space=pltpu.HBM)] * 2,
        out_specs=vmem(1)[0],
        scratch_shapes=[
            pltpu.VMEM(atm_flux.shape, F32),
            pltpu.VMEM(send_rows.shape, jnp.int32),
            pltpu.SemaphoreType.DMA((2,)),
        ],
        compiler_params=params(24),
        cost_estimate=work(40),
        name="pick",
    )(in_hbm(atm_flux), in_hbm(send_rows))
    table = lax.all_to_all(picked, "lon", split_axis=0, concat_axis=0, tiled=True)

    block = (rows, cols)
    lat_rows = ROW_T + 3 * depth
    two, one, t_0, edge_rows, pick_row, pick_lane, used, tracers, velocity = pl.pallas_call(
        edge_kernel,
        out_shape=(
            shape_of(2 * rows, cols),
            shape_of(2 * rows, cols),
            shape_of(*block),
            shape_of(2, 3 * depth, cols),
            jax.ShapeDtypeStruct((4, *block), jnp.int32),
            jax.ShapeDtypeStruct((4, *block), jnp.int32),
            shape_of(4, *block),
            shape_of(2, depth, *block),
            shape_of(2, depth, *block),
        ),
        in_specs=[pl.BlockSpec(memory_space=pl.ANY)] + [pl.BlockSpec(memory_space=pltpu.HBM)] * 2 + vmem(7),
        out_specs=vmem(9),
        scratch_shapes=[pltpu.SemaphoreType.DMA((4,))],
        compiler_params=params(),
        cost_estimate=work(2),
        name="edges",
    )(
        picked, in_hbm(tracers), in_hbm(velocity), ocean_levels, surface_height, transport, src_owner, src_slot,
        xgrid_weights, xgrid_count,
    )
    pairs = lon_pairs(n_lon)
    two = lax.ppermute(two, "lon", pairs[1])
    one = lax.ppermute(one, "lon", pairs[0])

    solved, unit, inv_rows = pl.pallas_call(
        tracer_kernel,
        out_shape=(shape_of(2, depth, *block), shape_of(depth, *block), shape_of(2, depth, cols)),
        in_specs=vmem(7),
        out_specs=vmem(3),
        scratch_shapes=[pltpu.VMEM((depth, *block), F32)],
        compiler_params=params(),
        cost_estimate=work(8),
        name="tracers",
    )(two, one, t_0, ocean_levels, diffusivity, tracers, velocity)

    second, first, edge_flux, edge_rim, tab, side = pl.pallas_call(
        rim_lookup_kernel,
        out_shape=(
            shape_of(lat_rows, cols),
            shape_of(lat_rows, cols),
            shape_of(2, 3, HALO, cols),
            shape_of(2, 3, HALO, cols),
            shape_of(4, n_lon // 2, 128),
            shape_of(3, n_lon, 128),
        ),
        in_specs=vmem(10) + [pl.BlockSpec(memory_space=pl.ANY)],
        out_specs=vmem(6),
        scratch_shapes=[pltpu.VMEM((2, lat_rows, cols), F32)],
        compiler_params=params(),
        cost_estimate=work(8),
        name="rim_lookup",
    )(
        table, two, one, pick_row, pick_lane, used, edge_rows, ocean_levels, surface_height, transport,
        inv_rows,
    )
    pairs = lat_pairs(n_lat, n_lon)
    second = lax.ppermute(second, ("lat", "lon"), pairs[1])
    first = lax.ppermute(first, ("lat", "lon"), pairs[0])

    flux, rim = pl.pallas_call(
        lookup_kernel,
        out_shape=(shape_of(4, *block), shape_of(FIELDS, *block)),
        in_specs=vmem(9),
        out_specs=vmem(2),
        compiler_params=params(),
        cost_estimate=work(8),
        name="lookup",
    )(edge_flux, edge_rim, tab, side, two, one, pick_row, pick_lane, used)

    return pl.pallas_call(
        step_kernel,
        out_shape=(shape_of(2, depth, rows, cols), shape_of(rows, cols), shape_of(2, rows, cols)),
        in_specs=vmem(12),
        out_specs=(pl.BlockSpec(memory_space=pl.ANY), *vmem(2)),
        scratch_shapes=[
            pltpu.VMEM((lat_rows, cols), F32),
            pltpu.VMEM((2, 2 * depth, cols), F32),
            pltpu.VMEM((2, depth, rows, cols), F32),
            pltpu.SemaphoreType.DMA((2,)),
        ],
        compiler_params=params(),
        name="step",
    )(
        second, first, surface_height, transport, ocean_levels, diffusivity, flux, rim, edge_rows, inv_rows,
        solved, unit,
    )


def solution(mesh):
    return jax.shard_map(
        per_device,
        mesh=mesh,
        in_specs=(
            P(None, None, "lat", "lon"),
            P(None, None, "lat", "lon"),
            P("lat", "lon"),
            P("lat", "lon"),
            P("lat", "lon"),
            P(None, "lat", "lon"),
            P("lat", None, "lon"),
            P("lat", "lon", None, None),
            P(None, "lat", "lon"),
            P(None, "lat", "lon"),
            P(None, "lat", "lon"),
            P("lat", "lon"),
        ),
        out_specs=(P(None, None, "lat", "lon"), P("lat", "lon"), P(None, "lat", "lon")),
        check_vma=False,
    )
```

```python
import jax
import jax.numpy as jnp
from jax import lax
from jax.experimental import pallas as pl
from jax.experimental.pallas import tpu as pltpu
from jax.sharding import PartitionSpec as P

SUBSTEPS = 6
HALO = 8
FIELDS = 7
HEIGHT, EAST, NORTH, LEVELS, FRESH, WIND_E, WIND_N = range(FIELDS)
ROW_RIM = FIELDS * HALO
ROW_T = ROW_RIM + HALO
LISTS = 256
OWNER, SLOT, USED = 32, 64, 96

adv_rate = 0.1
heat_gain = 0.5
salt_gain = 0.5
wave_div = 0.5
wave_grad = 0.8
fresh_gain = 0.2
wind_gain = 0.2

F32 = jnp.float32


def lanes(shape):
    return lax.broadcasted_iota(jnp.int32, shape, len(shape) - 1)


def rows_of(shape):
    return lax.broadcasted_iota(jnp.int32, shape, len(shape) - 2)


def turn(x, by, axis):
    size = x.shape[axis]
    by = by % size
    return x if by == 0 else pltpu.roll(x, by, axis)


def is_even(axis):
    return lax.rem(lax.axis_index(axis), 2) == 0


def is_top():
    return lax.axis_index("lat") == lax.axis_size("lat") - 1


def pick_kernel(atm_hbm, rows_hbm, out_ref, atm_ref, rows_ref, sems):
    copies = [
        pltpu.make_async_copy(atm_hbm, atm_ref, sems.at[0]),
        pltpu.make_async_copy(rows_hbm, rows_ref, sems.at[1]),
    ]
    for copy in copies:
        copy.start()
    for copy in copies:
        copy.wait()
    rows = rows_ref[0, 0]
    both = jnp.concatenate([rows, rows], axis=1)
    lane = both & 127
    part = both >> 7
    low = lanes(both.shape) < 64
    values = []
    for f in range(4):
        acc = None
        for k in range(atm_ref.shape[2] // 128):
            row = jnp.broadcast_to(atm_ref[0, f : f + 1, k * 128 : (k + 1) * 128], both.shape)
            value = jnp.take_along_axis(row, lane, axis=1)
            acc = value if k == 0 else jnp.where(part == k, value, acc)
        values.append(acc)
    out_ref[:, 0, 0:128] = jnp.where(low, values[0], values[1])
    out_ref[:, 0, 128:256] = jnp.where(low, values[2], values[3])
    for f in range(1, 4):
        at = 128 + f * 128
        out_ref[:, 0, at : at + 128] = jnp.where(low, turn(values[f], -1, 0), turn(values[f], 1, 0))


def edge_kernel(
    picked_ref, t_hbm, v_hbm, level_ref, height_ref, transport_ref, owner_ref, slot_ref, weight_ref, count_ref,
    two_ref, one_ref, t_0_ref, rows_ref, pick_row_ref, pick_lane_ref, used_ref, t_ref, v_ref, sems,
):
    copies = [
        pltpu.make_async_copy(t_hbm.at[0], t_ref.at[0], sems.at[0]),
        pltpu.make_async_copy(v_hbm.at[0], v_ref.at[0], sems.at[1]),
        pltpu.make_async_copy(t_hbm.at[1], t_ref.at[1], sems.at[2]),
        pltpu.make_async_copy(v_hbm.at[1], v_ref.at[1], sems.at[3]),
    ]
    for copy in copies:
        copy.start()
    depth = t_ref.shape[1]
    shape = t_ref.shape[2:]
    rows, cols = shape
    lane = lanes(shape)
    level = level_ref[...]
    half = lax.axis_size("lon") // 2
    count = count_ref[...]
    for k in range(owner_ref.shape[0]):
        owner = owner_ref[k]
        high = owner >= half
        pick_row_ref[k] = jnp.where(high, owner - half, owner)
        pick_lane_ref[k] = jnp.where(high, slot_ref[k] + 64, slot_ref[k])
        used_ref[k] = jnp.where(count > k, weight_ref[k], 0.0)
    fields = [height_ref[...], transport_ref[0], transport_ref[1], level.astype(F32)]
    fields += [owner_ref[k].astype(F32) for k in range(4)]
    fields += [slot_ref[k].astype(F32) for k in range(4)]
    fields += [used_ref[k] for k in range(4)]
    west = jnp.zeros(shape, F32)
    east = jnp.zeros(shape, F32)
    for g, field in enumerate(fields):
        here = (lane >= g * HALO) & (lane < (g + 1) * HALO)
        west = jnp.where(here, turn(field, g * HALO, 1), west)
        east = jnp.where(here, turn(field, (g + 1) * HALO, 1), east)
    west_t = jnp.zeros(shape, F32)
    east_t = jnp.zeros(shape, F32)
    for c in range(2):
        copies[2 * c].wait()
        for l in range(depth):
            f = c * depth + l
            moved = turn(t_ref[c, l], f + 1, 1)
            west_t = jnp.where(lane == f + 1, moved, west_t)
            east_t = jnp.where(lane == f, moved, east_t)
    copies[1].wait()
    for l in range(depth):
        at = 2 * depth + l
        east_t = jnp.where(lane == at, turn(v_ref[0, l], at + 1, 1), east_t)
    even = is_even("lon")
    one_ref[:rows] = jnp.where(even, east, west)
    two_ref[:rows] = jnp.where(even, west, east)
    one_ref[rows:] = jnp.where(even, east_t, west_t)
    two_ref[rows:] = jnp.where(even, west_t, east_t)
    t_0_ref[...] = turn(west_t, -1, 1)
    for c in range(2):
        for l in range(depth):
            at = c * depth + l
            rows_ref[0, at : at + 1] = t_ref[c, l, rows - 1 : rows]
            rows_ref[1, at : at + 1] = t_ref[c, l, 0:1]
    copies[3].wait()
    for l in range(depth):
        at = 2 * depth + l
        rows_ref[0, at : at + 1] = v_ref[1, l, rows - 1 : rows]
    rows_ref[1, 2 * depth :] = jnp.zeros((depth, cols), F32)

def own_lookup(tab, row_ref, lane_ref, used_ref, cut, fields):
    total = {f: None for f in fields}
    for k in range(used_ref.shape[0]):
        lane = lane_ref[k, cut]
        row = row_ref[k, cut]
        acc = {}
        for r in range(tab.shape[1]):
            here = row == r
            for f in fields:
                source = jnp.broadcast_to(tab[f, r : r + 1, :], lane.shape)
                value = jnp.take_along_axis(source, lane, axis=1)
                acc[f] = value if r == 0 else jnp.where(here, value, acc[f])
        used = used_ref[k, cut]
        for f in fields:
            total[f] = acc[f] * used if k == 0 else total[f] + acc[f] * used
    return total


def rim_of(east, west, by_east, by_west):
    lane = lanes(east.shape)
    outer = jnp.where(lane >= 128 - HALO, turn(west, by_west, 1), 0.0)
    return jnp.where(lane < HALO, turn(east, by_east, 1), outer)


def from_lon(one_ref, two_ref, cut):
    even = is_even("lon")
    one, two = one_ref[cut], two_ref[cut]
    return jnp.where(even, one, two), jnp.where(even, two, one)


def state_rims(east, west):
    return [rim_of(east, west, -g * HALO, 128 - (g + 1) * HALO) for g in range(4)]


def side_lookup(side, sides):
    (east, west), (east_2, west_2) = sides
    lane = lanes(east.shape)
    quarter = lane >> 5

    def gathered(by):
        parts = (turn(west_2, -32 - by, 1), turn(east, -by, 1), turn(west, 32 - by, 1), turn(east_2, 64 - by, 1))
        low = jnp.where(quarter == 0, parts[0], parts[1])
        return jnp.where(quarter < 2, low, jnp.where(quarter == 2, parts[2], parts[3]))

    owner = gathered(0).astype(jnp.int32)
    slot = gathered(32).astype(jnp.int32)
    used = gathered(64)
    slot = jnp.where((quarter & 1) == 0, slot + 64, slot)
    acc = [None] * 3
    for r in range(side.shape[1]):
        here = owner == r
        for f in range(3):
            source = jnp.broadcast_to(side[f, r : r + 1, :], slot.shape)
            value = jnp.take_along_axis(source, slot, axis=1)
            acc[f] = value if r == 0 else jnp.where(here, value, acc[f])
    rims = ([], [])
    for f in range(3):
        v = acc[f] * used
        v = v + turn(v, -16, 1)
        v = v + turn(v, -8, 1)
        rims[0].append(rim_of(v, v, -32, 56))
        rims[1].append(rim_of(v, v, -96, 120))
    return rims


def rim_lookup_kernel(
    table_ref, two_ref, one_ref, pick_row_ref, pick_lane_ref, used_ref, rows_ref, level_ref, height_ref,
    transport_ref, after_ref, second_ref, first_ref, flux_ref, rim_ref, tab, side, pack,
):
    n_lon = table_ref.shape[0]
    half = n_lon // 2
    rows, cols = height_ref.shape
    low = lanes((half, 128)) < 64
    for pair in range(2):
        part = table_ref[:, 0, pair * 128 : (pair + 1) * 128]
        lo, hi = part[:half], part[half:]
        tab[2 * pair] = jnp.where(low, lo, turn(hi, 64, 1))
        tab[2 * pair + 1] = jnp.where(low, turn(lo, 64, 1), hi)
    for f in range(3):
        side[f] = table_ref[:, 0, LISTS + f * 128 : LISTS + (f + 1) * 128]
    lane = lanes((HALO, cols))
    cuts = (slice(rows - HALO, rows), slice(0, HALO))
    sides = [from_lon(one_ref, two_ref, cut) for cut in cuts]
    side_rims = side_lookup(side, sides)
    for s, cut in enumerate(cuts):
        found = own_lookup(tab, pick_row_ref, pick_lane_ref, used_ref, cut, (1, 2, 3))
        for f in range(3):
            flux_ref[s, f] = found[f + 1]
            rim_ref[s, f] = side_rims[s][f]
        rims = state_rims(*sides[s]) + side_rims[s]
        own = [
            height_ref[cut], transport_ref[0, cut], transport_ref[1, cut], level_ref[cut].astype(F32),
            found[1], found[2], found[3],
        ]
        packed = jnp.zeros((HALO, cols), F32)
        for i in range(FIELDS):
            pack[s, i * HALO : (i + 1) * HALO] = own[i]
            start = 2 * HALO * i
            here = (lane >= start) & (lane < start + 2 * HALO)
            packed = jnp.where(here, turn(rims[i], start + HALO, 1), packed)
        pack[s, ROW_RIM:ROW_T] = packed
        pack[s, ROW_T:] = rows_ref[s]
    even = is_even("lat")
    north_going, south_going = pack[0], pack[1]
    second_ref[...] = jnp.where(even, south_going, north_going)
    first_ref[...] = jnp.where(even, north_going, south_going)


def lookup_kernel(
    edge_flux_ref, edge_rim_ref, tab, side, two_ref, one_ref, pick_row_ref, pick_lane_ref, used_ref,
    flux_ref, rim_ref,
):
    rows = used_ref.shape[1]
    cuts = [slice(at, at + HALO) for at in range(0, rows, HALO)]
    sides = [from_lon(one_ref, two_ref, cut) for cut in cuts]
    for at in range(1, len(cuts) - 1, 2):
        side_rims = side_lookup(side, sides[at : at + 2])
        for i in range(2):
            cut = cuts[at + i]
            found = own_lookup(tab, pick_row_ref, pick_lane_ref, used_ref, cut, (0, 1, 2, 3))
            for f in range(4):
                flux_ref[f, cut] = found[f]
            for g, rim in enumerate(state_rims(*sides[at + i]) + side_rims[i]):
                rim_ref[g, cut] = rim
    for s, at in ((0, len(cuts) - 1), (1, 0)):
        cut = cuts[at]
        flux_ref[0, cut] = own_lookup(tab, pick_row_ref, pick_lane_ref, used_ref, cut, (0,))[0]
        for f in range(3):
            flux_ref[f + 1, cut] = edge_flux_ref[s, f]
        for g, rim in enumerate(state_rims(*sides[at]) + [edge_rim_ref[s, f] for f in range(3)]):
            rim_ref[g, cut] = rim


def split(x):
    hi = x.astype(jnp.bfloat16)
    return hi, (x - hi.astype(F32)).astype(jnp.bfloat16)


def tracer_kernel(
    two_ref, one_ref, t_0_ref, level_ref, diff_ref, t_ref, v_ref, x_ref, unit_ref, inv_rows_ref, gain_ref,
    parts, rims, net_x,
):
    depth, rows, cols = t_ref.shape[1:]
    shape = (rows, cols)
    east, west = from_lon(one_ref, two_ref, slice(0, rows))
    t_e, t_w = from_lon(one_ref, two_ref, slice(rows, 2 * rows))
    level = level_ref[...]
    level_f = level.astype(F32)
    lane = lanes(shape)
    row = rows_of(shape)
    first = LEVELS * HALO
    last = cols - 1
    level_e = jnp.where(lane == last, turn(east, last - first, 1), turn(level_f, -1, 1))
    level_n = turn(level_f, -1, 0)
    face_e = jnp.minimum(level_f, level_e)
    face_n = jnp.where(row == rows - 1, 0.0, jnp.minimum(level_f, level_n))
    t_0 = t_0_ref[...]
    u_w = jnp.where(lane < depth, turn(t_w, -2 * depth, 1), turn(t_w, -depth, 1))
    layer = jnp.where(lane < depth, lane, lane - depth).astype(F32)
    level_w = west[:, first + HALO - 1 : first + HALO]
    face_w = jnp.broadcast_to(jnp.minimum(level_f[:, 0:1], level_w), shape)
    west_flux = jnp.where((layer < face_w) & (lane < 2 * depth), u_w * ((t_w + t_0) * 0.5), 0.0)
    both = []
    for x in (turn(t_e, -1, 1), west_flux):
        hi, lo = split(x)
        both.append(jnp.where(lane < 64, hi.astype(F32), turn(lo.astype(F32), 64, 1)))
    plane = lane & 63
    for f in range(2 * depth):
        at = slice(f * rows, (f + 1) * rows)
        here = plane == f
        parts[at, 0:128] = jnp.where(here, both[0], 0.0).astype(jnp.bfloat16)
        parts[at, 128:256] = jnp.where(here, both[1], 0.0).astype(jnp.bfloat16)
    k = lax.broadcasted_iota(jnp.int32, (2 * cols, cols), 0)
    into = jnp.where(k < cols, last, 0) == lanes((2 * cols, cols))
    rims[...] = jnp.dot(parts[...], into.astype(F32).astype(jnp.bfloat16), preferred_element_type=F32)
    for l in range(depth):
        mask_e = face_e > l
        u_l = v_ref[0, l] * 0.5
        for c in range(2):
            f = c * depth + l
            at = slice(f * rows, (f + 1) * rows)
            t = t_ref[c, l]
            t_east = jnp.where(lane == last, rims[at], turn(t, -1, 1))
            flux_e = jnp.where(mask_e, u_l * (t + t_east), 0.0)
            net_x[at] = flux_e - jnp.where(lane == 0, rims[at], turn(flux_e, 1, 1))
    diff = diff_ref[...]
    above = jnp.zeros(shape, F32)
    inv = None
    right = [None, None, None]
    for l in range(depth):
        below = jnp.where(level > l + 1, diff, 0.0) if l < depth - 1 else jnp.zeros(shape, F32)
        pivot = 1.0 + above + below
        if l > 0:
            pivot = pivot - above * above * inv
        inv = 1.0 / pivot
        inv_rows_ref[0, l : l + 1] = inv[rows - 1 : rows]
        inv_rows_ref[1, l : l + 1] = inv[0:1]
        gain_ref[l] = below * inv
        mask_n = face_n > l
        v_l = v_ref[1, l] * 0.5
        for c in range(2):
            f = c * depth + l
            at = slice(f * rows, (f + 1) * rows)
            t = t_ref[c, l]
            flux_n = jnp.where(mask_n, v_l * (t + turn(t, -1, 0)), 0.0)
            flux_s = turn(flux_n, 1, 0)
            forced = t - adv_rate * (net_x[at] + (flux_n - flux_s))
            right[c] = forced * inv if l == 0 else (forced + above * right[c]) * inv
            x_ref[c, l] = right[c]
        right[2] = inv if l == 0 else above * right[2] * inv
        unit_ref[l] = right[2]
        above = below
    for l in range(depth - 2, -1, -1):
        gain = gain_ref[l]
        for c in range(2):
            right[c] = x_ref[c, l] + gain * right[c]
            x_ref[c, l] = right[c]
        right[2] = unit_ref[l] + gain * right[2]
        unit_ref[l] = right[2]


def step_kernel(
    second_ref, first_ref, height_ref, transport_ref, level_ref, diff_ref, flux_ref, rim_ref, rows_ref, inv_rows_ref,
    x_ref, unit_ref, t_out, height_out, transport_out, north_ref, shift, fixed, result, sems,
):
    top = is_top()
    level = level_ref[...]
    level_f = level.astype(F32)
    rows, cols = level.shape
    depth = x_ref.shape[1]
    wet_0 = (level > 0).astype(F32)
    source = (heat_gain * flux_ref[0] * wet_0, -salt_gain * flux_ref[1] * wet_0)
    lo, hi = slice(0, HALO), slice(rows - HALO, rows)
    mid = slice(HALO, rows - HALO)
    copies = []

    def send(value, out):
        copies.append(pltpu.make_async_copy(value, out, sems.at[len(copies)]))
        copies[-1].start()

    for c in range(2):
        for l in range(depth):
            fixed[c, l, mid] = x_ref[c, l, mid] + unit_ref[l, mid] * source[c][mid]
        send(fixed.at[c, :, mid], t_out.at[c, :, mid])
    even = is_even("lat")
    a, b = first_ref[...], second_ref[...]
    south = jnp.where(even, b, a)
    north = jnp.where(even, a, b)
    mirrored = jnp.take_along_axis(north, 127 - lanes(north.shape), axis=1)
    north = jnp.where(top, mirrored, north)
    north_ref[...] = north

    first = LEVELS * HALO
    level_n = jnp.where(top, north[first + HALO - 1 : first + HALO], north[first : first + 1])
    level_s = south[first + HALO - 1 : first + HALO]
    sides = ((north, level_n, rows - 1, -adv_rate), (south, level_s, 0, adv_rate))
    chains = []
    for s, (message, level_out, at, gain) in enumerate(sides):
        level_in = level_f[at : at + 1]
        face = jnp.minimum(level_in, level_out)
        speed = rows_ref[0, 2 * depth :] if s == 0 else message[ROW_T + 2 * depth :]
        for c in range(2):
            planes = slice(c * depth, (c + 1) * depth)
            outside = message[ROW_T + c * depth : ROW_T + (c + 1) * depth]
            flux = speed * ((outside + rows_ref[s, planes]) * 0.5)
            deep = rows_of(flux.shape).astype(F32) < face
            shift[s, planes] = jnp.where(deep, gain * flux, 0.0)
            chains.append((s, c, level_in, diff_ref[at : at + 1]))
    right = [None] * 4
    for l in range(depth):
        for i, (s, c, level_in, diff_in) in enumerate(chains):
            at = c * depth + l
            inv = inv_rows_ref[s, l : l + 1]
            value = shift[s, at : at + 1]
            if l > 0:
                value = value + jnp.where(level_in > l, diff_in, 0.0) * right[i]
            right[i] = value * inv
            shift[s, at : at + 1] = right[i]
    for l in range(depth - 2, -1, -1):
        for i, (s, c, level_in, diff_in) in enumerate(chains):
            at = c * depth + l
            inv = inv_rows_ref[s, l : l + 1]
            below = jnp.where(level_in > l + 1, diff_in, 0.0) * inv
            right[i] = shift[s, at : at + 1] + below * right[i]
            shift[s, at : at + 1] = right[i]
    row = rows_of((HALO, cols))
    for s, cut, at_row in ((0, hi, HALO - 1), (1, lo, 0)):
        for c in range(2):
            for l in range(depth):
                at = c * depth + l
                add = jnp.broadcast_to(shift[s, at : at + 1], (HALO, cols))
                x = x_ref[c, l, cut] + unit_ref[l, cut] * source[c][cut]
                fixed[c, l, cut] = x + jnp.where(row == at_row, add, 0.0)
        send(fixed.at[:, :, cut], t_out.at[:, :, cut])

    own = (
        height_ref[...], transport_ref[0], transport_ref[1], level_f,
        flux_ref[1], flux_ref[2], flux_ref[3],
    )
    ext = []
    lane = lanes((HALO, cols))
    side = (lane < HALO) | (lane >= cols - HALO)
    for i in range(FIELDS):
        at = slice(i * HALO, (i + 1) * HALO)
        whole = jnp.concatenate([south[at], own[i], north[at]], axis=0)
        start = jnp.where(top, cols - 2 * HALO * (FIELDS - i) - HALO, cols - 2 * HALO * i - HALO)
        north_rim = jnp.where(side, pltpu.roll(north[ROW_RIM:ROW_T], start, 1), 0.0)
        south_rim = jnp.where(side, turn(south[ROW_RIM:ROW_T], -(2 * HALO * i + HALO), 1), 0.0)
        rim = jnp.concatenate([south_rim, rim_ref[i], north_rim], axis=0)
        ext.append(jnp.concatenate([whole, rim], axis=1))


    def coefficients(f):
        wet = (f[LEVELS] > 0.0).astype(F32)
        return (
            wet,
            wave_grad * (f[LEVELS] / depth),
            fresh_gain * f[FRESH] * wet,
            wind_gain * f[WIND_E] * wet,
            wind_gain * f[WIND_N] * wet,
        )

    mine = [x for x in ext]
    fold = [x[HALO + rows :] for x in ext]
    wet, grad, fresh, wind_e, wind_n = coefficients(mine)
    p_wet, p_grad, p_fresh, p_wind_e, p_wind_n = coefficients(fold)
    h, e, n = mine[HEIGHT], mine[EAST], mine[NORTH]
    p_h, p_e, p_n = fold[HEIGHT], fold[EAST], fold[NORTH]
    row = rows_of(h.shape)
    last = HALO + rows - 1
    across = (row == last) & top
    p_last = rows_of(p_h.shape) == HALO - 1
    for _ in range(SUBSTEPS):
        h = (h - wave_div * ((e - turn(e, 1, 1)) + (n - turn(n, 1, 0)))) * wet + fresh
        p_h = (p_h - wave_div * ((p_e - turn(p_e, -1, 1)) + (p_n - turn(p_n, 1, 0)))) * p_wet + p_fresh
        h_n = jnp.where(across, jnp.broadcast_to(p_h[HALO - 1 :], h.shape), turn(h, -1, 0))
        p_h_n = jnp.where(p_last, jnp.broadcast_to(h[last : last + 1], p_h.shape), turn(p_h, -1, 0))
        e = (e - grad * (turn(h, -1, 1) - h)) * wet + wind_e
        n = (n - grad * (h_n - h)) * wet + wind_n
        p_e = (p_e - p_grad * (turn(p_h, 1, 1) - p_h)) * p_wet + p_wind_e
        p_n = (p_n - p_grad * (p_h_n - p_h)) * p_wet + p_wind_n
    inside = slice(HALO, HALO + rows)
    result[0] = h[inside, :cols]
    result[1] = e[inside, :cols]
    result[2] = n[inside, :cols]
    send(result.at[0], height_out)
    send(result.at[1:3], transport_out)

    for copy in copies:
        copy.wait()


def vmem(count):
    return [pl.BlockSpec(memory_space=pltpu.VMEM)] * count


def params(mib=24):
    return pltpu.CompilerParams(vmem_limit_bytes=mib * 1024 * 1024)


def work(mb):
    return pl.CostEstimate(flops=mb * 1000000, bytes_accessed=mb * 1000000, transcendentals=0)


def in_hbm(x):
    return pltpu.with_memory_space_constraint(x, pltpu.HBM)


def shape_of(*shape):
    return jax.ShapeDtypeStruct(shape, F32)


def lat_pairs(n_lat, n_lon):
    def at(i, j):
        return i * n_lon + j

    first, second = [], []
    for j in range(n_lon):
        for i in range(0, n_lat, 2):
            first += [(at(i, j), at(i + 1, j)), (at(i + 1, j), at(i, j))]
        for i in range(1, n_lat - 1, 2):
            second += [(at(i, j), at(i + 1, j)), (at(i + 1, j), at(i, j))]
        second.append((at(n_lat - 1, j), at(n_lat - 1, n_lon - 1 - j)))
    return first, second


def lon_pairs(n_lon):
    first, second = [], []
    for j in range(0, n_lon, 2):
        first += [(j, j + 1), (j + 1, j)]
        k, m = j + 1, (j + 2) % n_lon
        second += [(k, m), (m, k)]
    return first, second


def per_device(
    tracers,
    velocity,
    diffusivity,
    ocean_levels,
    surface_height,
    transport,
    atm_flux,
    send_rows,
    src_owner,
    src_slot,
    xgrid_weights,
    xgrid_count,
):
    n_lat, n_lon = lax.axis_size("lat"), lax.axis_size("lon")
    depth, rows, cols = tracers.shape[1:]
    slots = send_rows.shape[3]
    picked = pl.pallas_call(
        pick_kernel,
        out_shape=shape_of(n_lon, 1, 10 * slots),
        in_specs=[pl.BlockSpec(memory_space=pltpu.HBM)] * 2,
        out_specs=vmem(1)[0],
        scratch_shapes=[
            pltpu.VMEM(atm_flux.shape, F32),
            pltpu.VMEM(send_rows.shape, jnp.int32),
            pltpu.SemaphoreType.DMA((2,)),
        ],
        compiler_params=params(24),
        cost_estimate=work(40),
        name="pick",
    )(in_hbm(atm_flux), in_hbm(send_rows))
    table = lax.all_to_all(picked, "lon", split_axis=0, concat_axis=0, tiled=True)

    block = (rows, cols)
    lat_rows = ROW_T + 3 * depth
    two, one, t_0, edge_rows, pick_row, pick_lane, used, tracers, velocity = pl.pallas_call(
        edge_kernel,
        out_shape=(
            shape_of(2 * rows, cols),
            shape_of(2 * rows, cols),
            shape_of(*block),
            shape_of(2, 3 * depth, cols),
            jax.ShapeDtypeStruct((4, *block), jnp.int32),
            jax.ShapeDtypeStruct((4, *block), jnp.int32),
            shape_of(4, *block),
            shape_of(2, depth, *block),
            shape_of(2, depth, *block),
        ),
        in_specs=[pl.BlockSpec(memory_space=pl.ANY)] + [pl.BlockSpec(memory_space=pltpu.HBM)] * 2 + vmem(7),
        out_specs=vmem(9),
        scratch_shapes=[pltpu.SemaphoreType.DMA((4,))],
        compiler_params=params(),
        cost_estimate=work(2),
        name="edges",
    )(
        picked, in_hbm(tracers), in_hbm(velocity), ocean_levels, surface_height, transport, src_owner, src_slot,
        xgrid_weights, xgrid_count,
    )
    pairs = lon_pairs(n_lon)
    two = lax.ppermute(two, "lon", pairs[1])
    one = lax.ppermute(one, "lon", pairs[0])

    solved, unit, inv_rows = pl.pallas_call(
        tracer_kernel,
        out_shape=(shape_of(2, depth, *block), shape_of(depth, *block), shape_of(2, depth, cols)),
        in_specs=vmem(7),
        out_specs=vmem(3),
        scratch_shapes=[
            pltpu.VMEM((depth, *block), F32),
            pltpu.VMEM((2 * depth * rows, 2 * cols), jnp.bfloat16),
            pltpu.VMEM((2 * depth * rows, cols), F32),
            pltpu.VMEM((2 * depth * rows, cols), F32),
        ],
        compiler_params=params(),
        cost_estimate=work(8),
        name="tracers",
    )(two, one, t_0, ocean_levels, diffusivity, tracers, velocity)

    second, first, edge_flux, edge_rim, tab, side = pl.pallas_call(
        rim_lookup_kernel,
        out_shape=(
            shape_of(lat_rows, cols),
            shape_of(lat_rows, cols),
            shape_of(2, 3, HALO, cols),
            shape_of(2, 3, HALO, cols),
            shape_of(4, n_lon // 2, 128),
            shape_of(3, n_lon, 128),
        ),
        in_specs=vmem(10) + [pl.BlockSpec(memory_space=pl.ANY)],
        out_specs=vmem(6),
        scratch_shapes=[pltpu.VMEM((2, lat_rows, cols), F32)],
        compiler_params=params(),
        cost_estimate=work(8),
        name="rim_lookup",
    )(
        table, two, one, pick_row, pick_lane, used, edge_rows, ocean_levels, surface_height, transport,
        inv_rows,
    )
    pairs = lat_pairs(n_lat, n_lon)
    second = lax.ppermute(second, ("lat", "lon"), pairs[1])
    first = lax.ppermute(first, ("lat", "lon"), pairs[0])

    flux, rim = pl.pallas_call(
        lookup_kernel,
        out_shape=(shape_of(4, *block), shape_of(FIELDS, *block)),
        in_specs=vmem(9),
        out_specs=vmem(2),
        compiler_params=params(),
        cost_estimate=work(8),
        name="lookup",
    )(edge_flux, edge_rim, tab, side, two, one, pick_row, pick_lane, used)

    return pl.pallas_call(
        step_kernel,
        out_shape=(shape_of(2, depth, rows, cols), shape_of(rows, cols), shape_of(2, rows, cols)),
        in_specs=vmem(12),
        out_specs=(pl.BlockSpec(memory_space=pl.ANY),) * 3,
        scratch_shapes=[
            pltpu.VMEM((lat_rows, cols), F32),
            pltpu.VMEM((2, 2 * depth, cols), F32),
            pltpu.VMEM((2, depth, rows, cols), F32),
            pltpu.VMEM((3, rows, cols), F32),
            pltpu.SemaphoreType.DMA((6,)),
        ],
        compiler_params=params(),
        name="step",
    )(
        second, first, surface_height, transport, ocean_levels, diffusivity, flux, rim, edge_rows, inv_rows,
        solved, unit,
    )


def solution(mesh):
    return jax.shard_map(
        per_device,
        mesh=mesh,
        in_specs=(
            P(None, None, "lat", "lon"),
            P(None, None, "lat", "lon"),
            P("lat", "lon"),
            P("lat", "lon"),
            P("lat", "lon"),
            P(None, "lat", "lon"),
            P("lat", None, "lon"),
            P("lat", "lon", None, None),
            P(None, "lat", "lon"),
            P(None, "lat", "lon"),
            P(None, "lat", "lon"),
            P("lat", "lon"),
        ),
        out_specs=(P(None, None, "lat", "lon"), P("lat", "lon"), P(None, "lat", "lon")),
        check_vma=False,
    )
```

```python
import jax
import jax.numpy as jnp
from jax import lax
from jax.experimental import pallas as pl
from jax.experimental.pallas import tpu as pltpu
from jax.sharding import PartitionSpec as P

SUBSTEPS = 6
HALO = 8
FIELDS = 7
HEIGHT, EAST, NORTH, LEVELS, FRESH, WIND_E, WIND_N = range(FIELDS)
ROW_RIM = FIELDS * HALO
ROW_T = ROW_RIM + HALO
LISTS = 256
OWNER, SLOT, USED = 32, 64, 96

adv_rate = 0.1
heat_gain = 0.5
salt_gain = 0.5
wave_div = 0.5
wave_grad = 0.8
fresh_gain = 0.2
wind_gain = 0.2

F32 = jnp.float32


def lanes(shape):
    return lax.broadcasted_iota(jnp.int32, shape, len(shape) - 1)


def rows_of(shape):
    return lax.broadcasted_iota(jnp.int32, shape, len(shape) - 2)


def turn(x, by, axis):
    size = x.shape[axis]
    by = by % size
    return x if by == 0 else pltpu.roll(x, by, axis)


def is_even(axis):
    return lax.rem(lax.axis_index(axis), 2) == 0


def is_top():
    return lax.axis_index("lat") == lax.axis_size("lat") - 1


def pick_kernel(atm_hbm, rows_hbm, out_ref, atm_ref, rows_ref, sems):
    copies = [
        pltpu.make_async_copy(atm_hbm, atm_ref, sems.at[0]),
        pltpu.make_async_copy(rows_hbm, rows_ref, sems.at[1]),
    ]
    for copy in copies:
        copy.start()
    for copy in copies:
        copy.wait()
    rows = rows_ref[0, 0]
    both = jnp.concatenate([rows, rows], axis=1)
    lane = both & 127
    part = both >> 7
    low = lanes(both.shape) < 64
    values = []
    for f in range(4):
        acc = None
        for k in range(atm_ref.shape[2] // 128):
            row = jnp.broadcast_to(atm_ref[0, f : f + 1, k * 128 : (k + 1) * 128], both.shape)
            value = jnp.take_along_axis(row, lane, axis=1)
            acc = value if k == 0 else jnp.where(part == k, value, acc)
        values.append(acc)
    out_ref[:, 0, 0:128] = jnp.where(low, values[0], values[1])
    out_ref[:, 0, 128:256] = jnp.where(low, values[2], values[3])
    for f in range(1, 4):
        at = 128 + f * 128
        out_ref[:, 0, at : at + 128] = jnp.where(low, turn(values[f], -1, 0), turn(values[f], 1, 0))


def edge_kernel(
    picked_ref, t_hbm, v_hbm, level_ref, height_ref, transport_ref, owner_ref, slot_ref, weight_ref, count_ref,
    two_ref, one_ref, t_0_ref, rows_ref, pick_row_ref, pick_lane_ref, used_ref, t_ref, u_ref, v_rows, sems,
):
    depth, rows, cols = t_ref.shape[1:]
    copies = [
        pltpu.make_async_copy(t_hbm.at[0], t_ref.at[0], sems.at[0]),
        pltpu.make_async_copy(v_hbm.at[0], u_ref, sems.at[1]),
        pltpu.make_async_copy(t_hbm.at[1], t_ref.at[1], sems.at[2]),
        pltpu.make_async_copy(v_hbm.at[1, :, rows - HALO : rows], v_rows, sems.at[3]),
    ]
    for copy in copies:
        copy.start()
    shape = (rows, cols)
    lane = lanes(shape)
    level = level_ref[...]
    half = lax.axis_size("lon") // 2
    count = count_ref[...]
    for k in range(owner_ref.shape[0]):
        owner = owner_ref[k]
        high = owner >= half
        pick_row_ref[k] = jnp.where(high, owner - half, owner)
        pick_lane_ref[k] = jnp.where(high, slot_ref[k] + 64, slot_ref[k])
        used_ref[k] = jnp.where(count > k, weight_ref[k], 0.0)
    fields = [height_ref[...], transport_ref[0], transport_ref[1], level.astype(F32)]
    fields += [owner_ref[k].astype(F32) for k in range(4)]
    fields += [slot_ref[k].astype(F32) for k in range(4)]
    fields += [used_ref[k] for k in range(4)]
    west = jnp.zeros(shape, F32)
    east = jnp.zeros(shape, F32)
    for g, field in enumerate(fields):
        here = (lane >= g * HALO) & (lane < (g + 1) * HALO)
        west = jnp.where(here, turn(field, g * HALO, 1), west)
        east = jnp.where(here, turn(field, (g + 1) * HALO, 1), east)
    west_t = jnp.zeros(shape, F32)
    east_t = jnp.zeros(shape, F32)
    for c in range(2):
        copies[2 * c].wait()
        for l in range(depth):
            f = c * depth + l
            moved = turn(t_ref[c, l], f + 1, 1)
            west_t = jnp.where(lane == f + 1, moved, west_t)
            east_t = jnp.where(lane == f, moved, east_t)
    copies[1].wait()
    for l in range(depth):
        at = 2 * depth + l
        east_t = jnp.where(lane == at, turn(u_ref[l], at + 1, 1), east_t)
    even = is_even("lon")
    one_ref[:rows] = jnp.where(even, east, west)
    two_ref[:rows] = jnp.where(even, west, east)
    one_ref[rows:] = jnp.where(even, east_t, west_t)
    two_ref[rows:] = jnp.where(even, west_t, east_t)
    t_0_ref[...] = turn(west_t, -1, 1)
    for c in range(2):
        for l in range(depth):
            at = c * depth + l
            rows_ref[0, at : at + 1] = t_ref[c, l, rows - 1 : rows]
            rows_ref[1, at : at + 1] = t_ref[c, l, 0:1]
    copies[3].wait()
    for l in range(depth):
        at = 2 * depth + l
        rows_ref[0, at : at + 1] = v_rows[l, HALO - 1 : HALO]
    rows_ref[1, 2 * depth :] = jnp.zeros((depth, cols), F32)

def own_lookup(tab, row_ref, lane_ref, used_ref, cut, fields):
    total = {f: None for f in fields}
    for k in range(used_ref.shape[0]):
        lane = lane_ref[k, cut]
        row = row_ref[k, cut]
        acc = {}
        for r in range(tab.shape[1]):
            here = row == r
            for f in fields:
                source = jnp.broadcast_to(tab[f, r : r + 1, :], lane.shape)
                value = jnp.take_along_axis(source, lane, axis=1)
                acc[f] = value if r == 0 else jnp.where(here, value, acc[f])
        used = used_ref[k, cut]
        for f in fields:
            total[f] = acc[f] * used if k == 0 else total[f] + acc[f] * used
    return total


def rim_of(east, west, by_east, by_west):
    lane = lanes(east.shape)
    outer = jnp.where(lane >= 128 - HALO, turn(west, by_west, 1), 0.0)
    return jnp.where(lane < HALO, turn(east, by_east, 1), outer)


def from_lon(one_ref, two_ref, cut):
    even = is_even("lon")
    one, two = one_ref[cut], two_ref[cut]
    return jnp.where(even, one, two), jnp.where(even, two, one)


def state_rims(east, west):
    return [rim_of(east, west, -g * HALO, 128 - (g + 1) * HALO) for g in range(4)]


def side_lookup(side, sides):
    (east, west), (east_2, west_2) = sides
    lane = lanes(east.shape)
    quarter = lane >> 5

    def gathered(by):
        parts = (turn(west_2, -32 - by, 1), turn(east, -by, 1), turn(west, 32 - by, 1), turn(east_2, 64 - by, 1))
        low = jnp.where(quarter == 0, parts[0], parts[1])
        return jnp.where(quarter < 2, low, jnp.where(quarter == 2, parts[2], parts[3]))

    owner = gathered(0).astype(jnp.int32)
    slot = gathered(32).astype(jnp.int32)
    used = gathered(64)
    slot = jnp.where((quarter & 1) == 0, slot + 64, slot)
    acc = [None] * 3
    for r in range(side.shape[1]):
        here = owner == r
        for f in range(3):
            source = jnp.broadcast_to(side[f, r : r + 1, :], slot.shape)
            value = jnp.take_along_axis(source, slot, axis=1)
            acc[f] = value if r == 0 else jnp.where(here, value, acc[f])
    rims = ([], [])
    for f in range(3):
        v = acc[f] * used
        v = v + turn(v, -16, 1)
        v = v + turn(v, -8, 1)
        rims[0].append(rim_of(v, v, -32, 56))
        rims[1].append(rim_of(v, v, -96, 120))
    return rims


def rim_lookup_kernel(
    table_ref, two_ref, one_ref, pick_row_ref, pick_lane_ref, used_ref, rows_ref, level_ref, height_ref,
    transport_ref, first_ref, second_ref, flux_ref, rim_ref, tab, side, pack,
):
    n_lon = table_ref.shape[0]
    half = n_lon // 2
    rows, cols = height_ref.shape
    low = lanes((half, 128)) < 64
    for pair in range(2):
        part = table_ref[:, 0, pair * 128 : (pair + 1) * 128]
        lo, hi = part[:half], part[half:]
        tab[2 * pair] = jnp.where(low, lo, turn(hi, 64, 1))
        tab[2 * pair + 1] = jnp.where(low, turn(lo, 64, 1), hi)
    for f in range(3):
        side[f] = table_ref[:, 0, LISTS + f * 128 : LISTS + (f + 1) * 128]
    lane = lanes((HALO, cols))
    cuts = (slice(rows - HALO, rows), slice(0, HALO))
    sides = [from_lon(one_ref, two_ref, cut) for cut in cuts]
    side_rims = side_lookup(side, sides)
    for s, cut in enumerate(cuts):
        found = own_lookup(tab, pick_row_ref, pick_lane_ref, used_ref, cut, (1, 2, 3))
        for f in range(3):
            flux_ref[s, f] = found[f + 1]
            rim_ref[s, f] = side_rims[s][f]
        rims = state_rims(*sides[s]) + side_rims[s]
        own = [
            height_ref[cut], transport_ref[0, cut], transport_ref[1, cut], level_ref[cut].astype(F32),
            found[1], found[2], found[3],
        ]
        packed = jnp.zeros((HALO, cols), F32)
        for i in range(FIELDS):
            pack[s, i * HALO : (i + 1) * HALO] = own[i]
            start = 2 * HALO * i
            here = (lane >= start) & (lane < start + 2 * HALO)
            packed = jnp.where(here, turn(rims[i], start + HALO, 1), packed)
        pack[s, ROW_RIM:ROW_T] = packed
        pack[s, ROW_T:] = rows_ref[s]
    even = is_even("lat")
    north_going, south_going = pack[0], pack[1]
    first_ref[...] = jnp.where(even, north_going, south_going)
    second_ref[...] = jnp.where(even, south_going, north_going)


def lookup_kernel(
    edge_flux_ref, edge_rim_ref, tab, side, two_ref, one_ref, pick_row_ref, pick_lane_ref, used_ref,
    flux_ref, rim_ref,
):
    rows = used_ref.shape[1]
    cuts = [slice(at, at + HALO) for at in range(0, rows, HALO)]
    sides = [from_lon(one_ref, two_ref, cut) for cut in cuts]
    for at in range(1, len(cuts) - 1, 2):
        side_rims = side_lookup(side, sides[at : at + 2])
        for i in range(2):
            cut = cuts[at + i]
            found = own_lookup(tab, pick_row_ref, pick_lane_ref, used_ref, cut, (0, 1, 2, 3))
            for f in range(4):
                flux_ref[f, cut] = found[f]
            for g, rim in enumerate(state_rims(*sides[at + i]) + side_rims[i]):
                rim_ref[g, cut] = rim
    for s, at in ((0, len(cuts) - 1), (1, 0)):
        cut = cuts[at]
        flux_ref[0, cut] = own_lookup(tab, pick_row_ref, pick_lane_ref, used_ref, cut, (0,))[0]
        for f in range(3):
            flux_ref[f + 1, cut] = edge_flux_ref[s, f]
        for g, rim in enumerate(state_rims(*sides[at]) + [edge_rim_ref[s, f] for f in range(3)]):
            rim_ref[g, cut] = rim


def split(x):
    hi = x.astype(jnp.bfloat16)
    return hi, (x - hi.astype(F32)).astype(jnp.bfloat16)


def tracer_kernel(
    two_ref, one_ref, t_0_ref, level_ref, diff_ref, t_ref, u_ref, v_hbm, x_ref, unit_ref, inv_rows_ref, gain_ref,
    parts, rims, net_x, v_ref, sem,
):
    depth, rows, cols = t_ref.shape[1:]
    copy = pltpu.make_async_copy(v_hbm.at[1], v_ref, sem)
    copy.start()
    shape = (rows, cols)
    east, west = from_lon(one_ref, two_ref, slice(0, rows))
    t_e, t_w = from_lon(one_ref, two_ref, slice(rows, 2 * rows))
    level = level_ref[...]
    level_f = level.astype(F32)
    lane = lanes(shape)
    row = rows_of(shape)
    first = LEVELS * HALO
    last = cols - 1
    level_e = jnp.where(lane == last, turn(east, last - first, 1), turn(level_f, -1, 1))
    level_n = turn(level_f, -1, 0)
    face_e = jnp.minimum(level_f, level_e)
    face_n = jnp.where(row == rows - 1, 0.0, jnp.minimum(level_f, level_n))
    t_0 = t_0_ref[...]
    u_w = jnp.where(lane < depth, turn(t_w, -2 * depth, 1), turn(t_w, -depth, 1))
    layer = jnp.where(lane < depth, lane, lane - depth).astype(F32)
    level_w = west[:, first + HALO - 1 : first + HALO]
    face_w = jnp.broadcast_to(jnp.minimum(level_f[:, 0:1], level_w), shape)
    west_flux = jnp.where((layer < face_w) & (lane < 2 * depth), u_w * ((t_w + t_0) * 0.5), 0.0)
    both = []
    for x in (turn(t_e, -1, 1), west_flux):
        hi, lo = split(x)
        both.append(jnp.where(lane < 64, hi.astype(F32), turn(lo.astype(F32), 64, 1)))
    plane = lane & 63
    for f in range(2 * depth):
        at = slice(f * rows, (f + 1) * rows)
        here = plane == f
        parts[at, 0:128] = jnp.where(here, both[0], 0.0).astype(jnp.bfloat16)
        parts[at, 128:256] = jnp.where(here, both[1], 0.0).astype(jnp.bfloat16)
    k = lax.broadcasted_iota(jnp.int32, (2 * cols, cols), 0)
    into = jnp.where(k < cols, last, 0) == lanes((2 * cols, cols))
    rims[...] = jnp.dot(parts[...], into.astype(F32).astype(jnp.bfloat16), preferred_element_type=F32)
    for l in range(depth):
        mask_e = face_e > l
        u_l = u_ref[l] * 0.5
        for c in range(2):
            f = c * depth + l
            at = slice(f * rows, (f + 1) * rows)
            t = t_ref[c, l]
            t_east = jnp.where(lane == last, rims[at], turn(t, -1, 1))
            flux_e = jnp.where(mask_e, u_l * (t + t_east), 0.0)
            net_x[at] = flux_e - jnp.where(lane == 0, rims[at], turn(flux_e, 1, 1))
    copy.wait()
    diff = diff_ref[...]
    above = jnp.zeros(shape, F32)
    inv = None
    right = [None, None, None]
    for l in range(depth):
        below = jnp.where(level > l + 1, diff, 0.0) if l < depth - 1 else jnp.zeros(shape, F32)
        pivot = 1.0 + above + below
        if l > 0:
            pivot = pivot - above * above * inv
        inv = 1.0 / pivot
        inv_rows_ref[0, l : l + 1] = inv[rows - 1 : rows]
        inv_rows_ref[1, l : l + 1] = inv[0:1]
        gain_ref[l] = below * inv
        mask_n = face_n > l
        v_l = v_ref[l] * 0.5
        for c in range(2):
            f = c * depth + l
            at = slice(f * rows, (f + 1) * rows)
            t = t_ref[c, l]
            flux_n = jnp.where(mask_n, v_l * (t + turn(t, -1, 0)), 0.0)
            flux_s = turn(flux_n, 1, 0)
            forced = t - adv_rate * (net_x[at] + (flux_n - flux_s))
            right[c] = forced * inv if l == 0 else (forced + above * right[c]) * inv
            x_ref[c, l] = right[c]
        right[2] = inv if l == 0 else above * right[2] * inv
        unit_ref[l] = right[2]
        above = below
    for l in range(depth - 2, -1, -1):
        gain = gain_ref[l]
        for c in range(2):
            right[c] = x_ref[c, l] + gain * right[c]
            x_ref[c, l] = right[c]
        right[2] = unit_ref[l] + gain * right[2]
        unit_ref[l] = right[2]


def step_kernel(
    first_ref, second_ref, height_ref, transport_ref, level_ref, diff_ref, flux_ref, rim_ref, rows_ref, inv_rows_ref,
    x_ref, unit_ref, t_out, height_out, transport_out, north_ref, shift, fixed, result, sems,
):
    top = is_top()
    level = level_ref[...]
    level_f = level.astype(F32)
    rows, cols = level.shape
    depth = x_ref.shape[1]
    wet_0 = (level > 0).astype(F32)
    source = (heat_gain * flux_ref[0] * wet_0, -salt_gain * flux_ref[1] * wet_0)
    lo, hi = slice(0, HALO), slice(rows - HALO, rows)
    mid = slice(HALO, rows - HALO)
    copies = []

    def send(value, out):
        copies.append(pltpu.make_async_copy(value, out, sems.at[len(copies)]))
        copies[-1].start()

    for c in range(2):
        for l in range(depth):
            fixed[c, l, mid] = x_ref[c, l, mid] + unit_ref[l, mid] * source[c][mid]
        send(fixed.at[c, :, mid], t_out.at[c, :, mid])
    even = is_even("lat")
    a, b = first_ref[...], second_ref[...]
    south = jnp.where(even, b, a)
    north = jnp.where(even, a, b)
    mirrored = jnp.take_along_axis(north, 127 - lanes(north.shape), axis=1)
    north = jnp.where(top, mirrored, north)
    north_ref[...] = north

    first = LEVELS * HALO
    level_n = jnp.where(top, north[first + HALO - 1 : first + HALO], north[first : first + 1])
    level_s = south[first + HALO - 1 : first + HALO]
    sides = ((north, level_n, rows - 1, -adv_rate), (south, level_s, 0, adv_rate))
    chains = []
    for s, (message, level_out, at, gain) in enumerate(sides):
        level_in = level_f[at : at + 1]
        face = jnp.minimum(level_in, level_out)
        speed = rows_ref[0, 2 * depth :] if s == 0 else message[ROW_T + 2 * depth :]
        for c in range(2):
            planes = slice(c * depth, (c + 1) * depth)
            outside = message[ROW_T + c * depth : ROW_T + (c + 1) * depth]
            flux = speed * ((outside + rows_ref[s, planes]) * 0.5)
            deep = rows_of(flux.shape).astype(F32) < face
            shift[s, planes] = jnp.where(deep, gain * flux, 0.0)
            chains.append((s, c, level_in, diff_ref[at : at + 1]))
    right = [None] * 4
    for l in range(depth):
        for i, (s, c, level_in, diff_in) in enumerate(chains):
            at = c * depth + l
            inv = inv_rows_ref[s, l : l + 1]
            value = shift[s, at : at + 1]
            if l > 0:
                value = value + jnp.where(level_in > l, diff_in, 0.0) * right[i]
            right[i] = value * inv
            shift[s, at : at + 1] = right[i]
    for l in range(depth - 2, -1, -1):
        for i, (s, c, level_in, diff_in) in enumerate(chains):
            at = c * depth + l
            inv = inv_rows_ref[s, l : l + 1]
            below = jnp.where(level_in > l + 1, diff_in, 0.0) * inv
            right[i] = shift[s, at : at + 1] + below * right[i]
            shift[s, at : at + 1] = right[i]
    row = rows_of((HALO, cols))
    for s, cut, at_row in ((0, hi, HALO - 1), (1, lo, 0)):
        for c in range(2):
            for l in range(depth):
                at = c * depth + l
                add = jnp.broadcast_to(shift[s, at : at + 1], (HALO, cols))
                x = x_ref[c, l, cut] + unit_ref[l, cut] * source[c][cut]
                fixed[c, l, cut] = x + jnp.where(row == at_row, add, 0.0)
        send(fixed.at[:, :, cut], t_out.at[:, :, cut])

    own = (
        height_ref[...], transport_ref[0], transport_ref[1], level_f,
        flux_ref[1], flux_ref[2], flux_ref[3],
    )
    ext = []
    lane = lanes((HALO, cols))
    side = (lane < HALO) | (lane >= cols - HALO)
    for i in range(FIELDS):
        at = slice(i * HALO, (i + 1) * HALO)
        whole = jnp.concatenate([south[at], own[i], north[at]], axis=0)
        start = jnp.where(top, cols - 2 * HALO * (FIELDS - i) - HALO, cols - 2 * HALO * i - HALO)
        north_rim = jnp.where(side, pltpu.roll(north[ROW_RIM:ROW_T], start, 1), 0.0)
        south_rim = jnp.where(side, turn(south[ROW_RIM:ROW_T], -(2 * HALO * i + HALO), 1), 0.0)
        rim = jnp.concatenate([south_rim, rim_ref[i], north_rim], axis=0)
        ext.append(jnp.concatenate([whole, rim], axis=1))


    def coefficients(f):
        wet = (f[LEVELS] > 0.0).astype(F32)
        return (
            wet,
            wave_grad * (f[LEVELS] / depth),
            fresh_gain * f[FRESH] * wet,
            wind_gain * f[WIND_E] * wet,
            wind_gain * f[WIND_N] * wet,
        )

    mine = [x for x in ext]
    fold = [x[HALO + rows :] for x in ext]
    wet, grad, fresh, wind_e, wind_n = coefficients(mine)
    p_wet, p_grad, p_fresh, p_wind_e, p_wind_n = coefficients(fold)
    h, e, n = mine[HEIGHT], mine[EAST], mine[NORTH]
    p_h, p_e, p_n = fold[HEIGHT], fold[EAST], fold[NORTH]
    row = rows_of(h.shape)
    last = HALO + rows - 1
    across = (row == last) & top
    p_last = rows_of(p_h.shape) == HALO - 1
    for _ in range(SUBSTEPS):
        h = (h - wave_div * ((e - turn(e, 1, 1)) + (n - turn(n, 1, 0)))) * wet + fresh
        p_h = (p_h - wave_div * ((p_e - turn(p_e, -1, 1)) + (p_n - turn(p_n, 1, 0)))) * p_wet + p_fresh
        h_n = jnp.where(across, jnp.broadcast_to(p_h[HALO - 1 :], h.shape), turn(h, -1, 0))
        p_h_n = jnp.where(p_last, jnp.broadcast_to(h[last : last + 1], p_h.shape), turn(p_h, -1, 0))
        e = (e - grad * (turn(h, -1, 1) - h)) * wet + wind_e
        n = (n - grad * (h_n - h)) * wet + wind_n
        p_e = (p_e - p_grad * (turn(p_h, 1, 1) - p_h)) * p_wet + p_wind_e
        p_n = (p_n - p_grad * (p_h_n - p_h)) * p_wet + p_wind_n
    inside = slice(HALO, HALO + rows)
    result[0] = h[inside, :cols]
    result[1] = e[inside, :cols]
    result[2] = n[inside, :cols]
    send(result.at[0], height_out)
    send(result.at[1:3], transport_out)

    for copy in copies:
        copy.wait()


def vmem(count):
    return [pl.BlockSpec(memory_space=pltpu.VMEM)] * count


def params(mib=24):
    return pltpu.CompilerParams(vmem_limit_bytes=mib * 1024 * 1024)


def work(mb):
    return pl.CostEstimate(flops=mb * 1000000, bytes_accessed=mb * 1000000, transcendentals=0)


def in_hbm(x):
    return pltpu.with_memory_space_constraint(x, pltpu.HBM)


def shape_of(*shape):
    return jax.ShapeDtypeStruct(shape, F32)


def lat_pairs(n_lat, n_lon):
    def at(i, j):
        return i * n_lon + j

    first, second = [], []
    for j in range(n_lon):
        for i in range(0, n_lat, 2):
            first += [(at(i, j), at(i + 1, j)), (at(i + 1, j), at(i, j))]
        for i in range(1, n_lat - 1, 2):
            second += [(at(i, j), at(i + 1, j)), (at(i + 1, j), at(i, j))]
        second.append((at(n_lat - 1, j), at(n_lat - 1, n_lon - 1 - j)))
    return first, second


def lon_pairs(n_lon):
    first, second = [], []
    for j in range(0, n_lon, 2):
        first += [(j, j + 1), (j + 1, j)]
        k, m = j + 1, (j + 2) % n_lon
        second += [(k, m), (m, k)]
    return first, second


def per_device(
    tracers,
    velocity,
    diffusivity,
    ocean_levels,
    surface_height,
    transport,
    atm_flux,
    send_rows,
    src_owner,
    src_slot,
    xgrid_weights,
    xgrid_count,
):
    n_lat, n_lon = lax.axis_size("lat"), lax.axis_size("lon")
    depth, rows, cols = tracers.shape[1:]
    slots = send_rows.shape[3]
    picked = pl.pallas_call(
        pick_kernel,
        out_shape=pltpu.VMEM((n_lon, 1, 10 * slots), F32),
        in_specs=[pl.BlockSpec(memory_space=pltpu.HBM)] * 2,
        out_specs=vmem(1)[0],
        scratch_shapes=[
            pltpu.VMEM(atm_flux.shape, F32),
            pltpu.VMEM(send_rows.shape, jnp.int32),
            pltpu.SemaphoreType.DMA((2,)),
        ],
        compiler_params=params(24),
        cost_estimate=work(40),
        name="pick",
    )(in_hbm(atm_flux), in_hbm(send_rows))
    table = lax.all_to_all(picked, "lon", split_axis=0, concat_axis=0, tiled=True)

    block = (rows, cols)
    lat_rows = ROW_T + 3 * depth
    two, one, t_0, edge_rows, pick_row, pick_lane, used, tracers, speed_e = pl.pallas_call(
        edge_kernel,
        out_shape=(
            shape_of(2 * rows, cols),
            shape_of(2 * rows, cols),
            shape_of(*block),
            shape_of(2, 3 * depth, cols),
            jax.ShapeDtypeStruct((4, *block), jnp.int32),
            jax.ShapeDtypeStruct((4, *block), jnp.int32),
            shape_of(4, *block),
            shape_of(2, depth, *block),
            shape_of(depth, *block),
        ),
        in_specs=[pl.BlockSpec(memory_space=pl.ANY)] + [pl.BlockSpec(memory_space=pltpu.HBM)] * 2 + vmem(7),
        out_specs=vmem(9),
        scratch_shapes=[pltpu.VMEM((depth, HALO, cols), F32), pltpu.SemaphoreType.DMA((4,))],
        compiler_params=params(),
        cost_estimate=work(2),
        name="edges",
    )(
        picked, in_hbm(tracers), in_hbm(velocity), ocean_levels, surface_height, transport, src_owner, src_slot,
        xgrid_weights, xgrid_count,
    )
    pairs = lon_pairs(n_lon)
    two = lax.ppermute(two, "lon", pairs[1])
    one = lax.ppermute(one, "lon", pairs[0])

    solved, unit, inv_rows = pl.pallas_call(
        tracer_kernel,
        out_shape=(shape_of(2, depth, *block), shape_of(depth, *block), shape_of(2, depth, cols)),
        in_specs=vmem(7) + [pl.BlockSpec(memory_space=pltpu.HBM)],
        out_specs=vmem(3),
        scratch_shapes=[
            pltpu.VMEM((depth, *block), F32),
            pltpu.VMEM((2 * depth * rows, 2 * cols), jnp.bfloat16),
            pltpu.VMEM((2 * depth * rows, cols), F32),
            pltpu.VMEM((2 * depth * rows, cols), F32),
            pltpu.VMEM((depth, *block), F32),
            pltpu.SemaphoreType.DMA,
        ],
        compiler_params=params(),
        cost_estimate=work(8),
        name="tracers",
    )(two, one, t_0, ocean_levels, diffusivity, tracers, speed_e, in_hbm(velocity))

    first, second, edge_flux, edge_rim, tab, side = pl.pallas_call(
        rim_lookup_kernel,
        out_shape=(
            shape_of(lat_rows, cols),
            shape_of(lat_rows, cols),
            shape_of(2, 3, HALO, cols),
            shape_of(2, 3, HALO, cols),
            shape_of(4, n_lon // 2, 128),
            shape_of(3, n_lon, 128),
        ),
        in_specs=vmem(10),
        out_specs=vmem(6),
        scratch_shapes=[pltpu.VMEM((2, lat_rows, cols), F32)],
        compiler_params=params(),
        cost_estimate=work(8),
        name="rim_lookup",
    )(
        table, two, one, pick_row, pick_lane, used, edge_rows, ocean_levels, surface_height, transport,
    )
    pairs = lat_pairs(n_lat, n_lon)
    first = lax.ppermute(first, ("lat", "lon"), pairs[0])
    second = lax.ppermute(second, ("lat", "lon"), pairs[1])

    flux, rim = pl.pallas_call(
        lookup_kernel,
        out_shape=(shape_of(4, *block), shape_of(FIELDS, *block)),
        in_specs=vmem(9),
        out_specs=vmem(2),
        compiler_params=params(),
        cost_estimate=work(8),
        name="lookup",
    )(edge_flux, edge_rim, tab, side, two, one, pick_row, pick_lane, used)

    return pl.pallas_call(
        step_kernel,
        out_shape=(shape_of(2, depth, rows, cols), shape_of(rows, cols), shape_of(2, rows, cols)),
        in_specs=vmem(12),
        out_specs=(pl.BlockSpec(memory_space=pl.ANY),) * 3,
        scratch_shapes=[
            pltpu.VMEM((lat_rows, cols), F32),
            pltpu.VMEM((2, 2 * depth, cols), F32),
            pltpu.VMEM((2, depth, rows, cols), F32),
            pltpu.VMEM((3, rows, cols), F32),
            pltpu.SemaphoreType.DMA((6,)),
        ],
        compiler_params=params(),
        name="step",
    )(
        first, second, surface_height, transport, ocean_levels, diffusivity, flux, rim, edge_rows, inv_rows,
        solved, unit,
    )


def solution(mesh):
    return jax.shard_map(
        per_device,
        mesh=mesh,
        in_specs=(
            P(None, None, "lat", "lon"),
            P(None, None, "lat", "lon"),
            P("lat", "lon"),
            P("lat", "lon"),
            P("lat", "lon"),
            P(None, "lat", "lon"),
            P("lat", None, "lon"),
            P("lat", "lon", None, None),
            P(None, "lat", "lon"),
            P(None, "lat", "lon"),
            P(None, "lat", "lon"),
            P("lat", "lon"),
        ),
        out_specs=(P(None, None, "lat", "lon"), P("lat", "lon"), P(None, "lat", "lon")),
        check_vma=False,
    )
```

```python
import jax
import jax.numpy as jnp
from jax import lax
from jax.experimental import pallas as pl
from jax.experimental.pallas import tpu as pltpu
from jax.sharding import PartitionSpec as P

SUBSTEPS = 6
HALO = 8
FIELDS = 7
HEIGHT, EAST, NORTH, LEVELS, FRESH, WIND_E, WIND_N = range(FIELDS)
ROW_RIM = FIELDS * HALO
ROW_T = ROW_RIM + HALO
LISTS = 256
OWNER, SLOT, USED = 32, 64, 96

adv_rate = 0.1
heat_gain = 0.5
salt_gain = 0.5
wave_div = 0.5
wave_grad = 0.8
fresh_gain = 0.2
wind_gain = 0.2

F32 = jnp.float32


def lanes(shape):
    return lax.broadcasted_iota(jnp.int32, shape, len(shape) - 1)


def rows_of(shape):
    return lax.broadcasted_iota(jnp.int32, shape, len(shape) - 2)


def turn(x, by, axis):
    size = x.shape[axis]
    by = by % size
    return x if by == 0 else pltpu.roll(x, by, axis)


def is_even(axis):
    return lax.rem(lax.axis_index(axis), 2) == 0


def is_top():
    return lax.axis_index("lat") == lax.axis_size("lat") - 1


def pick_kernel(atm_hbm, rows_hbm, out_ref, atm_ref, rows_ref, sems):
    copies = [
        pltpu.make_async_copy(atm_hbm, atm_ref, sems.at[0]),
        pltpu.make_async_copy(rows_hbm, rows_ref, sems.at[1]),
    ]
    for copy in copies:
        copy.start()
    for copy in copies:
        copy.wait()
    rows = rows_ref[0, 0]
    both = jnp.concatenate([rows, rows], axis=1)
    lane = both & 127
    part = both >> 7
    low = lanes(both.shape) < 64
    values = []
    for f in range(4):
        acc = None
        for k in range(atm_ref.shape[2] // 128):
            row = jnp.broadcast_to(atm_ref[0, f : f + 1, k * 128 : (k + 1) * 128], both.shape)
            value = jnp.take_along_axis(row, lane, axis=1)
            acc = value if k == 0 else jnp.where(part == k, value, acc)
        values.append(acc)
    out_ref[:, 0, 0:128] = jnp.where(low, values[0], values[1])
    out_ref[:, 0, 128:256] = jnp.where(low, values[2], values[3])
    for f in range(1, 4):
        at = 128 + f * 128
        out_ref[:, 0, at : at + 128] = jnp.where(low, turn(values[f], -1, 0), turn(values[f], 1, 0))


def edge_kernel(
    picked_ref, t_hbm, v_hbm, level_ref, height_ref, transport_ref, owner_ref, slot_ref, weight_ref, count_ref,
    two_ref, one_ref, t_0_ref, rows_ref, pick_row_ref, pick_lane_ref, used_ref, t_ref, u_ref, v_rows, sems,
):
    depth, rows, cols = t_ref.shape[1:]
    copies = [
        pltpu.make_async_copy(t_hbm.at[0], t_ref.at[0], sems.at[0]),
        pltpu.make_async_copy(v_hbm.at[0], u_ref, sems.at[1]),
        pltpu.make_async_copy(t_hbm.at[1], t_ref.at[1], sems.at[2]),
        pltpu.make_async_copy(v_hbm.at[1, :, rows - HALO : rows], v_rows, sems.at[3]),
    ]
    for copy in copies:
        copy.start()
    shape = (rows, cols)
    lane = lanes(shape)
    level = level_ref[...]
    half = lax.axis_size("lon") // 2
    count = count_ref[...]
    for k in range(owner_ref.shape[0]):
        owner = owner_ref[k]
        high = owner >= half
        pick_row_ref[k] = jnp.where(high, owner - half, owner)
        pick_lane_ref[k] = jnp.where(high, slot_ref[k] + 64, slot_ref[k])
        used_ref[k] = jnp.where(count > k, weight_ref[k], 0.0)
    fields = [height_ref[...], transport_ref[0], transport_ref[1], level.astype(F32)]
    fields += [owner_ref[k].astype(F32) for k in range(4)]
    fields += [slot_ref[k].astype(F32) for k in range(4)]
    fields += [used_ref[k] for k in range(4)]
    west = jnp.zeros(shape, F32)
    east = jnp.zeros(shape, F32)
    for g, field in enumerate(fields):
        here = (lane >= g * HALO) & (lane < (g + 1) * HALO)
        west = jnp.where(here, turn(field, g * HALO, 1), west)
        east = jnp.where(here, turn(field, (g + 1) * HALO, 1), east)
    west_t = jnp.zeros(shape, F32)
    east_t = jnp.zeros(shape, F32)
    for c in range(2):
        copies[2 * c].wait()
        for l in range(depth):
            f = c * depth + l
            moved = turn(t_ref[c, l], f + 1, 1)
            west_t = jnp.where(lane == f + 1, moved, west_t)
            east_t = jnp.where(lane == f, moved, east_t)
    copies[1].wait()
    for l in range(depth):
        at = 2 * depth + l
        east_t = jnp.where(lane == at, turn(u_ref[l], at + 1, 1), east_t)
    even = is_even("lon")
    one_ref[:rows] = jnp.where(even, east, west)
    two_ref[:rows] = jnp.where(even, west, east)
    one_ref[rows:] = jnp.where(even, east_t, west_t)
    two_ref[rows:] = jnp.where(even, west_t, east_t)
    t_0_ref[...] = turn(west_t, -1, 1)
    for c in range(2):
        for l in range(depth):
            at = c * depth + l
            rows_ref[0, at : at + 1] = t_ref[c, l, rows - 1 : rows]
            rows_ref[1, at : at + 1] = t_ref[c, l, 0:1]
    copies[3].wait()
    for l in range(depth):
        at = 2 * depth + l
        rows_ref[0, at : at + 1] = v_rows[l, HALO - 1 : HALO]
    rows_ref[1, 2 * depth :] = jnp.zeros((depth, cols), F32)

def own_lookup(tab, row_ref, lane_ref, used_ref, cut, fields):
    total = {f: None for f in fields}
    for k in range(used_ref.shape[0]):
        lane = lane_ref[k, cut]
        row = row_ref[k, cut]
        acc = {}
        for r in range(tab.shape[1]):
            here = row == r
            for f in fields:
                source = jnp.broadcast_to(tab[f, r : r + 1, :], lane.shape)
                value = jnp.take_along_axis(source, lane, axis=1)
                acc[f] = value if r == 0 else jnp.where(here, value, acc[f])
        used = used_ref[k, cut]
        for f in fields:
            total[f] = acc[f] * used if k == 0 else total[f] + acc[f] * used
    return total


def rim_of(east, west, by_east, by_west):
    lane = lanes(east.shape)
    outer = jnp.where(lane >= 128 - HALO, turn(west, by_west, 1), 0.0)
    return jnp.where(lane < HALO, turn(east, by_east, 1), outer)


def from_lon(one_ref, two_ref, cut):
    even = is_even("lon")
    one, two = one_ref[cut], two_ref[cut]
    return jnp.where(even, one, two), jnp.where(even, two, one)


def state_rims(east, west):
    return [rim_of(east, west, -g * HALO, 128 - (g + 1) * HALO) for g in range(4)]


def side_lookup(side, sides):
    (east, west), (east_2, west_2) = sides
    lane = lanes(east.shape)
    quarter = lane >> 5

    def gathered(by):
        parts = (turn(west_2, -32 - by, 1), turn(east, -by, 1), turn(west, 32 - by, 1), turn(east_2, 64 - by, 1))
        low = jnp.where(quarter == 0, parts[0], parts[1])
        return jnp.where(quarter < 2, low, jnp.where(quarter == 2, parts[2], parts[3]))

    owner = gathered(0).astype(jnp.int32)
    slot = gathered(32).astype(jnp.int32)
    used = gathered(64)
    slot = jnp.where((quarter & 1) == 0, slot + 64, slot)
    acc = [None] * 3
    for r in range(side.shape[1]):
        here = owner == r
        for f in range(3):
            source = jnp.broadcast_to(side[f, r : r + 1, :], slot.shape)
            value = jnp.take_along_axis(source, slot, axis=1)
            acc[f] = value if r == 0 else jnp.where(here, value, acc[f])
    rims = ([], [])
    for f in range(3):
        v = acc[f] * used
        v = v + turn(v, -16, 1)
        v = v + turn(v, -8, 1)
        rims[0].append(rim_of(v, v, -32, 56))
        rims[1].append(rim_of(v, v, -96, 120))
    return rims


def rim_lookup_kernel(
    table_ref, two_ref, one_ref, pick_row_ref, pick_lane_ref, used_ref, rows_ref, level_ref, height_ref,
    transport_ref, second_ref, first_ref, flux_ref, rim_ref, tab, side, pack,
):
    n_lon = table_ref.shape[0]
    half = n_lon // 2
    rows, cols = height_ref.shape
    low = lanes((half, 128)) < 64
    for pair in range(2):
        part = table_ref[:, 0, pair * 128 : (pair + 1) * 128]
        lo, hi = part[:half], part[half:]
        tab[2 * pair] = jnp.where(low, lo, turn(hi, 64, 1))
        tab[2 * pair + 1] = jnp.where(low, turn(lo, 64, 1), hi)
    for f in range(3):
        side[f] = table_ref[:, 0, LISTS + f * 128 : LISTS + (f + 1) * 128]
    lane = lanes((HALO, cols))
    cuts = (slice(rows - HALO, rows), slice(0, HALO))
    sides = [from_lon(one_ref, two_ref, cut) for cut in cuts]
    side_rims = side_lookup(side, sides)
    for s, cut in enumerate(cuts):
        found = own_lookup(tab, pick_row_ref, pick_lane_ref, used_ref, cut, (1, 2, 3))
        for f in range(3):
            flux_ref[s, f] = found[f + 1]
            rim_ref[s, f] = side_rims[s][f]
        rims = state_rims(*sides[s]) + side_rims[s]
        own = [
            height_ref[cut], transport_ref[0, cut], transport_ref[1, cut], level_ref[cut].astype(F32),
            found[1], found[2], found[3],
        ]
        packed = jnp.zeros((HALO, cols), F32)
        for i in range(FIELDS):
            pack[s, i * HALO : (i + 1) * HALO] = own[i]
            start = 2 * HALO * i
            here = (lane >= start) & (lane < start + 2 * HALO)
            packed = jnp.where(here, turn(rims[i], start + HALO, 1), packed)
        pack[s, ROW_RIM:ROW_T] = packed
        pack[s, ROW_T:] = rows_ref[s]
    even = is_even("lat")
    north_going, south_going = pack[0], pack[1]
    second_ref[...] = jnp.where(even, south_going, north_going)
    first_ref[...] = jnp.where(even, north_going, south_going)


def sources(flux_ref, level_ref, cut):
    wet = (level_ref[cut] > 0).astype(F32)
    return heat_gain * flux_ref[0, cut] * wet, -salt_gain * flux_ref[1, cut] * wet


def lookup_kernel(
    edge_flux_ref, edge_rim_ref, tab, side, two_ref, one_ref, pick_row_ref, pick_lane_ref, used_ref,
    level_ref, x_ref, unit_ref, flux_ref, rim_ref, t_out, fixed, sems,
):
    rows = used_ref.shape[1]
    depth = x_ref.shape[1]
    cuts = [slice(at, at + HALO) for at in range(0, rows, HALO)]
    sides = [from_lon(one_ref, two_ref, cut) for cut in cuts]
    for at in range(1, len(cuts) - 1, 2):
        side_rims = side_lookup(side, sides[at : at + 2])
        for i in range(2):
            cut = cuts[at + i]
            found = own_lookup(tab, pick_row_ref, pick_lane_ref, used_ref, cut, (0, 1, 2, 3))
            for f in range(4):
                flux_ref[f, cut] = found[f]
            for g, rim in enumerate(state_rims(*sides[at + i]) + side_rims[i]):
                rim_ref[g, cut] = rim
    mid = slice(HALO, rows - HALO)
    source = sources(flux_ref, level_ref, mid)
    copies = []
    for c in range(2):
        for l in range(depth):
            fixed[c, l] = x_ref[c, l, mid] + unit_ref[l, mid] * source[c]
        copies.append(pltpu.make_async_copy(fixed.at[c], t_out.at[c, :, mid], sems.at[c]))
        copies[c].start()
    for s, at in ((0, len(cuts) - 1), (1, 0)):
        cut = cuts[at]
        flux_ref[0, cut] = own_lookup(tab, pick_row_ref, pick_lane_ref, used_ref, cut, (0,))[0]
        for f in range(3):
            flux_ref[f + 1, cut] = edge_flux_ref[s, f]
        for g, rim in enumerate(state_rims(*sides[at]) + [edge_rim_ref[s, f] for f in range(3)]):
            rim_ref[g, cut] = rim
    for copy in copies:
        copy.wait()


def split(x):
    hi = x.astype(jnp.bfloat16)
    return hi, (x - hi.astype(F32)).astype(jnp.bfloat16)


def tracer_kernel(
    two_ref, one_ref, t_0_ref, level_ref, diff_ref, t_ref, u_ref, v_hbm, x_ref, unit_ref, inv_rows_ref, gain_ref,
    parts, rims, net_x, v_ref, sem,
):
    depth, rows, cols = t_ref.shape[1:]
    copy = pltpu.make_async_copy(v_hbm.at[1], v_ref, sem)
    copy.start()
    shape = (rows, cols)
    east, west = from_lon(one_ref, two_ref, slice(0, rows))
    t_e, t_w = from_lon(one_ref, two_ref, slice(rows, 2 * rows))
    level = level_ref[...]
    level_f = level.astype(F32)
    lane = lanes(shape)
    row = rows_of(shape)
    first = LEVELS * HALO
    last = cols - 1
    level_e = jnp.where(lane == last, turn(east, last - first, 1), turn(level_f, -1, 1))
    level_n = turn(level_f, -1, 0)
    face_e = jnp.minimum(level_f, level_e)
    face_n = jnp.where(row == rows - 1, 0.0, jnp.minimum(level_f, level_n))
    t_0 = t_0_ref[...]
    u_w = jnp.where(lane < depth, turn(t_w, -2 * depth, 1), turn(t_w, -depth, 1))
    layer = jnp.where(lane < depth, lane, lane - depth).astype(F32)
    level_w = west[:, first + HALO - 1 : first + HALO]
    face_w = jnp.broadcast_to(jnp.minimum(level_f[:, 0:1], level_w), shape)
    west_flux = jnp.where((layer < face_w) & (lane < 2 * depth), u_w * ((t_w + t_0) * 0.5), 0.0)
    both = []
    for x in (turn(t_e, -1, 1), west_flux):
        hi, lo = split(x)
        both.append(jnp.where(lane < 64, hi.astype(F32), turn(lo.astype(F32), 64, 1)))
    plane = lane & 63
    for f in range(2 * depth):
        at = slice(f * rows, (f + 1) * rows)
        here = plane == f
        parts[at, 0:128] = jnp.where(here, both[0], 0.0).astype(jnp.bfloat16)
        parts[at, 128:256] = jnp.where(here, both[1], 0.0).astype(jnp.bfloat16)
    k = lax.broadcasted_iota(jnp.int32, (2 * cols, cols), 0)
    into = jnp.where(k < cols, last, 0) == lanes((2 * cols, cols))
    rims[...] = jnp.dot(parts[...], into.astype(F32).astype(jnp.bfloat16), preferred_element_type=F32)
    for l in range(depth):
        mask_e = face_e > l
        u_l = u_ref[l] * 0.5
        for c in range(2):
            f = c * depth + l
            at = slice(f * rows, (f + 1) * rows)
            t = t_ref[c, l]
            t_east = jnp.where(lane == last, rims[at], turn(t, -1, 1))
            flux_e = jnp.where(mask_e, u_l * (t + t_east), 0.0)
            net_x[at] = flux_e - jnp.where(lane == 0, rims[at], turn(flux_e, 1, 1))
    copy.wait()
    diff = diff_ref[...]
    above = jnp.zeros(shape, F32)
    inv = None
    right = [None, None, None]
    for l in range(depth):
        below = jnp.where(level > l + 1, diff, 0.0) if l < depth - 1 else jnp.zeros(shape, F32)
        pivot = 1.0 + above + below
        if l > 0:
            pivot = pivot - above * above * inv
        inv = 1.0 / pivot
        inv_rows_ref[0, l : l + 1] = inv[rows - 1 : rows]
        inv_rows_ref[1, l : l + 1] = inv[0:1]
        gain_ref[l] = below * inv
        mask_n = face_n > l
        v_l = v_ref[l] * 0.5
        for c in range(2):
            f = c * depth + l
            at = slice(f * rows, (f + 1) * rows)
            t = t_ref[c, l]
            flux_n = jnp.where(mask_n, v_l * (t + turn(t, -1, 0)), 0.0)
            flux_s = turn(flux_n, 1, 0)
            forced = t - adv_rate * (net_x[at] + (flux_n - flux_s))
            right[c] = forced * inv if l == 0 else (forced + above * right[c]) * inv
            x_ref[c, l] = right[c]
        right[2] = inv if l == 0 else above * right[2] * inv
        unit_ref[l] = right[2]
        above = below
    for l in range(depth - 2, -1, -1):
        gain = gain_ref[l]
        for c in range(2):
            right[c] = x_ref[c, l] + gain * right[c]
            x_ref[c, l] = right[c]
        right[2] = unit_ref[l] + gain * right[2]
        unit_ref[l] = right[2]


def step_kernel(
    second_ref, first_ref, height_ref, transport_ref, level_ref, diff_ref, flux_ref, rim_ref, rows_ref, inv_rows_ref,
    x_ref, unit_ref, t_middle, t_out, height_out, transport_out, north_ref, shift, fixed, result, sems,
):
    top = is_top()
    level = level_ref[...]
    level_f = level.astype(F32)
    rows, cols = level.shape
    depth = x_ref.shape[1]
    lo, hi = slice(0, HALO), slice(rows - HALO, rows)
    copies = []

    def send(value, out):
        copies.append(pltpu.make_async_copy(value, out, sems.at[len(copies)]))
        copies[-1].start()

    even = is_even("lat")
    a, b = first_ref[...], second_ref[...]
    south = jnp.where(even, b, a)
    north = jnp.where(even, a, b)
    mirrored = jnp.take_along_axis(north, 127 - lanes(north.shape), axis=1)
    north = jnp.where(top, mirrored, north)
    north_ref[...] = north

    first = LEVELS * HALO
    level_n = jnp.where(top, north[first + HALO - 1 : first + HALO], north[first : first + 1])
    level_s = south[first + HALO - 1 : first + HALO]
    sides = ((north, level_n, rows - 1, -adv_rate), (south, level_s, 0, adv_rate))
    chains = []
    for s, (message, level_out, at, gain) in enumerate(sides):
        level_in = level_f[at : at + 1]
        face = jnp.minimum(level_in, level_out)
        speed = rows_ref[0, 2 * depth :] if s == 0 else message[ROW_T + 2 * depth :]
        for c in range(2):
            planes = slice(c * depth, (c + 1) * depth)
            outside = message[ROW_T + c * depth : ROW_T + (c + 1) * depth]
            flux = speed * ((outside + rows_ref[s, planes]) * 0.5)
            deep = rows_of(flux.shape).astype(F32) < face
            shift[s, planes] = jnp.where(deep, gain * flux, 0.0)
            chains.append((s, c, level_in, diff_ref[at : at + 1]))
    right = [None] * 4
    for l in range(depth):
        for i, (s, c, level_in, diff_in) in enumerate(chains):
            at = c * depth + l
            inv = inv_rows_ref[s, l : l + 1]
            value = shift[s, at : at + 1]
            if l > 0:
                value = value + jnp.where(level_in > l, diff_in, 0.0) * right[i]
            right[i] = value * inv
            shift[s, at : at + 1] = right[i]
    for l in range(depth - 2, -1, -1):
        for i, (s, c, level_in, diff_in) in enumerate(chains):
            at = c * depth + l
            inv = inv_rows_ref[s, l : l + 1]
            below = jnp.where(level_in > l + 1, diff_in, 0.0) * inv
            right[i] = shift[s, at : at + 1] + below * right[i]
            shift[s, at : at + 1] = right[i]
    row = rows_of((HALO, cols))
    for s, cut, at_row in ((0, hi, HALO - 1), (1, lo, 0)):
        source = sources(flux_ref, level_ref, cut)
        for c in range(2):
            for l in range(depth):
                at = c * depth + l
                add = jnp.broadcast_to(shift[s, at : at + 1], (HALO, cols))
                x = x_ref[c, l, cut] + unit_ref[l, cut] * source[c]
                fixed[s, c, l] = x + jnp.where(row == at_row, add, 0.0)
        send(fixed.at[s], t_out.at[:, :, cut])

    own = (
        height_ref[...], transport_ref[0], transport_ref[1], level_f,
        flux_ref[1], flux_ref[2], flux_ref[3],
    )
    ext = []
    lane = lanes((HALO, cols))
    side = (lane < HALO) | (lane >= cols - HALO)
    for i in range(FIELDS):
        at = slice(i * HALO, (i + 1) * HALO)
        whole = jnp.concatenate([south[at], own[i], north[at]], axis=0)
        start = jnp.where(top, cols - 2 * HALO * (FIELDS - i) - HALO, cols - 2 * HALO * i - HALO)
        north_rim = jnp.where(side, pltpu.roll(north[ROW_RIM:ROW_T], start, 1), 0.0)
        south_rim = jnp.where(side, turn(south[ROW_RIM:ROW_T], -(2 * HALO * i + HALO), 1), 0.0)
        rim = jnp.concatenate([south_rim, rim_ref[i], north_rim], axis=0)
        ext.append(jnp.concatenate([whole, rim], axis=1))


    def coefficients(f):
        wet = (f[LEVELS] > 0.0).astype(F32)
        return (
            wet,
            wave_grad * (f[LEVELS] / depth),
            fresh_gain * f[FRESH] * wet,
            wind_gain * f[WIND_E] * wet,
            wind_gain * f[WIND_N] * wet,
        )

    mine = [x for x in ext]
    fold = [x[HALO + rows :] for x in ext]
    wet, grad, fresh, wind_e, wind_n = coefficients(mine)
    p_wet, p_grad, p_fresh, p_wind_e, p_wind_n = coefficients(fold)
    h, e, n = mine[HEIGHT], mine[EAST], mine[NORTH]
    p_h, p_e, p_n = fold[HEIGHT], fold[EAST], fold[NORTH]
    row = rows_of(h.shape)
    last = HALO + rows - 1
    across = (row == last) & top
    p_last = rows_of(p_h.shape) == HALO - 1
    for _ in range(SUBSTEPS):
        h = (h - wave_div * ((e - turn(e, 1, 1)) + (n - turn(n, 1, 0)))) * wet + fresh
        p_h = (p_h - wave_div * ((p_e - turn(p_e, -1, 1)) + (p_n - turn(p_n, 1, 0)))) * p_wet + p_fresh
        h_n = jnp.where(across, jnp.broadcast_to(p_h[HALO - 1 :], h.shape), turn(h, -1, 0))
        p_h_n = jnp.where(p_last, jnp.broadcast_to(h[last : last + 1], p_h.shape), turn(p_h, -1, 0))
        e = (e - grad * (turn(h, -1, 1) - h)) * wet + wind_e
        n = (n - grad * (h_n - h)) * wet + wind_n
        p_e = (p_e - p_grad * (turn(p_h, 1, 1) - p_h)) * p_wet + p_wind_e
        p_n = (p_n - p_grad * (p_h_n - p_h)) * p_wet + p_wind_n
    inside = slice(HALO, HALO + rows)
    result[0] = h[inside, :cols]
    result[1] = e[inside, :cols]
    result[2] = n[inside, :cols]
    send(result.at[0], height_out)
    send(result.at[1:3], transport_out)

    for copy in copies:
        copy.wait()


def vmem(count):
    return [pl.BlockSpec(memory_space=pltpu.VMEM)] * count


def params(mib=24):
    return pltpu.CompilerParams(vmem_limit_bytes=mib * 1024 * 1024)


def work(mb):
    return pl.CostEstimate(flops=mb * 1000000, bytes_accessed=mb * 1000000, transcendentals=0)


def in_hbm(x):
    return pltpu.with_memory_space_constraint(x, pltpu.HBM)


def shape_of(*shape):
    return jax.ShapeDtypeStruct(shape, F32)


def lat_pairs(n_lat, n_lon):
    def at(i, j):
        return i * n_lon + j

    first, second = [], []
    for j in range(n_lon):
        for i in range(0, n_lat, 2):
            first += [(at(i, j), at(i + 1, j)), (at(i + 1, j), at(i, j))]
        for i in range(1, n_lat - 1, 2):
            second += [(at(i, j), at(i + 1, j)), (at(i + 1, j), at(i, j))]
        second.append((at(n_lat - 1, j), at(n_lat - 1, n_lon - 1 - j)))
    return first, second


def lon_pairs(n_lon):
    first, second = [], []
    for j in range(0, n_lon, 2):
        first += [(j, j + 1), (j + 1, j)]
        k, m = j + 1, (j + 2) % n_lon
        second += [(k, m), (m, k)]
    return first, second


def per_device(
    tracers,
    velocity,
    diffusivity,
    ocean_levels,
    surface_height,
    transport,
    atm_flux,
    send_rows,
    src_owner,
    src_slot,
    xgrid_weights,
    xgrid_count,
):
    n_lat, n_lon = lax.axis_size("lat"), lax.axis_size("lon")
    depth, rows, cols = tracers.shape[1:]
    slots = send_rows.shape[3]
    picked = pl.pallas_call(
        pick_kernel,
        out_shape=pltpu.VMEM((n_lon, 1, 10 * slots), F32),
        in_specs=[pl.BlockSpec(memory_space=pltpu.HBM)] * 2,
        out_specs=vmem(1)[0],
        scratch_shapes=[
            pltpu.VMEM(atm_flux.shape, F32),
            pltpu.VMEM(send_rows.shape, jnp.int32),
            pltpu.SemaphoreType.DMA((2,)),
        ],
        compiler_params=params(24),
        cost_estimate=work(40),
        name="pick",
    )(in_hbm(atm_flux), in_hbm(send_rows))
    table = lax.all_to_all(picked, "lon", split_axis=0, concat_axis=0, tiled=True)

    block = (rows, cols)
    lat_rows = ROW_T + 3 * depth
    two, one, t_0, edge_rows, pick_row, pick_lane, used, tracers, speed_e = pl.pallas_call(
        edge_kernel,
        out_shape=(
            shape_of(2 * rows, cols),
            shape_of(2 * rows, cols),
            shape_of(*block),
            shape_of(2, 3 * depth, cols),
            jax.ShapeDtypeStruct((4, *block), jnp.int32),
            jax.ShapeDtypeStruct((4, *block), jnp.int32),
            shape_of(4, *block),
            shape_of(2, depth, *block),
            shape_of(depth, *block),
        ),
        in_specs=[pl.BlockSpec(memory_space=pl.ANY)] + [pl.BlockSpec(memory_space=pltpu.HBM)] * 2 + vmem(7),
        out_specs=vmem(9),
        scratch_shapes=[pltpu.VMEM((depth, HALO, cols), F32), pltpu.SemaphoreType.DMA((4,))],
        compiler_params=params(),
        cost_estimate=work(2),
        name="edges",
    )(
        picked, in_hbm(tracers), in_hbm(velocity), ocean_levels, surface_height, transport, src_owner, src_slot,
        xgrid_weights, xgrid_count,
    )
    pairs = lon_pairs(n_lon)
    two = lax.ppermute(two, "lon", pairs[1])
    one = lax.ppermute(one, "lon", pairs[0])

    solved, unit, inv_rows = pl.pallas_call(
        tracer_kernel,
        out_shape=(shape_of(2, depth, *block), shape_of(depth, *block), shape_of(2, depth, cols)),
        in_specs=vmem(7) + [pl.BlockSpec(memory_space=pltpu.HBM)],
        out_specs=vmem(3),
        scratch_shapes=[
            pltpu.VMEM((depth, *block), F32),
            pltpu.VMEM((2 * depth * rows, 2 * cols), jnp.bfloat16),
            pltpu.VMEM((2 * depth * rows, cols), F32),
            pltpu.VMEM((2 * depth * rows, cols), F32),
            pltpu.VMEM((depth, *block), F32),
            pltpu.SemaphoreType.DMA,
        ],
        compiler_params=params(),
        cost_estimate=work(8),
        name="tracers",
    )(two, one, t_0, ocean_levels, diffusivity, tracers, speed_e, in_hbm(velocity))

    second, first, edge_flux, edge_rim, tab, side = pl.pallas_call(
        rim_lookup_kernel,
        out_shape=(
            shape_of(lat_rows, cols),
            shape_of(lat_rows, cols),
            shape_of(2, 3, HALO, cols),
            shape_of(2, 3, HALO, cols),
            shape_of(4, n_lon // 2, 128),
            shape_of(3, n_lon, 128),
        ),
        in_specs=vmem(10),
        out_specs=vmem(6),
        scratch_shapes=[pltpu.VMEM((2, lat_rows, cols), F32)],
        compiler_params=params(),
        cost_estimate=work(8),
        name="rim_lookup",
    )(
        table, two, one, pick_row, pick_lane, used, edge_rows, ocean_levels, surface_height, transport,
    )
    pairs = lat_pairs(n_lat, n_lon)
    second = lax.ppermute(second, ("lat", "lon"), pairs[1])
    first = lax.ppermute(first, ("lat", "lon"), pairs[0])

    flux, rim, t_middle = pl.pallas_call(
        lookup_kernel,
        out_shape=(shape_of(4, *block), shape_of(FIELDS, *block), shape_of(2, depth, *block)),
        in_specs=vmem(12),
        out_specs=vmem(2) + [pl.BlockSpec(memory_space=pltpu.HBM)],
        scratch_shapes=[pltpu.VMEM((2, depth, rows - 2 * HALO, cols), F32), pltpu.SemaphoreType.DMA((2,))],
        compiler_params=params(),
        cost_estimate=work(8),
        name="lookup",
    )(
        edge_flux, edge_rim, tab, side, two, one, pick_row, pick_lane, used, ocean_levels, solved, unit,
    )

    return pl.pallas_call(
        step_kernel,
        out_shape=(shape_of(2, depth, rows, cols), shape_of(rows, cols), shape_of(2, rows, cols)),
        in_specs=vmem(12) + [pl.BlockSpec(memory_space=pltpu.HBM)],
        out_specs=(pl.BlockSpec(memory_space=pltpu.HBM),) * 3,
        input_output_aliases={12: 0},
        scratch_shapes=[
            pltpu.VMEM((lat_rows, cols), F32),
            pltpu.VMEM((2, 2 * depth, cols), F32),
            pltpu.VMEM((2, 2, depth, HALO, cols), F32),
            pltpu.VMEM((3, rows, cols), F32),
            pltpu.SemaphoreType.DMA((4,)),
        ],
        compiler_params=params(),
        name="step",
    )(
        second, first, surface_height, transport, ocean_levels, diffusivity, flux, rim, edge_rows, inv_rows,
        solved, unit, t_middle,
    )


def solution(mesh):
    return jax.shard_map(
        per_device,
        mesh=mesh,
        in_specs=(
            P(None, None, "lat", "lon"),
            P(None, None, "lat", "lon"),
            P("lat", "lon"),
            P("lat", "lon"),
            P("lat", "lon"),
            P(None, "lat", "lon"),
            P("lat", None, "lon"),
            P("lat", "lon", None, None),
            P(None, "lat", "lon"),
            P(None, "lat", "lon"),
            P(None, "lat", "lon"),
            P("lat", "lon"),
        ),
        out_specs=(P(None, None, "lat", "lon"), P("lat", "lon"), P(None, "lat", "lon")),
        check_vma=False,
    )
```

```python
import jax
import jax.numpy as jnp
from jax import lax
from jax.experimental import pallas as pl
from jax.experimental.pallas import tpu as pltpu
from jax.sharding import PartitionSpec as P

SUBSTEPS = 6
HALO = 8
FIELDS = 7
HEIGHT, EAST, NORTH, LEVELS, FRESH, WIND_E, WIND_N = range(FIELDS)
ROW_RIM = FIELDS * HALO
ROW_T = ROW_RIM + HALO
LISTS = 256
OWNER, SLOT, USED = 32, 64, 96

adv_rate = 0.1
heat_gain = 0.5
salt_gain = 0.5
wave_div = 0.5
wave_grad = 0.8
fresh_gain = 0.2
wind_gain = 0.2

F32 = jnp.float32


def lanes(shape):
    return lax.broadcasted_iota(jnp.int32, shape, len(shape) - 1)


def rows_of(shape):
    return lax.broadcasted_iota(jnp.int32, shape, len(shape) - 2)


def turn(x, by, axis):
    size = x.shape[axis]
    by = by % size
    return x if by == 0 else pltpu.roll(x, by, axis)


def is_even(axis):
    return lax.rem(lax.axis_index(axis), 2) == 0


def is_top():
    return lax.axis_index("lat") == lax.axis_size("lat") - 1


def pick_kernel(atm_hbm, rows_hbm, out_ref, atm_ref, rows_ref, sems):
    copies = [
        pltpu.make_async_copy(atm_hbm, atm_ref, sems.at[0]),
        pltpu.make_async_copy(rows_hbm, rows_ref, sems.at[1]),
    ]
    for copy in copies:
        copy.start()
    for copy in copies:
        copy.wait()
    rows = rows_ref[0, 0]
    both = jnp.concatenate([rows, rows], axis=1)
    lane = both & 127
    part = both >> 7
    low = lanes(both.shape) < 64
    values = []
    for f in range(4):
        acc = None
        for k in range(atm_ref.shape[2] // 128):
            row = jnp.broadcast_to(atm_ref[0, f : f + 1, k * 128 : (k + 1) * 128], both.shape)
            value = jnp.take_along_axis(row, lane, axis=1)
            acc = value if k == 0 else jnp.where(part == k, value, acc)
        values.append(acc)
    out_ref[:, 0, 0:128] = jnp.where(low, values[0], values[1])
    out_ref[:, 0, 128:256] = jnp.where(low, values[2], values[3])
    for f in range(1, 4):
        at = 128 + f * 128
        out_ref[:, 0, at : at + 128] = jnp.where(low, turn(values[f], -1, 0), turn(values[f], 1, 0))


def edge_kernel(
    picked_ref, t_hbm, v_hbm, level_ref, height_ref, transport_ref, owner_ref, slot_ref, weight_ref, count_ref,
    two_ref, one_ref, t_0_ref, rows_ref, pick_row_ref, pick_lane_ref, used_ref, t_ref, u_ref, v_rows, sems,
):
    depth, rows, cols = t_ref.shape[1:]
    copies = [
        pltpu.make_async_copy(t_hbm.at[0], t_ref.at[0], sems.at[0]),
        pltpu.make_async_copy(v_hbm.at[0], u_ref, sems.at[1]),
        pltpu.make_async_copy(t_hbm.at[1], t_ref.at[1], sems.at[2]),
        pltpu.make_async_copy(v_hbm.at[1, :, rows - HALO : rows], v_rows, sems.at[3]),
    ]
    for copy in copies:
        copy.start()
    shape = (rows, cols)
    lane = lanes(shape)
    level = level_ref[...]
    half = lax.axis_size("lon") // 2
    count = count_ref[...]
    for k in range(owner_ref.shape[0]):
        owner = owner_ref[k]
        high = owner >= half
        pick_row_ref[k] = jnp.where(high, owner - half, owner)
        pick_lane_ref[k] = jnp.where(high, slot_ref[k] + 64, slot_ref[k])
        used_ref[k] = jnp.where(count > k, weight_ref[k], 0.0)
    fields = [height_ref[...], transport_ref[0], transport_ref[1], level.astype(F32)]
    fields += [owner_ref[k].astype(F32) for k in range(4)]
    fields += [slot_ref[k].astype(F32) for k in range(4)]
    fields += [used_ref[k] for k in range(4)]
    west = jnp.zeros(shape, F32)
    east = jnp.zeros(shape, F32)
    for g, field in enumerate(fields):
        here = (lane >= g * HALO) & (lane < (g + 1) * HALO)
        west = jnp.where(here, turn(field, g * HALO, 1), west)
        east = jnp.where(here, turn(field, (g + 1) * HALO, 1), east)
    west_t = jnp.zeros(shape, F32)
    east_t = jnp.zeros(shape, F32)
    for c in range(2):
        copies[2 * c].wait()
        for l in range(depth):
            f = c * depth + l
            moved = turn(t_ref[c, l], f + 1, 1)
            west_t = jnp.where(lane == f + 1, moved, west_t)
            east_t = jnp.where(lane == f, moved, east_t)
    copies[1].wait()
    for l in range(depth):
        at = 2 * depth + l
        east_t = jnp.where(lane == at, turn(u_ref[l], at + 1, 1), east_t)
    even = is_even("lon")
    one_ref[:rows] = jnp.where(even, east, west)
    two_ref[:rows] = jnp.where(even, west, east)
    one_ref[rows:] = jnp.where(even, east_t, west_t)
    two_ref[rows:] = jnp.where(even, west_t, east_t)
    t_0_ref[...] = turn(west_t, -1, 1)
    for c in range(2):
        for l in range(depth):
            at = c * depth + l
            rows_ref[0, at : at + 1] = t_ref[c, l, rows - 1 : rows]
            rows_ref[1, at : at + 1] = t_ref[c, l, 0:1]
    copies[3].wait()
    for l in range(depth):
        at = 2 * depth + l
        rows_ref[0, at : at + 1] = v_rows[l, HALO - 1 : HALO]
    rows_ref[1, 2 * depth :] = jnp.zeros((depth, cols), F32)

def own_lookup(tab, row_ref, lane_ref, used_ref, cut, fields):
    total = {f: None for f in fields}
    for k in range(used_ref.shape[0]):
        lane = lane_ref[k, cut]
        row = row_ref[k, cut]
        acc = {}
        for r in range(tab.shape[1]):
            here = row == r
            for f in fields:
                source = jnp.broadcast_to(tab[f, r : r + 1, :], lane.shape)
                value = jnp.take_along_axis(source, lane, axis=1)
                acc[f] = value if r == 0 else jnp.where(here, value, acc[f])
        used = used_ref[k, cut]
        for f in fields:
            total[f] = acc[f] * used if k == 0 else total[f] + acc[f] * used
    return total


def rim_of(east, west, by_east, by_west):
    lane = lanes(east.shape)
    outer = jnp.where(lane >= 128 - HALO, turn(west, by_west, 1), 0.0)
    return jnp.where(lane < HALO, turn(east, by_east, 1), outer)


def from_lon(one_ref, two_ref, cut):
    even = is_even("lon")
    one, two = one_ref[cut], two_ref[cut]
    return jnp.where(even, one, two), jnp.where(even, two, one)


def state_rims(east, west):
    return [rim_of(east, west, -g * HALO, 128 - (g + 1) * HALO) for g in range(4)]


def side_lookup(side, sides):
    (east, west), (east_2, west_2) = sides
    lane = lanes(east.shape)
    quarter = lane >> 5

    def gathered(by):
        parts = (turn(west_2, -32 - by, 1), turn(east, -by, 1), turn(west, 32 - by, 1), turn(east_2, 64 - by, 1))
        low = jnp.where(quarter == 0, parts[0], parts[1])
        return jnp.where(quarter < 2, low, jnp.where(quarter == 2, parts[2], parts[3]))

    owner = gathered(0).astype(jnp.int32)
    slot = gathered(32).astype(jnp.int32)
    used = gathered(64)
    slot = jnp.where((quarter & 1) == 0, slot + 64, slot)
    acc = [None] * 3
    for r in range(side.shape[1]):
        here = owner == r
        for f in range(3):
            source = jnp.broadcast_to(side[f, r : r + 1, :], slot.shape)
            value = jnp.take_along_axis(source, slot, axis=1)
            acc[f] = value if r == 0 else jnp.where(here, value, acc[f])
    rims = ([], [])
    for f in range(3):
        v = acc[f] * used
        v = v + turn(v, -16, 1)
        v = v + turn(v, -8, 1)
        rims[0].append(rim_of(v, v, -32, 56))
        rims[1].append(rim_of(v, v, -96, 120))
    return rims


def rim_lookup_kernel(
    table_ref, two_ref, one_ref, pick_row_ref, pick_lane_ref, used_ref, rows_ref, level_ref, height_ref,
    transport_ref, after_ref, second_ref, first_ref, flux_ref, rim_ref, tab, side, pack,
):
    n_lon = table_ref.shape[0]
    half = n_lon // 2
    rows, cols = height_ref.shape
    low = lanes((half, 128)) < 64
    for pair in range(2):
        part = table_ref[:, 0, pair * 128 : (pair + 1) * 128]
        lo, hi = part[:half], part[half:]
        tab[2 * pair] = jnp.where(low, lo, turn(hi, 64, 1))
        tab[2 * pair + 1] = jnp.where(low, turn(lo, 64, 1), hi)
    for f in range(3):
        side[f] = table_ref[:, 0, LISTS + f * 128 : LISTS + (f + 1) * 128]
    lane = lanes((HALO, cols))
    cuts = (slice(rows - HALO, rows), slice(0, HALO))
    sides = [from_lon(one_ref, two_ref, cut) for cut in cuts]
    side_rims = side_lookup(side, sides)
    for s, cut in enumerate(cuts):
        found = own_lookup(tab, pick_row_ref, pick_lane_ref, used_ref, cut, (1, 2, 3))
        for f in range(3):
            flux_ref[s, f] = found[f + 1]
            rim_ref[s, f] = side_rims[s][f]
        rims = state_rims(*sides[s]) + side_rims[s]
        own = [
            height_ref[cut], transport_ref[0, cut], transport_ref[1, cut], level_ref[cut].astype(F32),
            found[1], found[2], found[3],
        ]
        packed = jnp.zeros((HALO, cols), F32)
        for i in range(FIELDS):
            pack[s, i * HALO : (i + 1) * HALO] = own[i]
            start = 2 * HALO * i
            here = (lane >= start) & (lane < start + 2 * HALO)
            packed = jnp.where(here, turn(rims[i], start + HALO, 1), packed)
        pack[s, ROW_RIM:ROW_T] = packed
        pack[s, ROW_T:] = rows_ref[s]
    even = is_even("lat")
    north_going, south_going = pack[0], pack[1]
    second_ref[...] = jnp.where(even, south_going, north_going)
    first_ref[...] = jnp.where(even, north_going, south_going)


def lookup_kernel(
    edge_flux_ref, edge_rim_ref, tab, side, two_ref, one_ref, pick_row_ref, pick_lane_ref, used_ref,
    flux_ref, rim_ref,
):
    rows = used_ref.shape[1]
    cuts = [slice(at, at + HALO) for at in range(0, rows, HALO)]
    sides = [from_lon(one_ref, two_ref, cut) for cut in cuts]
    for at in range(1, len(cuts) - 1, 2):
        side_rims = side_lookup(side, sides[at : at + 2])
        for i in range(2):
            cut = cuts[at + i]
            found = own_lookup(tab, pick_row_ref, pick_lane_ref, used_ref, cut, (0, 1, 2, 3))
            for f in range(4):
                flux_ref[f, cut] = found[f]
            for g, rim in enumerate(state_rims(*sides[at + i]) + side_rims[i]):
                rim_ref[g, cut] = rim
    for s, at in ((0, len(cuts) - 1), (1, 0)):
        cut = cuts[at]
        flux_ref[0, cut] = own_lookup(tab, pick_row_ref, pick_lane_ref, used_ref, cut, (0,))[0]
        for f in range(3):
            flux_ref[f + 1, cut] = edge_flux_ref[s, f]
        for g, rim in enumerate(state_rims(*sides[at]) + [edge_rim_ref[s, f] for f in range(3)]):
            rim_ref[g, cut] = rim


def split(x):
    hi = x.astype(jnp.bfloat16)
    return hi, (x - hi.astype(F32)).astype(jnp.bfloat16)


def faces_kernel(
    two_ref, one_ref, t_0_ref, level_ref, diff_ref, t_ref, u_ref, v_hbm,
    net_x, v_ref, inv_ref, gain_ref, unit_ref, inv_rows_ref, parts, rims, sem,
):
    depth, rows, cols = t_ref.shape[1:]
    copy = pltpu.make_async_copy(v_hbm.at[1], v_ref, sem)
    copy.start()
    shape = (rows, cols)
    east, west = from_lon(one_ref, two_ref, slice(0, rows))
    t_e, t_w = from_lon(one_ref, two_ref, slice(rows, 2 * rows))
    level = level_ref[...]
    level_f = level.astype(F32)
    lane = lanes(shape)
    first = LEVELS * HALO
    last = cols - 1
    level_e = jnp.where(lane == last, turn(east, last - first, 1), turn(level_f, -1, 1))
    face_e = jnp.minimum(level_f, level_e)
    t_0 = t_0_ref[...]
    u_w = jnp.where(lane < depth, turn(t_w, -2 * depth, 1), turn(t_w, -depth, 1))
    layer = jnp.where(lane < depth, lane, lane - depth).astype(F32)
    level_w = west[:, first + HALO - 1 : first + HALO]
    face_w = jnp.broadcast_to(jnp.minimum(level_f[:, 0:1], level_w), shape)
    west_flux = jnp.where((layer < face_w) & (lane < 2 * depth), u_w * ((t_w + t_0) * 0.5), 0.0)
    both = []
    for x in (turn(t_e, -1, 1), west_flux):
        hi, lo = split(x)
        both.append(jnp.where(lane < 64, hi.astype(F32), turn(lo.astype(F32), 64, 1)))
    plane = lane & 63
    for f in range(2 * depth):
        at = slice(f * rows, (f + 1) * rows)
        here = plane == f
        parts[at, 0:128] = jnp.where(here, both[0], 0.0).astype(jnp.bfloat16)
        parts[at, 128:256] = jnp.where(here, both[1], 0.0).astype(jnp.bfloat16)
    k = lax.broadcasted_iota(jnp.int32, (2 * cols, cols), 0)
    into = jnp.where(k < cols, last, 0) == lanes((2 * cols, cols))
    rims[...] = jnp.dot(parts[...], into.astype(F32).astype(jnp.bfloat16), preferred_element_type=F32)
    for l in range(depth):
        mask_e = face_e > l
        u_l = u_ref[l] * 0.5
        for c in range(2):
            f = c * depth + l
            at = slice(f * rows, (f + 1) * rows)
            t = t_ref[c, l]
            t_east = jnp.where(lane == last, rims[at], turn(t, -1, 1))
            flux_e = jnp.where(mask_e, u_l * (t + t_east), 0.0)
            net_x[at] = flux_e - jnp.where(lane == 0, rims[at], turn(flux_e, 1, 1))
    diff = diff_ref[...]
    above = jnp.zeros(shape, F32)
    inv = unit = None
    for l in range(depth):
        below = jnp.where(level > l + 1, diff, 0.0) if l < depth - 1 else jnp.zeros(shape, F32)
        pivot = 1.0 + above + below
        if l > 0:
            pivot = pivot - above * above * inv
        inv = 1.0 / pivot
        inv_ref[l] = inv
        inv_rows_ref[0, l : l + 1] = inv[rows - 1 : rows]
        inv_rows_ref[1, l : l + 1] = inv[0:1]
        gain_ref[l] = below * inv
        unit = inv if l == 0 else above * unit * inv
        unit_ref[l] = unit
        above = below
    for l in range(depth - 2, -1, -1):
        unit = unit_ref[l] + gain_ref[l] * unit
        unit_ref[l] = unit
    copy.wait()


def solve_kernel(net_x, level_ref, diff_ref, t_ref, v_ref, inv_ref, gain_ref, x_ref):
    depth, rows, cols = t_ref.shape[1:]
    shape = (rows, cols)
    level = level_ref[...]
    level_f = level.astype(F32)
    face_n = jnp.where(rows_of(shape) == rows - 1, 0.0, jnp.minimum(level_f, turn(level_f, -1, 0)))
    diff = diff_ref[...]
    right = [None, None]
    for l in range(depth):
        above = jnp.where(level > l, diff, 0.0)
        inv = inv_ref[l]
        mask_n = face_n > l
        v_l = v_ref[l] * 0.5
        for c in range(2):
            f = c * depth + l
            t = t_ref[c, l]
            flux_n = jnp.where(mask_n, v_l * (t + turn(t, -1, 0)), 0.0)
            flux_s = turn(flux_n, 1, 0)
            forced = t - adv_rate * (net_x[f * rows : (f + 1) * rows] + (flux_n - flux_s))
            right[c] = forced * inv if l == 0 else (forced + above * right[c]) * inv
            x_ref[c, l] = right[c]
    for l in range(depth - 2, -1, -1):
        gain = gain_ref[l]
        for c in range(2):
            right[c] = x_ref[c, l] + gain * right[c]
            x_ref[c, l] = right[c]


def step_kernel(
    second_ref, first_ref, height_ref, transport_ref, level_ref, diff_ref, flux_ref, rim_ref, rows_ref, inv_rows_ref,
    x_ref, unit_ref, t_out, height_out, transport_out, north_ref, shift, fixed, result, sems,
):
    top = is_top()
    level = level_ref[...]
    level_f = level.astype(F32)
    rows, cols = level.shape
    depth = x_ref.shape[1]
    wet_0 = (level > 0).astype(F32)
    source = (heat_gain * flux_ref[0] * wet_0, -salt_gain * flux_ref[1] * wet_0)
    lo, hi = slice(0, HALO), slice(rows - HALO, rows)
    mid = slice(HALO, rows - HALO)
    copies = []

    def send(value, out):
        copies.append(pltpu.make_async_copy(value, out, sems.at[len(copies)]))
        copies[-1].start()

    for c in range(2):
        for l in range(depth):
            fixed[c, l, mid] = x_ref[c, l, mid] + unit_ref[l, mid] * source[c][mid]
        send(fixed.at[c, :, mid], t_out.at[c, :, mid])
    even = is_even("lat")
    a, b = first_ref[...], second_ref[...]
    south = jnp.where(even, b, a)
    north = jnp.where(even, a, b)
    mirrored = jnp.take_along_axis(north, 127 - lanes(north.shape), axis=1)
    north = jnp.where(top, mirrored, north)
    north_ref[...] = north

    first = LEVELS * HALO
    level_n = jnp.where(top, north[first + HALO - 1 : first + HALO], north[first : first + 1])
    level_s = south[first + HALO - 1 : first + HALO]
    sides = ((north, level_n, rows - 1, -adv_rate), (south, level_s, 0, adv_rate))
    chains = []
    for s, (message, level_out, at, gain) in enumerate(sides):
        level_in = level_f[at : at + 1]
        face = jnp.minimum(level_in, level_out)
        speed = rows_ref[0, 2 * depth :] if s == 0 else message[ROW_T + 2 * depth :]
        for c in range(2):
            planes = slice(c * depth, (c + 1) * depth)
            outside = message[ROW_T + c * depth : ROW_T + (c + 1) * depth]
            flux = speed * ((outside + rows_ref[s, planes]) * 0.5)
            deep = rows_of(flux.shape).astype(F32) < face
            shift[s, planes] = jnp.where(deep, gain * flux, 0.0)
            chains.append((s, c, level_in, diff_ref[at : at + 1]))
    right = [None] * 4
    for l in range(depth):
        for i, (s, c, level_in, diff_in) in enumerate(chains):
            at = c * depth + l
            inv = inv_rows_ref[s, l : l + 1]
            value = shift[s, at : at + 1]
            if l > 0:
                value = value + jnp.where(level_in > l, diff_in, 0.0) * right[i]
            right[i] = value * inv
            shift[s, at : at + 1] = right[i]
    for l in range(depth - 2, -1, -1):
        for i, (s, c, level_in, diff_in) in enumerate(chains):
            at = c * depth + l
            inv = inv_rows_ref[s, l : l + 1]
            below = jnp.where(level_in > l + 1, diff_in, 0.0) * inv
            right[i] = shift[s, at : at + 1] + below * right[i]
            shift[s, at : at + 1] = right[i]
    row = rows_of((HALO, cols))
    for s, cut, at_row in ((0, hi, HALO - 1), (1, lo, 0)):
        for c in range(2):
            for l in range(depth):
                at = c * depth + l
                add = jnp.broadcast_to(shift[s, at : at + 1], (HALO, cols))
                x = x_ref[c, l, cut] + unit_ref[l, cut] * source[c][cut]
                fixed[c, l, cut] = x + jnp.where(row == at_row, add, 0.0)
        send(fixed.at[:, :, cut], t_out.at[:, :, cut])

    own = (
        height_ref[...], transport_ref[0], transport_ref[1], level_f,
        flux_ref[1], flux_ref[2], flux_ref[3],
    )
    ext = []
    lane = lanes((HALO, cols))
    side = (lane < HALO) | (lane >= cols - HALO)
    for i in range(FIELDS):
        at = slice(i * HALO, (i + 1) * HALO)
        whole = jnp.concatenate([south[at], own[i], north[at]], axis=0)
        start = jnp.where(top, cols - 2 * HALO * (FIELDS - i) - HALO, cols - 2 * HALO * i - HALO)
        north_rim = jnp.where(side, pltpu.roll(north[ROW_RIM:ROW_T], start, 1), 0.0)
        south_rim = jnp.where(side, turn(south[ROW_RIM:ROW_T], -(2 * HALO * i + HALO), 1), 0.0)
        rim = jnp.concatenate([south_rim, rim_ref[i], north_rim], axis=0)
        ext.append(jnp.concatenate([whole, rim], axis=1))


    def coefficients(f):
        wet = (f[LEVELS] > 0.0).astype(F32)
        return (
            wet,
            wave_grad * (f[LEVELS] / depth),
            fresh_gain * f[FRESH] * wet,
            wind_gain * f[WIND_E] * wet,
            wind_gain * f[WIND_N] * wet,
        )

    mine = [x for x in ext]
    fold = [x[HALO + rows :] for x in ext]
    wet, grad, fresh, wind_e, wind_n = coefficients(mine)
    p_wet, p_grad, p_fresh, p_wind_e, p_wind_n = coefficients(fold)
    h, e, n = mine[HEIGHT], mine[EAST], mine[NORTH]
    p_h, p_e, p_n = fold[HEIGHT], fold[EAST], fold[NORTH]
    row = rows_of(h.shape)
    last = HALO + rows - 1
    across = (row == last) & top
    p_last = rows_of(p_h.shape) == HALO - 1
    for _ in range(SUBSTEPS):
        h = (h - wave_div * ((e - turn(e, 1, 1)) + (n - turn(n, 1, 0)))) * wet + fresh
        p_h = (p_h - wave_div * ((p_e - turn(p_e, -1, 1)) + (p_n - turn(p_n, 1, 0)))) * p_wet + p_fresh
        h_n = jnp.where(across, jnp.broadcast_to(p_h[HALO - 1 :], h.shape), turn(h, -1, 0))
        p_h_n = jnp.where(p_last, jnp.broadcast_to(h[last : last + 1], p_h.shape), turn(p_h, -1, 0))
        e = (e - grad * (turn(h, -1, 1) - h)) * wet + wind_e
        n = (n - grad * (h_n - h)) * wet + wind_n
        p_e = (p_e - p_grad * (turn(p_h, 1, 1) - p_h)) * p_wet + p_wind_e
        p_n = (p_n - p_grad * (p_h_n - p_h)) * p_wet + p_wind_n
    inside = slice(HALO, HALO + rows)
    result[0] = h[inside, :cols]
    result[1] = e[inside, :cols]
    result[2] = n[inside, :cols]
    send(result.at[0], height_out)
    send(result.at[1:3], transport_out)

    for copy in copies:
        copy.wait()


def vmem(count):
    return [pl.BlockSpec(memory_space=pltpu.VMEM)] * count


def params(mib=24):
    return pltpu.CompilerParams(vmem_limit_bytes=mib * 1024 * 1024)


def work(mb):
    return pl.CostEstimate(flops=mb * 1000000, bytes_accessed=mb * 1000000, transcendentals=0)


def in_hbm(x):
    return pltpu.with_memory_space_constraint(x, pltpu.HBM)


def shape_of(*shape):
    return jax.ShapeDtypeStruct(shape, F32)


def lat_pairs(n_lat, n_lon):
    def at(i, j):
        return i * n_lon + j

    first, second = [], []
    for j in range(n_lon):
        for i in range(0, n_lat, 2):
            first += [(at(i, j), at(i + 1, j)), (at(i + 1, j), at(i, j))]
        for i in range(1, n_lat - 1, 2):
            second += [(at(i, j), at(i + 1, j)), (at(i + 1, j), at(i, j))]
        second.append((at(n_lat - 1, j), at(n_lat - 1, n_lon - 1 - j)))
    return first, second


def lon_pairs(n_lon):
    first, second = [], []
    for j in range(0, n_lon, 2):
        first += [(j, j + 1), (j + 1, j)]
        k, m = j + 1, (j + 2) % n_lon
        second += [(k, m), (m, k)]
    return first, second


def per_device(
    tracers,
    velocity,
    diffusivity,
    ocean_levels,
    surface_height,
    transport,
    atm_flux,
    send_rows,
    src_owner,
    src_slot,
    xgrid_weights,
    xgrid_count,
):
    n_lat, n_lon = lax.axis_size("lat"), lax.axis_size("lon")
    depth, rows, cols = tracers.shape[1:]
    slots = send_rows.shape[3]
    picked = pl.pallas_call(
        pick_kernel,
        out_shape=pltpu.VMEM((n_lon, 1, 10 * slots), F32),
        in_specs=[pl.BlockSpec(memory_space=pltpu.HBM)] * 2,
        out_specs=vmem(1)[0],
        scratch_shapes=[
            pltpu.VMEM(atm_flux.shape, F32),
            pltpu.VMEM(send_rows.shape, jnp.int32),
            pltpu.SemaphoreType.DMA((2,)),
        ],
        compiler_params=params(24),
        cost_estimate=work(40),
        name="pick",
    )(in_hbm(atm_flux), in_hbm(send_rows))
    table = lax.all_to_all(picked, "lon", split_axis=0, concat_axis=0, tiled=True)

    block = (rows, cols)
    lat_rows = ROW_T + 3 * depth
    two, one, t_0, edge_rows, pick_row, pick_lane, used, tracers, speed_e = pl.pallas_call(
        edge_kernel,
        out_shape=(
            shape_of(2 * rows, cols),
            shape_of(2 * rows, cols),
            shape_of(*block),
            shape_of(2, 3 * depth, cols),
            jax.ShapeDtypeStruct((4, *block), jnp.int32),
            jax.ShapeDtypeStruct((4, *block), jnp.int32),
            shape_of(4, *block),
            shape_of(2, depth, *block),
            shape_of(depth, *block),
        ),
        in_specs=[pl.BlockSpec(memory_space=pl.ANY)] + [pl.BlockSpec(memory_space=pltpu.HBM)] * 2 + vmem(7),
        out_specs=vmem(9),
        scratch_shapes=[pltpu.VMEM((depth, HALO, cols), F32), pltpu.SemaphoreType.DMA((4,))],
        compiler_params=params(),
        cost_estimate=work(2),
        name="edges",
    )(
        picked, in_hbm(tracers), in_hbm(velocity), ocean_levels, surface_height, transport, src_owner, src_slot,
        xgrid_weights, xgrid_count,
    )
    pairs = lon_pairs(n_lon)
    two = lax.ppermute(two, "lon", pairs[1])
    one = lax.ppermute(one, "lon", pairs[0])

    net_x, speed_n, inv, gain, unit, inv_rows = pl.pallas_call(
        faces_kernel,
        out_shape=(
            shape_of(2 * depth * rows, cols),
            shape_of(depth, *block),
            shape_of(depth, *block),
            shape_of(depth, *block),
            shape_of(depth, *block),
            shape_of(2, depth, cols),
        ),
        in_specs=vmem(7) + [pl.BlockSpec(memory_space=pltpu.HBM)],
        out_specs=vmem(6),
        scratch_shapes=[
            pltpu.VMEM((2 * depth * rows, 2 * cols), jnp.bfloat16),
            pltpu.VMEM((2 * depth * rows, cols), F32),
            pltpu.SemaphoreType.DMA,
        ],
        compiler_params=params(),
        cost_estimate=work(4),
        name="faces",
    )(two, one, t_0, ocean_levels, diffusivity, tracers, speed_e, in_hbm(velocity))

    second, first, edge_flux, edge_rim, tab, side = pl.pallas_call(
        rim_lookup_kernel,
        out_shape=(
            shape_of(lat_rows, cols),
            shape_of(lat_rows, cols),
            shape_of(2, 3, HALO, cols),
            shape_of(2, 3, HALO, cols),
            shape_of(4, n_lon // 2, 128),
            shape_of(3, n_lon, 128),
        ),
        in_specs=vmem(10) + [pl.BlockSpec(memory_space=pl.ANY)],
        out_specs=vmem(6),
        scratch_shapes=[pltpu.VMEM((2, lat_rows, cols), F32)],
        compiler_params=params(),
        cost_estimate=work(8),
        name="rim_lookup",
    )(
        table, two, one, pick_row, pick_lane, used, edge_rows, ocean_levels, surface_height, transport,
        inv_rows,
    )
    pairs = lat_pairs(n_lat, n_lon)
    second = lax.ppermute(second, ("lat", "lon"), pairs[1])
    first = lax.ppermute(first, ("lat", "lon"), pairs[0])

    solved = pl.pallas_call(
        solve_kernel,
        out_shape=shape_of(2, depth, *block),
        in_specs=vmem(7),
        out_specs=vmem(1)[0],
        compiler_params=params(),
        cost_estimate=work(4),
        name="solve",
    )(net_x, ocean_levels, diffusivity, tracers, speed_n, inv, gain)

    flux, rim = pl.pallas_call(
        lookup_kernel,
        out_shape=(shape_of(4, *block), shape_of(FIELDS, *block)),
        in_specs=vmem(9),
        out_specs=vmem(2),
        compiler_params=params(),
        cost_estimate=work(8),
        name="lookup",
    )(edge_flux, edge_rim, tab, side, two, one, pick_row, pick_lane, used)

    return pl.pallas_call(
        step_kernel,
        out_shape=(shape_of(2, depth, rows, cols), shape_of(rows, cols), shape_of(2, rows, cols)),
        in_specs=vmem(12),
        out_specs=(pl.BlockSpec(memory_space=pl.ANY),) * 3,
        scratch_shapes=[
            pltpu.VMEM((lat_rows, cols), F32),
            pltpu.VMEM((2, 2 * depth, cols), F32),
            pltpu.VMEM((2, depth, rows, cols), F32),
            pltpu.VMEM((3, rows, cols), F32),
            pltpu.SemaphoreType.DMA((6,)),
        ],
        compiler_params=params(),
        name="step",
    )(
        second, first, surface_height, transport, ocean_levels, diffusivity, flux, rim, edge_rows, inv_rows,
        solved, unit,
    )


def solution(mesh):
    return jax.shard_map(
        per_device,
        mesh=mesh,
        in_specs=(
            P(None, None, "lat", "lon"),
            P(None, None, "lat", "lon"),
            P("lat", "lon"),
            P("lat", "lon"),
            P("lat", "lon"),
            P(None, "lat", "lon"),
            P("lat", None, "lon"),
            P("lat", "lon", None, None),
            P(None, "lat", "lon"),
            P(None, "lat", "lon"),
            P(None, "lat", "lon"),
            P("lat", "lon"),
        ),
        out_specs=(P(None, None, "lat", "lon"), P("lat", "lon"), P(None, "lat", "lon")),
        check_vma=False,
    )
```

```python
import jax
import jax.numpy as jnp
from jax import lax
from jax.experimental import pallas as pl
from jax.experimental.pallas import tpu as pltpu
from jax.sharding import PartitionSpec as P

SUBSTEPS = 6
HALO = 8
FIELDS = 7
HEIGHT, EAST, NORTH, LEVELS, FRESH, WIND_E, WIND_N = range(FIELDS)
ROW_RIM = FIELDS * HALO
ROW_T = ROW_RIM + HALO
LISTS = 256
OWNER, SLOT, USED = 32, 64, 96

adv_rate = 0.1
heat_gain = 0.5
salt_gain = 0.5
wave_div = 0.5
wave_grad = 0.8
fresh_gain = 0.2
wind_gain = 0.2

F32 = jnp.float32


def lanes(shape):
    return lax.broadcasted_iota(jnp.int32, shape, len(shape) - 1)


def rows_of(shape):
    return lax.broadcasted_iota(jnp.int32, shape, len(shape) - 2)


def turn(x, by, axis):
    size = x.shape[axis]
    by = by % size
    return x if by == 0 else pltpu.roll(x, by, axis)


def is_even(axis):
    return lax.rem(lax.axis_index(axis), 2) == 0


def is_top():
    return lax.axis_index("lat") == lax.axis_size("lat") - 1


def pick_kernel(
    atm_hbm, rows_hbm, t_hbm, v_hbm, out_ref, t_ref, u_ref, atm_ref, rows_ref, sems,
):
    copies = [
        pltpu.make_async_copy(atm_hbm, atm_ref, sems.at[0]),
        pltpu.make_async_copy(rows_hbm, rows_ref, sems.at[1]),
        pltpu.make_async_copy(t_hbm, t_ref, sems.at[2]),
        pltpu.make_async_copy(v_hbm.at[0], u_ref, sems.at[3]),
    ]
    for copy in copies:
        copy.start()
    for copy in copies[:2]:
        copy.wait()
    rows = rows_ref[0, 0]
    both = jnp.concatenate([rows, rows], axis=1)
    lane = both & 127
    part = both >> 7
    low = lanes(both.shape) < 64
    values = []
    for f in range(4):
        acc = None
        for k in range(atm_ref.shape[2] // 128):
            row = jnp.broadcast_to(atm_ref[0, f : f + 1, k * 128 : (k + 1) * 128], both.shape)
            value = jnp.take_along_axis(row, lane, axis=1)
            acc = value if k == 0 else jnp.where(part == k, value, acc)
        values.append(acc)
    out_ref[:, 0, 0:128] = jnp.where(low, values[0], values[1])
    out_ref[:, 0, 128:256] = jnp.where(low, values[2], values[3])
    for f in range(1, 4):
        at = 128 + f * 128
        out_ref[:, 0, at : at + 128] = jnp.where(low, turn(values[f], -1, 0), turn(values[f], 1, 0))
    for copy in copies[2:]:
        copy.wait()


def edge_kernel(
    picked_ref, v_hbm, t_ref, u_ref, level_ref, height_ref, transport_ref, owner_ref, slot_ref, weight_ref, count_ref,
    two_ref, one_ref, t_0_ref, rows_ref, pick_row_ref, pick_lane_ref, used_ref, v_rows, sem,
):
    depth, rows, cols = t_ref.shape[1:]
    copy = pltpu.make_async_copy(v_hbm.at[1, :, rows - HALO : rows], v_rows, sem)
    copy.start()
    shape = (rows, cols)
    lane = lanes(shape)
    level = level_ref[...]
    half = lax.axis_size("lon") // 2
    count = count_ref[...]
    for k in range(owner_ref.shape[0]):
        owner = owner_ref[k]
        high = owner >= half
        pick_row_ref[k] = jnp.where(high, owner - half, owner)
        pick_lane_ref[k] = jnp.where(high, slot_ref[k] + 64, slot_ref[k])
        used_ref[k] = jnp.where(count > k, weight_ref[k], 0.0)
    fields = [height_ref[...], transport_ref[0], transport_ref[1], level.astype(F32)]
    fields += [owner_ref[k].astype(F32) for k in range(4)]
    fields += [slot_ref[k].astype(F32) for k in range(4)]
    fields += [used_ref[k] for k in range(4)]
    west = jnp.zeros(shape, F32)
    east = jnp.zeros(shape, F32)
    for g, field in enumerate(fields):
        here = (lane >= g * HALO) & (lane < (g + 1) * HALO)
        west = jnp.where(here, turn(field, g * HALO, 1), west)
        east = jnp.where(here, turn(field, (g + 1) * HALO, 1), east)
    west_t = jnp.zeros(shape, F32)
    east_t = jnp.zeros(shape, F32)
    for c in range(2):
        for l in range(depth):
            f = c * depth + l
            moved = turn(t_ref[c, l], f + 1, 1)
            west_t = jnp.where(lane == f + 1, moved, west_t)
            east_t = jnp.where(lane == f, moved, east_t)
    for l in range(depth):
        at = 2 * depth + l
        east_t = jnp.where(lane == at, turn(u_ref[l], at + 1, 1), east_t)
    even = is_even("lon")
    one_ref[:rows] = jnp.where(even, east, west)
    two_ref[:rows] = jnp.where(even, west, east)
    one_ref[rows:] = jnp.where(even, east_t, west_t)
    two_ref[rows:] = jnp.where(even, west_t, east_t)
    t_0_ref[...] = turn(west_t, -1, 1)
    for c in range(2):
        for l in range(depth):
            at = c * depth + l
            rows_ref[0, at : at + 1] = t_ref[c, l, rows - 1 : rows]
            rows_ref[1, at : at + 1] = t_ref[c, l, 0:1]
    copy.wait()
    for l in range(depth):
        at = 2 * depth + l
        rows_ref[0, at : at + 1] = v_rows[l, HALO - 1 : HALO]
    rows_ref[1, 2 * depth :] = jnp.zeros((depth, cols), F32)

def own_lookup(tab, row_ref, lane_ref, used_ref, cut, fields):
    total = {f: None for f in fields}
    for k in range(used_ref.shape[0]):
        lane = lane_ref[k, cut]
        row = row_ref[k, cut]
        acc = {}
        for r in range(tab.shape[1]):
            here = row == r
            for f in fields:
                source = jnp.broadcast_to(tab[f, r : r + 1, :], lane.shape)
                value = jnp.take_along_axis(source, lane, axis=1)
                acc[f] = value if r == 0 else jnp.where(here, value, acc[f])
        used = used_ref[k, cut]
        for f in fields:
            total[f] = acc[f] * used if k == 0 else total[f] + acc[f] * used
    return total


def rim_of(east, west, by_east, by_west):
    lane = lanes(east.shape)
    outer = jnp.where(lane >= 128 - HALO, turn(west, by_west, 1), 0.0)
    return jnp.where(lane < HALO, turn(east, by_east, 1), outer)


def from_lon(one_ref, two_ref, cut):
    even = is_even("lon")
    one, two = one_ref[cut], two_ref[cut]
    return jnp.where(even, one, two), jnp.where(even, two, one)


def state_rims(east, west):
    return [rim_of(east, west, -g * HALO, 128 - (g + 1) * HALO) for g in range(4)]


def side_lookup(side, sides):
    (east, west), (east_2, west_2) = sides
    lane = lanes(east.shape)
    quarter = lane >> 5

    def gathered(by):
        parts = (turn(west_2, -32 - by, 1), turn(east, -by, 1), turn(west, 32 - by, 1), turn(east_2, 64 - by, 1))
        low = jnp.where(quarter == 0, parts[0], parts[1])
        return jnp.where(quarter < 2, low, jnp.where(quarter == 2, parts[2], parts[3]))

    owner = gathered(0).astype(jnp.int32)
    slot = gathered(32).astype(jnp.int32)
    used = gathered(64)
    slot = jnp.where((quarter & 1) == 0, slot + 64, slot)
    acc = [None] * 3
    for r in range(side.shape[1]):
        here = owner == r
        for f in range(3):
            source = jnp.broadcast_to(side[f, r : r + 1, :], slot.shape)
            value = jnp.take_along_axis(source, slot, axis=1)
            acc[f] = value if r == 0 else jnp.where(here, value, acc[f])
    rims = ([], [])
    for f in range(3):
        v = acc[f] * used
        v = v + turn(v, -16, 1)
        v = v + turn(v, -8, 1)
        rims[0].append(rim_of(v, v, -32, 56))
        rims[1].append(rim_of(v, v, -96, 120))
    return rims


def rim_lookup_kernel(
    table_ref, two_ref, one_ref, pick_row_ref, pick_lane_ref, used_ref, rows_ref, level_ref, height_ref,
    transport_ref, second_ref, first_ref, flux_ref, rim_ref, tab, side, pack,
):
    n_lon = table_ref.shape[0]
    half = n_lon // 2
    rows, cols = height_ref.shape
    low = lanes((half, 128)) < 64
    for pair in range(2):
        part = table_ref[:, 0, pair * 128 : (pair + 1) * 128]
        lo, hi = part[:half], part[half:]
        tab[2 * pair] = jnp.where(low, lo, turn(hi, 64, 1))
        tab[2 * pair + 1] = jnp.where(low, turn(lo, 64, 1), hi)
    for f in range(3):
        side[f] = table_ref[:, 0, LISTS + f * 128 : LISTS + (f + 1) * 128]
    lane = lanes((HALO, cols))
    cuts = (slice(rows - HALO, rows), slice(0, HALO))
    sides = [from_lon(one_ref, two_ref, cut) for cut in cuts]
    side_rims = side_lookup(side, sides)
    for s, cut in enumerate(cuts):
        found = own_lookup(tab, pick_row_ref, pick_lane_ref, used_ref, cut, (1, 2, 3))
        for f in range(3):
            flux_ref[s, f] = found[f + 1]
            rim_ref[s, f] = side_rims[s][f]
        rims = state_rims(*sides[s]) + side_rims[s]
        own = [
            height_ref[cut], transport_ref[0, cut], transport_ref[1, cut], level_ref[cut].astype(F32),
            found[1], found[2], found[3],
        ]
        packed = jnp.zeros((HALO, cols), F32)
        for i in range(FIELDS):
            pack[s, i * HALO : (i + 1) * HALO] = own[i]
            start = 2 * HALO * i
            here = (lane >= start) & (lane < start + 2 * HALO)
            packed = jnp.where(here, turn(rims[i], start + HALO, 1), packed)
        pack[s, ROW_RIM:ROW_T] = packed
        pack[s, ROW_T:] = rows_ref[s]
    even = is_even("lat")
    north_going, south_going = pack[0], pack[1]
    second_ref[...] = jnp.where(even, south_going, north_going)
    first_ref[...] = jnp.where(even, north_going, south_going)


def lookup_kernel(
    edge_flux_ref, edge_rim_ref, tab, side, two_ref, one_ref, pick_row_ref, pick_lane_ref, used_ref,
    flux_ref, rim_ref,
):
    rows = used_ref.shape[1]
    cuts = [slice(at, at + HALO) for at in range(0, rows, HALO)]
    sides = [from_lon(one_ref, two_ref, cut) for cut in cuts]
    for at in range(1, len(cuts) - 1, 2):
        side_rims = side_lookup(side, sides[at : at + 2])
        for i in range(2):
            cut = cuts[at + i]
            found = own_lookup(tab, pick_row_ref, pick_lane_ref, used_ref, cut, (0, 1, 2, 3))
            for f in range(4):
                flux_ref[f, cut] = found[f]
            for g, rim in enumerate(state_rims(*sides[at + i]) + side_rims[i]):
                rim_ref[g, cut] = rim
    for s, at in ((0, len(cuts) - 1), (1, 0)):
        cut = cuts[at]
        flux_ref[0, cut] = own_lookup(tab, pick_row_ref, pick_lane_ref, used_ref, cut, (0,))[0]
        for f in range(3):
            flux_ref[f + 1, cut] = edge_flux_ref[s, f]
        for g, rim in enumerate(state_rims(*sides[at]) + [edge_rim_ref[s, f] for f in range(3)]):
            rim_ref[g, cut] = rim


def split(x):
    hi = x.astype(jnp.bfloat16)
    return hi, (x - hi.astype(F32)).astype(jnp.bfloat16)


def tracer_kernel(
    two_ref, one_ref, t_0_ref, level_ref, diff_ref, t_ref, u_ref, v_hbm, x_ref, unit_ref, inv_rows_ref, gain_ref,
    parts, rims, net_x, v_ref, inv_ref, sem,
):
    depth, rows, cols = t_ref.shape[1:]
    copy = pltpu.make_async_copy(v_hbm.at[1], v_ref, sem)
    copy.start()
    shape = (rows, cols)
    east, west = from_lon(one_ref, two_ref, slice(0, rows))
    t_e, t_w = from_lon(one_ref, two_ref, slice(rows, 2 * rows))
    level = level_ref[...]
    level_f = level.astype(F32)
    lane = lanes(shape)
    row = rows_of(shape)
    first = LEVELS * HALO
    last = cols - 1
    level_e = jnp.where(lane == last, turn(east, last - first, 1), turn(level_f, -1, 1))
    level_n = turn(level_f, -1, 0)
    face_e = jnp.minimum(level_f, level_e)
    face_n = jnp.where(row == rows - 1, 0.0, jnp.minimum(level_f, level_n))
    t_0 = t_0_ref[...]
    u_w = jnp.where(lane < depth, turn(t_w, -2 * depth, 1), turn(t_w, -depth, 1))
    layer = jnp.where(lane < depth, lane, lane - depth).astype(F32)
    level_w = west[:, first + HALO - 1 : first + HALO]
    face_w = jnp.broadcast_to(jnp.minimum(level_f[:, 0:1], level_w), shape)
    west_flux = jnp.where((layer < face_w) & (lane < 2 * depth), u_w * ((t_w + t_0) * 0.5), 0.0)
    both = []
    for x in (turn(t_e, -1, 1), west_flux):
        hi, lo = split(x)
        both.append(jnp.where(lane < 64, hi.astype(F32), turn(lo.astype(F32), 64, 1)))
    plane = lane & 63
    for f in range(2 * depth):
        at = slice(f * rows, (f + 1) * rows)
        here = plane == f
        parts[at, 0:128] = jnp.where(here, both[0], 0.0).astype(jnp.bfloat16)
        parts[at, 128:256] = jnp.where(here, both[1], 0.0).astype(jnp.bfloat16)
    k = lax.broadcasted_iota(jnp.int32, (2 * cols, cols), 0)
    into = jnp.where(k < cols, last, 0) == lanes((2 * cols, cols))
    rims[...] = jnp.dot(parts[...], into.astype(F32).astype(jnp.bfloat16), preferred_element_type=F32)
    for l in range(depth):
        mask_e = face_e > l
        u_l = u_ref[l] * 0.5
        for c in range(2):
            f = c * depth + l
            at = slice(f * rows, (f + 1) * rows)
            t = t_ref[c, l]
            t_east = jnp.where(lane == last, rims[at], turn(t, -1, 1))
            flux_e = jnp.where(mask_e, u_l * (t + t_east), 0.0)
            net_x[at] = flux_e - jnp.where(lane == 0, rims[at], turn(flux_e, 1, 1))
    diff = diff_ref[...]
    above = jnp.zeros(shape, F32)
    inv = unit = None
    for l in range(depth):
        below = jnp.where(level > l + 1, diff, 0.0) if l < depth - 1 else jnp.zeros(shape, F32)
        pivot = 1.0 + above + below
        if l > 0:
            pivot = pivot - above * above * inv
        inv = 1.0 / pivot
        inv_ref[l] = inv
        inv_rows_ref[0, l : l + 1] = inv[rows - 1 : rows]
        inv_rows_ref[1, l : l + 1] = inv[0:1]
        gain_ref[l] = below * inv
        unit = inv if l == 0 else above * unit * inv
        unit_ref[l] = unit
        above = below
    for l in range(depth - 2, -1, -1):
        unit = unit_ref[l] + gain_ref[l] * unit
        unit_ref[l] = unit
    copy.wait()
    right = [None, None]
    for l in range(depth):
        above = jnp.where(level > l, diff, 0.0)
        inv = inv_ref[l]
        mask_n = face_n > l
        v_l = v_ref[l] * 0.5
        for c in range(2):
            f = c * depth + l
            t = t_ref[c, l]
            flux_n = jnp.where(mask_n, v_l * (t + turn(t, -1, 0)), 0.0)
            flux_s = turn(flux_n, 1, 0)
            forced = t - adv_rate * (net_x[f * rows : (f + 1) * rows] + (flux_n - flux_s))
            right[c] = forced * inv if l == 0 else (forced + above * right[c]) * inv
            x_ref[c, l] = right[c]
    for l in range(depth - 2, -1, -1):
        gain = gain_ref[l]
        for c in range(2):
            right[c] = x_ref[c, l] + gain * right[c]
            x_ref[c, l] = right[c]


def step_kernel(
    second_ref, first_ref, height_ref, transport_ref, level_ref, diff_ref, flux_ref, rim_ref, rows_ref, inv_rows_ref,
    x_ref, unit_ref, t_out, height_out, transport_out, north_ref, shift, fixed, result, sems,
):
    top = is_top()
    level = level_ref[...]
    level_f = level.astype(F32)
    rows, cols = level.shape
    depth = x_ref.shape[1]
    wet_0 = (level > 0).astype(F32)
    source = (heat_gain * flux_ref[0] * wet_0, -salt_gain * flux_ref[1] * wet_0)
    lo, hi = slice(0, HALO), slice(rows - HALO, rows)
    mid = slice(HALO, rows - HALO)
    copies = []

    def send(value, out):
        copies.append(pltpu.make_async_copy(value, out, sems.at[len(copies)]))
        copies[-1].start()

    for c in range(2):
        for l in range(depth):
            fixed[c, l, mid] = x_ref[c, l, mid] + unit_ref[l, mid] * source[c][mid]
        send(fixed.at[c, :, mid], t_out.at[c, :, mid])
    even = is_even("lat")
    a, b = first_ref[...], second_ref[...]
    south = jnp.where(even, b, a)
    north = jnp.where(even, a, b)
    mirrored = jnp.take_along_axis(north, 127 - lanes(north.shape), axis=1)
    north = jnp.where(top, mirrored, north)
    north_ref[...] = north

    first = LEVELS * HALO
    level_n = jnp.where(top, north[first + HALO - 1 : first + HALO], north[first : first + 1])
    level_s = south[first + HALO - 1 : first + HALO]
    sides = ((north, level_n, rows - 1, -adv_rate), (south, level_s, 0, adv_rate))
    chains = []
    for s, (message, level_out, at, gain) in enumerate(sides):
        level_in = level_f[at : at + 1]
        face = jnp.minimum(level_in, level_out)
        speed = rows_ref[0, 2 * depth :] if s == 0 else message[ROW_T + 2 * depth :]
        for c in range(2):
            planes = slice(c * depth, (c + 1) * depth)
            outside = message[ROW_T + c * depth : ROW_T + (c + 1) * depth]
            flux = speed * ((outside + rows_ref[s, planes]) * 0.5)
            deep = rows_of(flux.shape).astype(F32) < face
            shift[s, planes] = jnp.where(deep, gain * flux, 0.0)
            chains.append((s, c, level_in, diff_ref[at : at + 1]))
    right = [None] * 4
    for l in range(depth):
        for i, (s, c, level_in, diff_in) in enumerate(chains):
            at = c * depth + l
            inv = inv_rows_ref[s, l : l + 1]
            value = shift[s, at : at + 1]
            if l > 0:
                value = value + jnp.where(level_in > l, diff_in, 0.0) * right[i]
            right[i] = value * inv
            shift[s, at : at + 1] = right[i]
    for l in range(depth - 2, -1, -1):
        for i, (s, c, level_in, diff_in) in enumerate(chains):
            at = c * depth + l
            inv = inv_rows_ref[s, l : l + 1]
            below = jnp.where(level_in > l + 1, diff_in, 0.0) * inv
            right[i] = shift[s, at : at + 1] + below * right[i]
            shift[s, at : at + 1] = right[i]
    own = (
        height_ref[...], transport_ref[0], transport_ref[1], level_f,
        flux_ref[1], flux_ref[2], flux_ref[3],
    )
    ext = []
    lane = lanes((HALO, cols))
    side = (lane < HALO) | (lane >= cols - HALO)
    for i in range(FIELDS):
        at = slice(i * HALO, (i + 1) * HALO)
        whole = jnp.concatenate([south[at], own[i], north[at]], axis=0)
        start = jnp.where(top, cols - 2 * HALO * (FIELDS - i) - HALO, cols - 2 * HALO * i - HALO)
        north_rim = jnp.where(side, pltpu.roll(north[ROW_RIM:ROW_T], start, 1), 0.0)
        south_rim = jnp.where(side, turn(south[ROW_RIM:ROW_T], -(2 * HALO * i + HALO), 1), 0.0)
        rim = jnp.concatenate([south_rim, rim_ref[i], north_rim], axis=0)
        ext.append(jnp.concatenate([whole, rim], axis=1))


    def coefficients(f):
        wet = (f[LEVELS] > 0.0).astype(F32)
        return (
            wet,
            wave_grad * (f[LEVELS] / depth),
            fresh_gain * f[FRESH] * wet,
            wind_gain * f[WIND_E] * wet,
            wind_gain * f[WIND_N] * wet,
        )

    mine = [x for x in ext]
    fold = [x[HALO + rows :] for x in ext]
    wet, grad, fresh, wind_e, wind_n = coefficients(mine)
    p_wet, p_grad, p_fresh, p_wind_e, p_wind_n = coefficients(fold)
    h, e, n = mine[HEIGHT], mine[EAST], mine[NORTH]
    p_h, p_e, p_n = fold[HEIGHT], fold[EAST], fold[NORTH]
    row_h = rows_of(h.shape)
    last = HALO + rows - 1
    across = (row_h == last) & top
    p_last = rows_of(p_h.shape) == HALO - 1
    for step in range(SUBSTEPS):
        if step == 4:
            row = rows_of((HALO, cols))
            for s, cut, at_row in ((0, hi, HALO - 1), (1, lo, 0)):
                for c in range(2):
                    for l in range(depth):
                        at = c * depth + l
                        add = jnp.broadcast_to(shift[s, at : at + 1], (HALO, cols))
                        x = x_ref[c, l, cut] + unit_ref[l, cut] * source[c][cut]
                        fixed[c, l, cut] = x + jnp.where(row == at_row, add, 0.0)
                send(fixed.at[:, :, cut], t_out.at[:, :, cut])
        h = (h - wave_div * ((e - turn(e, 1, 1)) + (n - turn(n, 1, 0)))) * wet + fresh
        p_h = (p_h - wave_div * ((p_e - turn(p_e, -1, 1)) + (p_n - turn(p_n, 1, 0)))) * p_wet + p_fresh
        h_n = jnp.where(across, jnp.broadcast_to(p_h[HALO - 1 :], h.shape), turn(h, -1, 0))
        p_h_n = jnp.where(p_last, jnp.broadcast_to(h[last : last + 1], p_h.shape), turn(p_h, -1, 0))
        e = (e - grad * (turn(h, -1, 1) - h)) * wet + wind_e
        n = (n - grad * (h_n - h)) * wet + wind_n
        p_e = (p_e - p_grad * (turn(p_h, 1, 1) - p_h)) * p_wet + p_wind_e
        p_n = (p_n - p_grad * (p_h_n - p_h)) * p_wet + p_wind_n
    inside = slice(HALO, HALO + rows)
    result[0] = h[inside, :cols]
    result[1] = e[inside, :cols]
    result[2] = n[inside, :cols]
    send(result.at[0], height_out)
    send(result.at[1:3], transport_out)

    for copy in copies:
        copy.wait()


def vmem(count):
    return [pl.BlockSpec(memory_space=pltpu.VMEM)] * count


def params(mib=24):
    return pltpu.CompilerParams(vmem_limit_bytes=mib * 1024 * 1024)


def work(mb):
    return pl.CostEstimate(flops=mb * 1000000, bytes_accessed=mb * 1000000, transcendentals=0)


def in_hbm(x):
    return pltpu.with_memory_space_constraint(x, pltpu.HBM)


def shape_of(*shape):
    return jax.ShapeDtypeStruct(shape, F32)


def lat_pairs(n_lat, n_lon):
    def at(i, j):
        return i * n_lon + j

    first, second = [], []
    for j in range(n_lon):
        for i in range(0, n_lat, 2):
            first += [(at(i, j), at(i + 1, j)), (at(i + 1, j), at(i, j))]
        for i in range(1, n_lat - 1, 2):
            second += [(at(i, j), at(i + 1, j)), (at(i + 1, j), at(i, j))]
        second.append((at(n_lat - 1, j), at(n_lat - 1, n_lon - 1 - j)))
    return first, second


def lon_pairs(n_lon):
    first, second = [], []
    for j in range(0, n_lon, 2):
        first += [(j, j + 1), (j + 1, j)]
        k, m = j + 1, (j + 2) % n_lon
        second += [(k, m), (m, k)]
    return first, second


def per_device(
    tracers,
    velocity,
    diffusivity,
    ocean_levels,
    surface_height,
    transport,
    atm_flux,
    send_rows,
    src_owner,
    src_slot,
    xgrid_weights,
    xgrid_count,
):
    n_lat, n_lon = lax.axis_size("lat"), lax.axis_size("lon")
    depth, rows, cols = tracers.shape[1:]
    slots = send_rows.shape[3]
    block = (rows, cols)
    picked, t_near, u_near = pl.pallas_call(
        pick_kernel,
        out_shape=(
            shape_of(n_lon, 1, 10 * slots),
            shape_of(2, depth, *block),
            shape_of(depth, *block),
        ),
        in_specs=[pl.BlockSpec(memory_space=pltpu.HBM)] * 4,
        out_specs=vmem(3),
        scratch_shapes=[
            pltpu.VMEM(atm_flux.shape, F32),
            pltpu.VMEM(send_rows.shape, jnp.int32),
            pltpu.SemaphoreType.DMA((4,)),
        ],
        compiler_params=params(24),
        cost_estimate=work(40),
        name="pick",
    )(in_hbm(atm_flux), in_hbm(send_rows), in_hbm(tracers), in_hbm(velocity))
    table = lax.all_to_all(picked, "lon", split_axis=0, concat_axis=0, tiled=True)

    lat_rows = ROW_T + 3 * depth
    two, one, t_0, edge_rows, pick_row, pick_lane, used = pl.pallas_call(
        edge_kernel,
        out_shape=(
            shape_of(2 * rows, cols),
            shape_of(2 * rows, cols),
            shape_of(*block),
            shape_of(2, 3 * depth, cols),
            jax.ShapeDtypeStruct((4, *block), jnp.int32),
            jax.ShapeDtypeStruct((4, *block), jnp.int32),
            shape_of(4, *block),
        ),
        in_specs=[pl.BlockSpec(memory_space=pl.ANY), pl.BlockSpec(memory_space=pltpu.HBM)] + vmem(9),
        out_specs=vmem(7),
        scratch_shapes=[pltpu.VMEM((depth, HALO, cols), F32), pltpu.SemaphoreType.DMA],
        compiler_params=params(),
        cost_estimate=work(2),
        name="edges",
    )(
        picked, in_hbm(velocity), t_near, u_near, ocean_levels, surface_height, transport, src_owner, src_slot,
        xgrid_weights, xgrid_count,
    )
    pairs = lon_pairs(n_lon)
    two = lax.ppermute(two, "lon", pairs[1])
    one = lax.ppermute(one, "lon", pairs[0])

    solved, unit, inv_rows = pl.pallas_call(
        tracer_kernel,
        out_shape=(shape_of(2, depth, *block), shape_of(depth, *block), shape_of(2, depth, cols)),
        in_specs=vmem(7) + [pl.BlockSpec(memory_space=pltpu.HBM)],
        out_specs=vmem(3),
        scratch_shapes=[
            pltpu.VMEM((depth, *block), F32),
            pltpu.VMEM((2 * depth * rows, 2 * cols), jnp.bfloat16),
            pltpu.VMEM((2 * depth * rows, cols), F32),
            pltpu.VMEM((2 * depth * rows, cols), F32),
            pltpu.VMEM((depth, *block), F32),
            pltpu.VMEM((depth, *block), F32),
            pltpu.SemaphoreType.DMA,
        ],
        compiler_params=params(),
        cost_estimate=work(8),
        name="tracers",
    )(two, one, t_0, ocean_levels, diffusivity, t_near, u_near, in_hbm(velocity))

    second, first, edge_flux, edge_rim, tab, side = pl.pallas_call(
        rim_lookup_kernel,
        out_shape=(
            shape_of(lat_rows, cols),
            shape_of(lat_rows, cols),
            shape_of(2, 3, HALO, cols),
            shape_of(2, 3, HALO, cols),
            shape_of(4, n_lon // 2, 128),
            shape_of(3, n_lon, 128),
        ),
        in_specs=vmem(10),
        out_specs=vmem(6),
        scratch_shapes=[pltpu.VMEM((2, lat_rows, cols), F32)],
        compiler_params=params(),
        cost_estimate=work(8),
        name="rim_lookup",
    )(
        table, two, one, pick_row, pick_lane, used, edge_rows, ocean_levels, surface_height, transport,
    )
    pairs = lat_pairs(n_lat, n_lon)
    second = lax.ppermute(second, ("lat", "lon"), pairs[1])
    first = lax.ppermute(first, ("lat", "lon"), pairs[0])

    flux, rim = pl.pallas_call(
        lookup_kernel,
        out_shape=(shape_of(4, *block), shape_of(FIELDS, *block)),
        in_specs=vmem(9),
        out_specs=vmem(2),
        compiler_params=params(),
        cost_estimate=work(8),
        name="lookup",
    )(edge_flux, edge_rim, tab, side, two, one, pick_row, pick_lane, used)

    return pl.pallas_call(
        step_kernel,
        out_shape=(shape_of(2, depth, rows, cols), shape_of(rows, cols), shape_of(2, rows, cols)),
        in_specs=vmem(12),
        out_specs=(pl.BlockSpec(memory_space=pl.ANY),) * 3,
        scratch_shapes=[
            pltpu.VMEM((lat_rows, cols), F32),
            pltpu.VMEM((2, 2 * depth, cols), F32),
            pltpu.VMEM((2, depth, rows, cols), F32),
            pltpu.VMEM((3, rows, cols), F32),
            pltpu.SemaphoreType.DMA((6,)),
        ],
        compiler_params=params(),
        name="step",
    )(
        second, first, surface_height, transport, ocean_levels, diffusivity, flux, rim, edge_rows, inv_rows,
        solved, unit,
    )


def solution(mesh):
    return jax.shard_map(
        per_device,
        mesh=mesh,
        in_specs=(
            P(None, None, "lat", "lon"),
            P(None, None, "lat", "lon"),
            P("lat", "lon"),
            P("lat", "lon"),
            P("lat", "lon"),
            P(None, "lat", "lon"),
            P("lat", None, "lon"),
            P("lat", "lon", None, None),
            P(None, "lat", "lon"),
            P(None, "lat", "lon"),
            P(None, "lat", "lon"),
            P("lat", "lon"),
        ),
        out_specs=(P(None, None, "lat", "lon"), P("lat", "lon"), P(None, "lat", "lon")),
        check_vma=False,
    )
```

```python
import jax
import jax.numpy as jnp
from jax import lax
from jax.experimental import pallas as pl
from jax.experimental.pallas import tpu as pltpu
from jax.sharding import PartitionSpec as P

SUBSTEPS = 6
HALO = 8
FIELDS = 7
HEIGHT, EAST, NORTH, LEVELS, FRESH, WIND_E, WIND_N = range(FIELDS)
ROW_RIM = FIELDS * HALO
ROW_T = ROW_RIM + HALO
LISTS = 256
OWNER, SLOT, USED = 32, 64, 96

adv_rate = 0.1
heat_gain = 0.5
salt_gain = 0.5
wave_div = 0.5
wave_grad = 0.8
fresh_gain = 0.2
wind_gain = 0.2

F32 = jnp.float32


def lanes(shape):
    return lax.broadcasted_iota(jnp.int32, shape, len(shape) - 1)


def rows_of(shape):
    return lax.broadcasted_iota(jnp.int32, shape, len(shape) - 2)


def turn(x, by, axis):
    size = x.shape[axis]
    by = by % size
    return x if by == 0 else pltpu.roll(x, by, axis)


def is_even(axis):
    return lax.rem(lax.axis_index(axis), 2) == 0


def is_top():
    return lax.axis_index("lat") == lax.axis_size("lat") - 1


def pick_kernel(
    atm_hbm, rows_hbm, t_hbm, v_hbm, out_hbm, t_ref, u_ref, v_rows, atm_ref, rows_ref, out_ref, sems,
):
    last = t_ref.shape[2] - HALO
    copies = [
        pltpu.make_async_copy(atm_hbm, atm_ref, sems.at[0]),
        pltpu.make_async_copy(rows_hbm, rows_ref, sems.at[1]),
        pltpu.make_async_copy(t_hbm, t_ref, sems.at[2]),
        pltpu.make_async_copy(v_hbm.at[0], u_ref, sems.at[3]),
        pltpu.make_async_copy(v_hbm.at[1, :, last:], v_rows, sems.at[4]),
    ]
    for copy in copies:
        copy.start()
    for copy in copies[:2]:
        copy.wait()
    rows = rows_ref[0, 0]
    both = jnp.concatenate([rows, rows], axis=1)
    lane = both & 127
    part = both >> 7
    low = lanes(both.shape) < 64
    values = []
    for f in range(4):
        acc = None
        for k in range(atm_ref.shape[2] // 128):
            row = jnp.broadcast_to(atm_ref[0, f : f + 1, k * 128 : (k + 1) * 128], both.shape)
            value = jnp.take_along_axis(row, lane, axis=1)
            acc = value if k == 0 else jnp.where(part == k, value, acc)
        values.append(acc)
    out_ref[:, 0, 0:128] = jnp.where(low, values[0], values[1])
    out_ref[:, 0, 128:256] = jnp.where(low, values[2], values[3])
    for f in range(1, 4):
        at = 128 + f * 128
        out_ref[:, 0, at : at + 128] = jnp.where(low, turn(values[f], -1, 0), turn(values[f], 1, 0))
    copies.append(pltpu.make_async_copy(out_ref, out_hbm, sems.at[5]))
    copies[-1].start()
    for copy in copies[2:]:
        copy.wait()


def edge_kernel(
    picked_ref, v_rows, t_ref, u_ref, level_ref, height_ref, transport_ref, owner_ref, slot_ref, weight_ref, count_ref,
    two_ref, one_ref, t_0_ref, rows_ref, pick_row_ref, pick_lane_ref, used_ref,
):
    depth, rows, cols = t_ref.shape[1:]
    shape = (rows, cols)
    lane = lanes(shape)
    level = level_ref[...]
    half = lax.axis_size("lon") // 2
    count = count_ref[...]
    for k in range(owner_ref.shape[0]):
        owner = owner_ref[k]
        high = owner >= half
        pick_row_ref[k] = jnp.where(high, owner - half, owner)
        pick_lane_ref[k] = jnp.where(high, slot_ref[k] + 64, slot_ref[k])
        used_ref[k] = jnp.where(count > k, weight_ref[k], 0.0)
    fields = [height_ref[...], transport_ref[0], transport_ref[1], level.astype(F32)]
    fields += [owner_ref[k].astype(F32) for k in range(4)]
    fields += [slot_ref[k].astype(F32) for k in range(4)]
    fields += [used_ref[k] for k in range(4)]
    west = jnp.zeros(shape, F32)
    east = jnp.zeros(shape, F32)
    for g, field in enumerate(fields):
        here = (lane >= g * HALO) & (lane < (g + 1) * HALO)
        west = jnp.where(here, turn(field, g * HALO, 1), west)
        east = jnp.where(here, turn(field, (g + 1) * HALO, 1), east)
    west_t = jnp.zeros(shape, F32)
    east_t = jnp.zeros(shape, F32)
    for c in range(2):
        for l in range(depth):
            f = c * depth + l
            moved = turn(t_ref[c, l], f + 1, 1)
            west_t = jnp.where(lane == f + 1, moved, west_t)
            east_t = jnp.where(lane == f, moved, east_t)
    for l in range(depth):
        at = 2 * depth + l
        east_t = jnp.where(lane == at, turn(u_ref[l], at + 1, 1), east_t)
    even = is_even("lon")
    one_ref[:rows] = jnp.where(even, east, west)
    two_ref[:rows] = jnp.where(even, west, east)
    one_ref[rows:] = jnp.where(even, east_t, west_t)
    two_ref[rows:] = jnp.where(even, west_t, east_t)
    t_0_ref[...] = turn(west_t, -1, 1)
    for c in range(2):
        for l in range(depth):
            at = c * depth + l
            rows_ref[0, at : at + 1] = t_ref[c, l, rows - 1 : rows]
            rows_ref[1, at : at + 1] = t_ref[c, l, 0:1]
    for l in range(depth):
        at = 2 * depth + l
        rows_ref[0, at : at + 1] = v_rows[l, HALO - 1 : HALO]
    rows_ref[1, 2 * depth :] = jnp.zeros((depth, cols), F32)

def own_lookup(tab, row_ref, lane_ref, used_ref, cut, fields):
    total = {f: None for f in fields}
    for k in range(used_ref.shape[0]):
        lane = lane_ref[k, cut]
        row = row_ref[k, cut]
        acc = {}
        for r in range(tab.shape[1]):
            here = row == r
            for f in fields:
                source = jnp.broadcast_to(tab[f, r : r + 1, :], lane.shape)
                value = jnp.take_along_axis(source, lane, axis=1)
                acc[f] = value if r == 0 else jnp.where(here, value, acc[f])
        used = used_ref[k, cut]
        for f in fields:
            total[f] = acc[f] * used if k == 0 else total[f] + acc[f] * used
    return total


def rim_of(east, west, by_east, by_west):
    lane = lanes(east.shape)
    outer = jnp.where(lane >= 128 - HALO, turn(west, by_west, 1), 0.0)
    return jnp.where(lane < HALO, turn(east, by_east, 1), outer)


def from_lon(one_ref, two_ref, cut):
    even = is_even("lon")
    one, two = one_ref[cut], two_ref[cut]
    return jnp.where(even, one, two), jnp.where(even, two, one)


def state_rims(east, west):
    return [rim_of(east, west, -g * HALO, 128 - (g + 1) * HALO) for g in range(4)]


def side_lookup(side, sides):
    (east, west), (east_2, west_2) = sides
    lane = lanes(east.shape)
    quarter = lane >> 5

    def gathered(by):
        parts = (turn(west_2, -32 - by, 1), turn(east, -by, 1), turn(west, 32 - by, 1), turn(east_2, 64 - by, 1))
        low = jnp.where(quarter == 0, parts[0], parts[1])
        return jnp.where(quarter < 2, low, jnp.where(quarter == 2, parts[2], parts[3]))

    owner = gathered(0).astype(jnp.int32)
    slot = gathered(32).astype(jnp.int32)
    used = gathered(64)
    slot = jnp.where((quarter & 1) == 0, slot + 64, slot)
    acc = [None] * 3
    for r in range(side.shape[1]):
        here = owner == r
        for f in range(3):
            source = jnp.broadcast_to(side[f, r : r + 1, :], slot.shape)
            value = jnp.take_along_axis(source, slot, axis=1)
            acc[f] = value if r == 0 else jnp.where(here, value, acc[f])
    rims = ([], [])
    for f in range(3):
        v = acc[f] * used
        v = v + turn(v, -16, 1)
        v = v + turn(v, -8, 1)
        rims[0].append(rim_of(v, v, -32, 56))
        rims[1].append(rim_of(v, v, -96, 120))
    return rims


def rim_lookup_kernel(
    table_ref, two_ref, one_ref, pick_row_ref, pick_lane_ref, used_ref, rows_ref, level_ref, height_ref,
    transport_ref, second_ref, first_ref, flux_ref, rim_ref, tab, side, pack,
):
    n_lon = table_ref.shape[0]
    half = n_lon // 2
    rows, cols = height_ref.shape
    low = lanes((half, 128)) < 64
    for pair in range(2):
        part = table_ref[:, 0, pair * 128 : (pair + 1) * 128]
        lo, hi = part[:half], part[half:]
        tab[2 * pair] = jnp.where(low, lo, turn(hi, 64, 1))
        tab[2 * pair + 1] = jnp.where(low, turn(lo, 64, 1), hi)
    for f in range(3):
        side[f] = table_ref[:, 0, LISTS + f * 128 : LISTS + (f + 1) * 128]
    lane = lanes((HALO, cols))
    cuts = (slice(rows - HALO, rows), slice(0, HALO))
    sides = [from_lon(one_ref, two_ref, cut) for cut in cuts]
    side_rims = side_lookup(side, sides)
    for s, cut in enumerate(cuts):
        found = own_lookup(tab, pick_row_ref, pick_lane_ref, used_ref, cut, (1, 2, 3))
        for f in range(3):
            flux_ref[s, f] = found[f + 1]
            rim_ref[s, f] = side_rims[s][f]
        rims = state_rims(*sides[s]) + side_rims[s]
        own = [
            height_ref[cut], transport_ref[0, cut], transport_ref[1, cut], level_ref[cut].astype(F32),
            found[1], found[2], found[3],
        ]
        packed = jnp.zeros((HALO, cols), F32)
        for i in range(FIELDS):
            pack[s, i * HALO : (i + 1) * HALO] = own[i]
            start = 2 * HALO * i
            here = (lane >= start) & (lane < start + 2 * HALO)
            packed = jnp.where(here, turn(rims[i], start + HALO, 1), packed)
        pack[s, ROW_RIM:ROW_T] = packed
        pack[s, ROW_T:] = rows_ref[s]
    even = is_even("lat")
    north_going, south_going = pack[0], pack[1]
    second_ref[...] = jnp.where(even, south_going, north_going)
    first_ref[...] = jnp.where(even, north_going, south_going)


def lookup_kernel(
    edge_flux_ref, edge_rim_ref, tab, side, two_ref, one_ref, pick_row_ref, pick_lane_ref, used_ref,
    flux_ref, rim_ref,
):
    rows = used_ref.shape[1]
    cuts = [slice(at, at + HALO) for at in range(0, rows, HALO)]
    sides = [from_lon(one_ref, two_ref, cut) for cut in cuts]
    for at in range(1, len(cuts) - 1, 2):
        side_rims = side_lookup(side, sides[at : at + 2])
        for i in range(2):
            cut = cuts[at + i]
            found = own_lookup(tab, pick_row_ref, pick_lane_ref, used_ref, cut, (0, 1, 2, 3))
            for f in range(4):
                flux_ref[f, cut] = found[f]
            for g, rim in enumerate(state_rims(*sides[at + i]) + side_rims[i]):
                rim_ref[g, cut] = rim
    for s, at in ((0, len(cuts) - 1), (1, 0)):
        cut = cuts[at]
        flux_ref[0, cut] = own_lookup(tab, pick_row_ref, pick_lane_ref, used_ref, cut, (0,))[0]
        for f in range(3):
            flux_ref[f + 1, cut] = edge_flux_ref[s, f]
        for g, rim in enumerate(state_rims(*sides[at]) + [edge_rim_ref[s, f] for f in range(3)]):
            rim_ref[g, cut] = rim


def split(x):
    hi = x.astype(jnp.bfloat16)
    return hi, (x - hi.astype(F32)).astype(jnp.bfloat16)


def tracer_kernel(
    two_ref, one_ref, t_0_ref, level_ref, diff_ref, t_ref, u_ref, v_hbm, x_ref, unit_ref, inv_rows_ref, gain_ref,
    parts, rims, net_x, v_ref, sem,
):
    depth, rows, cols = t_ref.shape[1:]
    copy = pltpu.make_async_copy(v_hbm.at[1], v_ref, sem)
    copy.start()
    shape = (rows, cols)
    east, west = from_lon(one_ref, two_ref, slice(0, rows))
    t_e, t_w = from_lon(one_ref, two_ref, slice(rows, 2 * rows))
    level = level_ref[...]
    level_f = level.astype(F32)
    lane = lanes(shape)
    row = rows_of(shape)
    first = LEVELS * HALO
    last = cols - 1
    level_e = jnp.where(lane == last, turn(east, last - first, 1), turn(level_f, -1, 1))
    level_n = turn(level_f, -1, 0)
    face_e = jnp.minimum(level_f, level_e)
    face_n = jnp.where(row == rows - 1, 0.0, jnp.minimum(level_f, level_n))
    t_0 = t_0_ref[...]
    u_w = jnp.where(lane < depth, turn(t_w, -2 * depth, 1), turn(t_w, -depth, 1))
    layer = jnp.where(lane < depth, lane, lane - depth).astype(F32)
    level_w = west[:, first + HALO - 1 : first + HALO]
    face_w = jnp.broadcast_to(jnp.minimum(level_f[:, 0:1], level_w), shape)
    west_flux = jnp.where((layer < face_w) & (lane < 2 * depth), u_w * ((t_w + t_0) * 0.5), 0.0)
    both = []
    for x in (turn(t_e, -1, 1), west_flux):
        hi, lo = split(x)
        both.append(jnp.where(lane < 64, hi.astype(F32), turn(lo.astype(F32), 64, 1)))
    plane = lane & 63
    for f in range(2 * depth):
        at = slice(f * rows, (f + 1) * rows)
        here = plane == f
        parts[at, 0:128] = jnp.where(here, both[0], 0.0).astype(jnp.bfloat16)
        parts[at, 128:256] = jnp.where(here, both[1], 0.0).astype(jnp.bfloat16)
    k = lax.broadcasted_iota(jnp.int32, (2 * cols, cols), 0)
    into = jnp.where(k < cols, last, 0) == lanes((2 * cols, cols))
    rims[...] = jnp.dot(parts[...], into.astype(F32).astype(jnp.bfloat16), preferred_element_type=F32)
    for l in range(depth):
        mask_e = face_e > l
        u_l = u_ref[l] * 0.5
        for c in range(2):
            f = c * depth + l
            at = slice(f * rows, (f + 1) * rows)
            t = t_ref[c, l]
            t_east = jnp.where(lane == last, rims[at], turn(t, -1, 1))
            flux_e = jnp.where(mask_e, u_l * (t + t_east), 0.0)
            net_x[at] = flux_e - jnp.where(lane == 0, rims[at], turn(flux_e, 1, 1))
    copy.wait()
    diff = diff_ref[...]
    above = jnp.zeros(shape, F32)
    inv = None
    right = [None, None, None]
    for l in range(depth):
        below = jnp.where(level > l + 1, diff, 0.0) if l < depth - 1 else jnp.zeros(shape, F32)
        pivot = 1.0 + above + below
        if l > 0:
            pivot = pivot - above * above * inv
        inv = 1.0 / pivot
        inv_rows_ref[0, l : l + 1] = inv[rows - 1 : rows]
        inv_rows_ref[1, l : l + 1] = inv[0:1]
        gain_ref[l] = below * inv
        mask_n = face_n > l
        v_l = v_ref[l] * 0.5
        for c in range(2):
            f = c * depth + l
            at = slice(f * rows, (f + 1) * rows)
            t = t_ref[c, l]
            flux_n = jnp.where(mask_n, v_l * (t + turn(t, -1, 0)), 0.0)
            flux_s = turn(flux_n, 1, 0)
            forced = t - adv_rate * (net_x[at] + (flux_n - flux_s))
            right[c] = forced * inv if l == 0 else (forced + above * right[c]) * inv
            x_ref[c, l] = right[c]
        right[2] = inv if l == 0 else above * right[2] * inv
        unit_ref[l] = right[2]
        above = below
    for l in range(depth - 2, -1, -1):
        gain = gain_ref[l]
        for c in range(2):
            right[c] = x_ref[c, l] + gain * right[c]
            x_ref[c, l] = right[c]
        right[2] = unit_ref[l] + gain * right[2]
        unit_ref[l] = right[2]


def step_kernel(
    second_ref, first_ref, height_ref, transport_ref, level_ref, diff_ref, flux_ref, rim_ref, rows_ref, inv_rows_ref,
    x_ref, unit_ref, t_out, height_out, transport_out, north_ref, shift, fixed, result, sems,
):
    top = is_top()
    level = level_ref[...]
    level_f = level.astype(F32)
    rows, cols = level.shape
    depth = x_ref.shape[1]
    wet_0 = (level > 0).astype(F32)
    source = (heat_gain * flux_ref[0] * wet_0, -salt_gain * flux_ref[1] * wet_0)
    lo, hi = slice(0, HALO), slice(rows - HALO, rows)
    mid = slice(HALO, rows - HALO)
    copies = []

    def send(value, out):
        copies.append(pltpu.make_async_copy(value, out, sems.at[len(copies)]))
        copies[-1].start()

    for c in range(2):
        for l in range(depth):
            fixed[c, l, mid] = x_ref[c, l, mid] + unit_ref[l, mid] * source[c][mid]
        send(fixed.at[c, :, mid], t_out.at[c, :, mid])
    even = is_even("lat")
    a, b = first_ref[...], second_ref[...]
    south = jnp.where(even, b, a)
    north = jnp.where(even, a, b)
    mirrored = jnp.take_along_axis(north, 127 - lanes(north.shape), axis=1)
    north = jnp.where(top, mirrored, north)
    north_ref[...] = north

    first = LEVELS * HALO
    level_n = jnp.where(top, north[first + HALO - 1 : first + HALO], north[first : first + 1])
    level_s = south[first + HALO - 1 : first + HALO]
    sides = ((north, level_n, rows - 1, -adv_rate), (south, level_s, 0, adv_rate))
    chains = []
    for s, (message, level_out, at, gain) in enumerate(sides):
        level_in = level_f[at : at + 1]
        face = jnp.minimum(level_in, level_out)
        speed = rows_ref[0, 2 * depth :] if s == 0 else message[ROW_T + 2 * depth :]
        for c in range(2):
            planes = slice(c * depth, (c + 1) * depth)
            outside = message[ROW_T + c * depth : ROW_T + (c + 1) * depth]
            flux = speed * ((outside + rows_ref[s, planes]) * 0.5)
            deep = rows_of(flux.shape).astype(F32) < face
            shift[s, planes] = jnp.where(deep, gain * flux, 0.0)
            chains.append((s, c, level_in, diff_ref[at : at + 1]))
    right = [None] * 4
    for l in range(depth):
        for i, (s, c, level_in, diff_in) in enumerate(chains):
            at = c * depth + l
            inv = inv_rows_ref[s, l : l + 1]
            value = shift[s, at : at + 1]
            if l > 0:
                value = value + jnp.where(level_in > l, diff_in, 0.0) * right[i]
            right[i] = value * inv
            shift[s, at : at + 1] = right[i]
    for l in range(depth - 2, -1, -1):
        for i, (s, c, level_in, diff_in) in enumerate(chains):
            at = c * depth + l
            inv = inv_rows_ref[s, l : l + 1]
            below = jnp.where(level_in > l + 1, diff_in, 0.0) * inv
            right[i] = shift[s, at : at + 1] + below * right[i]
            shift[s, at : at + 1] = right[i]
    own = (
        height_ref[...], transport_ref[0], transport_ref[1], level_f,
        flux_ref[1], flux_ref[2], flux_ref[3],
    )
    ext = []
    lane = lanes((HALO, cols))
    side = (lane < HALO) | (lane >= cols - HALO)
    for i in range(FIELDS):
        at = slice(i * HALO, (i + 1) * HALO)
        whole = jnp.concatenate([south[at], own[i], north[at]], axis=0)
        start = jnp.where(top, cols - 2 * HALO * (FIELDS - i) - HALO, cols - 2 * HALO * i - HALO)
        north_rim = jnp.where(side, pltpu.roll(north[ROW_RIM:ROW_T], start, 1), 0.0)
        south_rim = jnp.where(side, turn(south[ROW_RIM:ROW_T], -(2 * HALO * i + HALO), 1), 0.0)
        rim = jnp.concatenate([south_rim, rim_ref[i], north_rim], axis=0)
        ext.append(jnp.concatenate([whole, rim], axis=1))


    def coefficients(f):
        wet = (f[LEVELS] > 0.0).astype(F32)
        return (
            wet,
            wave_grad * (f[LEVELS] / depth),
            fresh_gain * f[FRESH] * wet,
            wind_gain * f[WIND_E] * wet,
            wind_gain * f[WIND_N] * wet,
        )

    mine = [x for x in ext]
    fold = [x[HALO + rows :] for x in ext]
    wet, grad, fresh, wind_e, wind_n = coefficients(mine)
    p_wet, p_grad, p_fresh, p_wind_e, p_wind_n = coefficients(fold)
    h, e, n = mine[HEIGHT], mine[EAST], mine[NORTH]
    p_h, p_e, p_n = fold[HEIGHT], fold[EAST], fold[NORTH]
    row_h = rows_of(h.shape)
    last = HALO + rows - 1
    across = (row_h == last) & top
    p_last = rows_of(p_h.shape) == HALO - 1
    for step in range(SUBSTEPS):
        if step == 4:
            row = rows_of((HALO, cols))
            for s, cut, at_row in ((0, hi, HALO - 1), (1, lo, 0)):
                for c in range(2):
                    for l in range(depth):
                        at = c * depth + l
                        add = jnp.broadcast_to(shift[s, at : at + 1], (HALO, cols))
                        x = x_ref[c, l, cut] + unit_ref[l, cut] * source[c][cut]
                        fixed[c, l, cut] = x + jnp.where(row == at_row, add, 0.0)
                send(fixed.at[:, :, cut], t_out.at[:, :, cut])
        h = (h - wave_div * ((e - turn(e, 1, 1)) + (n - turn(n, 1, 0)))) * wet + fresh
        p_h = (p_h - wave_div * ((p_e - turn(p_e, -1, 1)) + (p_n - turn(p_n, 1, 0)))) * p_wet + p_fresh
        h_n = jnp.where(across, jnp.broadcast_to(p_h[HALO - 1 :], h.shape), turn(h, -1, 0))
        p_h_n = jnp.where(p_last, jnp.broadcast_to(h[last : last + 1], p_h.shape), turn(p_h, -1, 0))
        e = (e - grad * (turn(h, -1, 1) - h)) * wet + wind_e
        n = (n - grad * (h_n - h)) * wet + wind_n
        p_e = (p_e - p_grad * (turn(p_h, 1, 1) - p_h)) * p_wet + p_wind_e
        p_n = (p_n - p_grad * (p_h_n - p_h)) * p_wet + p_wind_n
    inside = slice(HALO, HALO + rows)
    result[0] = h[inside, :cols]
    result[1] = e[inside, :cols]
    result[2] = n[inside, :cols]
    send(result.at[0], height_out)
    send(result.at[1:3], transport_out)

    for copy in copies:
        copy.wait()


def vmem(count):
    return [pl.BlockSpec(memory_space=pltpu.VMEM)] * count


def params(mib=24):
    return pltpu.CompilerParams(vmem_limit_bytes=mib * 1024 * 1024)


def work(mb):
    return pl.CostEstimate(flops=mb * 1000000, bytes_accessed=mb * 1000000, transcendentals=0)


def in_hbm(x):
    return pltpu.with_memory_space_constraint(x, pltpu.HBM)


def shape_of(*shape):
    return jax.ShapeDtypeStruct(shape, F32)


def lat_pairs(n_lat, n_lon):
    def at(i, j):
        return i * n_lon + j

    first, second = [], []
    for j in range(n_lon):
        for i in range(0, n_lat, 2):
            first += [(at(i, j), at(i + 1, j)), (at(i + 1, j), at(i, j))]
        for i in range(1, n_lat - 1, 2):
            second += [(at(i, j), at(i + 1, j)), (at(i + 1, j), at(i, j))]
        second.append((at(n_lat - 1, j), at(n_lat - 1, n_lon - 1 - j)))
    return first, second


def lon_pairs(n_lon):
    first, second = [], []
    for j in range(0, n_lon, 2):
        first += [(j, j + 1), (j + 1, j)]
        k, m = j + 1, (j + 2) % n_lon
        second += [(k, m), (m, k)]
    return first, second


def per_device(
    tracers,
    velocity,
    diffusivity,
    ocean_levels,
    surface_height,
    transport,
    atm_flux,
    send_rows,
    src_owner,
    src_slot,
    xgrid_weights,
    xgrid_count,
):
    n_lat, n_lon = lax.axis_size("lat"), lax.axis_size("lon")
    depth, rows, cols = tracers.shape[1:]
    slots = send_rows.shape[3]
    block = (rows, cols)
    picked, t_near, u_near, v_rows = pl.pallas_call(
        pick_kernel,
        out_shape=(
            shape_of(n_lon, 1, 10 * slots),
            shape_of(2, depth, *block),
            shape_of(depth, *block),
            shape_of(depth, HALO, cols),
        ),
        in_specs=[pl.BlockSpec(memory_space=pltpu.HBM)] * 4,
        out_specs=[pl.BlockSpec(memory_space=pltpu.HBM)] + vmem(3),
        scratch_shapes=[
            pltpu.VMEM(atm_flux.shape, F32),
            pltpu.VMEM(send_rows.shape, jnp.int32),
            pltpu.VMEM((n_lon, 1, 10 * slots), F32),
            pltpu.SemaphoreType.DMA((6,)),
        ],
        compiler_params=params(24),
        cost_estimate=work(40),
        name="pick",
    )(in_hbm(atm_flux), in_hbm(send_rows), in_hbm(tracers), in_hbm(velocity))
    table = lax.all_to_all(picked, "lon", split_axis=0, concat_axis=0, tiled=True)

    lat_rows = ROW_T + 3 * depth
    two, one, t_0, edge_rows, pick_row, pick_lane, used = pl.pallas_call(
        edge_kernel,
        out_shape=(
            shape_of(2 * rows, cols),
            shape_of(2 * rows, cols),
            shape_of(*block),
            shape_of(2, 3 * depth, cols),
            jax.ShapeDtypeStruct((4, *block), jnp.int32),
            jax.ShapeDtypeStruct((4, *block), jnp.int32),
            shape_of(4, *block),
        ),
        in_specs=[pl.BlockSpec(memory_space=pl.ANY)] + vmem(10),
        out_specs=vmem(7),
        compiler_params=params(),
        cost_estimate=work(2),
        name="edges",
    )(
        picked, v_rows, t_near, u_near, ocean_levels, surface_height, transport, src_owner, src_slot,
        xgrid_weights, xgrid_count,
    )
    pairs = lon_pairs(n_lon)
    two = lax.ppermute(two, "lon", pairs[1])
    one = lax.ppermute(one, "lon", pairs[0])

    solved, unit, inv_rows = pl.pallas_call(
        tracer_kernel,
        out_shape=(shape_of(2, depth, *block), shape_of(depth, *block), shape_of(2, depth, cols)),
        in_specs=vmem(7) + [pl.BlockSpec(memory_space=pltpu.HBM)],
        out_specs=vmem(3),
        scratch_shapes=[
            pltpu.VMEM((depth, *block), F32),
            pltpu.VMEM((2 * depth * rows, 2 * cols), jnp.bfloat16),
            pltpu.VMEM((2 * depth * rows, cols), F32),
            pltpu.VMEM((2 * depth * rows, cols), F32),
            pltpu.VMEM((depth, *block), F32),
            pltpu.SemaphoreType.DMA,
        ],
        compiler_params=params(),
        cost_estimate=work(8),
        name="tracers",
    )(two, one, t_0, ocean_levels, diffusivity, t_near, u_near, in_hbm(velocity))

    second, first, edge_flux, edge_rim, tab, side = pl.pallas_call(
        rim_lookup_kernel,
        out_shape=(
            shape_of(lat_rows, cols),
            shape_of(lat_rows, cols),
            shape_of(2, 3, HALO, cols),
            shape_of(2, 3, HALO, cols),
            shape_of(4, n_lon // 2, 128),
            shape_of(3, n_lon, 128),
        ),
        in_specs=vmem(10),
        out_specs=vmem(6),
        scratch_shapes=[pltpu.VMEM((2, lat_rows, cols), F32)],
        compiler_params=params(),
        cost_estimate=work(8),
        name="rim_lookup",
    )(
        table, two, one, pick_row, pick_lane, used, edge_rows, ocean_levels, surface_height, transport,
    )
    pairs = lat_pairs(n_lat, n_lon)
    second = lax.ppermute(second, ("lat", "lon"), pairs[1])
    first = lax.ppermute(first, ("lat", "lon"), pairs[0])

    flux, rim = pl.pallas_call(
        lookup_kernel,
        out_shape=(shape_of(4, *block), shape_of(FIELDS, *block)),
        in_specs=vmem(9),
        out_specs=vmem(2),
        compiler_params=params(),
        cost_estimate=work(8),
        name="lookup",
    )(edge_flux, edge_rim, tab, side, two, one, pick_row, pick_lane, used)

    return pl.pallas_call(
        step_kernel,
        out_shape=(shape_of(2, depth, rows, cols), shape_of(rows, cols), shape_of(2, rows, cols)),
        in_specs=vmem(12),
        out_specs=(pl.BlockSpec(memory_space=pl.ANY),) * 3,
        scratch_shapes=[
            pltpu.VMEM((lat_rows, cols), F32),
            pltpu.VMEM((2, 2 * depth, cols), F32),
            pltpu.VMEM((2, depth, rows, cols), F32),
            pltpu.VMEM((3, rows, cols), F32),
            pltpu.SemaphoreType.DMA((6,)),
        ],
        compiler_params=params(),
        name="step",
    )(
        second, first, surface_height, transport, ocean_levels, diffusivity, flux, rim, edge_rows, inv_rows,
        solved, unit,
    )


def solution(mesh):
    return jax.shard_map(
        per_device,
        mesh=mesh,
        in_specs=(
            P(None, None, "lat", "lon"),
            P(None, None, "lat", "lon"),
            P("lat", "lon"),
            P("lat", "lon"),
            P("lat", "lon"),
            P(None, "lat", "lon"),
            P("lat", None, "lon"),
            P("lat", "lon", None, None),
            P(None, "lat", "lon"),
            P(None, "lat", "lon"),
            P(None, "lat", "lon"),
            P("lat", "lon"),
        ),
        out_specs=(P(None, None, "lat", "lon"), P("lat", "lon"), P(None, "lat", "lon")),
        check_vma=False,
    )
```

```python
import jax
import jax.numpy as jnp
from jax import lax
from jax.experimental import pallas as pl
from jax.experimental.pallas import tpu as pltpu
from jax.sharding import PartitionSpec as P

SUBSTEPS = 6
HALO = 8
FIELDS = 7
HEIGHT, EAST, NORTH, LEVELS, FRESH, WIND_E, WIND_N = range(FIELDS)
ROW_RIM = FIELDS * HALO
ROW_T = ROW_RIM + HALO
LISTS = 256
OWNER, SLOT, USED = 32, 64, 96

adv_rate = 0.1
heat_gain = 0.5
salt_gain = 0.5
wave_div = 0.5
wave_grad = 0.8
fresh_gain = 0.2
wind_gain = 0.2

F32 = jnp.float32


def lanes(shape):
    return lax.broadcasted_iota(jnp.int32, shape, len(shape) - 1)


def rows_of(shape):
    return lax.broadcasted_iota(jnp.int32, shape, len(shape) - 2)


def turn(x, by, axis):
    size = x.shape[axis]
    by = by % size
    return x if by == 0 else pltpu.roll(x, by, axis)


def is_even(axis):
    return lax.rem(lax.axis_index(axis), 2) == 0


def is_top():
    return lax.axis_index("lat") == lax.axis_size("lat") - 1


def pick_kernel(
    atm_hbm, rows_hbm, t_hbm, v_hbm, out_hbm, t_ref, u_ref, v_rows, atm_ref, rows_ref, out_ref, sems,
):
    last = t_ref.shape[2] - HALO
    copies = [
        pltpu.make_async_copy(atm_hbm, atm_ref, sems.at[0]),
        pltpu.make_async_copy(rows_hbm, rows_ref, sems.at[1]),
        pltpu.make_async_copy(t_hbm, t_ref, sems.at[2]),
        pltpu.make_async_copy(v_hbm.at[0], u_ref, sems.at[3]),
        pltpu.make_async_copy(v_hbm.at[1, :, last:], v_rows, sems.at[4]),
    ]
    for copy in copies:
        copy.start()
    for copy in copies[:2]:
        copy.wait()
    rows = rows_ref[0, 0]
    both = jnp.concatenate([rows, rows], axis=1)
    lane = both & 127
    part = both >> 7
    low = lanes(both.shape) < 64
    values = []
    for f in range(4):
        acc = None
        for k in range(atm_ref.shape[2] // 128):
            row = jnp.broadcast_to(atm_ref[0, f : f + 1, k * 128 : (k + 1) * 128], both.shape)
            value = jnp.take_along_axis(row, lane, axis=1)
            acc = value if k == 0 else jnp.where(part == k, value, acc)
        values.append(acc)
    out_ref[:, 0, 0:128] = jnp.where(low, values[0], values[1])
    out_ref[:, 0, 128:256] = jnp.where(low, values[2], values[3])
    for f in range(1, 4):
        at = 128 + f * 128
        out_ref[:, 0, at : at + 128] = jnp.where(low, turn(values[f], -1, 0), turn(values[f], 1, 0))
    copies.append(pltpu.make_async_copy(out_ref, out_hbm, sems.at[5]))
    copies[-1].start()
    for copy in copies[2:]:
        copy.wait()


def edge_kernel(
    picked_ref, v_rows, t_ref, u_ref, level_ref, height_ref, transport_ref, owner_ref, slot_ref, weight_ref, count_ref,
    two_ref, one_ref, t_0_ref, rows_ref, pick_row_ref, pick_lane_ref, used_ref,
):
    depth, rows, cols = t_ref.shape[1:]
    shape = (rows, cols)
    lane = lanes(shape)
    level = level_ref[...]
    half = lax.axis_size("lon") // 2
    count = count_ref[...]
    for k in range(owner_ref.shape[0]):
        owner = owner_ref[k]
        high = owner >= half
        pick_row_ref[k] = jnp.where(high, owner - half, owner)
        pick_lane_ref[k] = jnp.where(high, slot_ref[k] + 64, slot_ref[k])
        used_ref[k] = jnp.where(count > k, weight_ref[k], 0.0)
    fields = [height_ref[...], transport_ref[0], transport_ref[1], level.astype(F32)]
    fields += [owner_ref[k].astype(F32) for k in range(4)]
    fields += [slot_ref[k].astype(F32) for k in range(4)]
    fields += [used_ref[k] for k in range(4)]
    west = jnp.zeros(shape, F32)
    east = jnp.zeros(shape, F32)
    for g, field in enumerate(fields):
        here = (lane >= g * HALO) & (lane < (g + 1) * HALO)
        west = jnp.where(here, turn(field, g * HALO, 1), west)
        east = jnp.where(here, turn(field, (g + 1) * HALO, 1), east)
    west_t = jnp.zeros(shape, F32)
    east_t = jnp.zeros(shape, F32)
    for c in range(2):
        for l in range(depth):
            f = c * depth + l
            moved = turn(t_ref[c, l], f + 1, 1)
            west_t = jnp.where(lane == f + 1, moved, west_t)
            east_t = jnp.where(lane == f, moved, east_t)
    for l in range(depth):
        at = 2 * depth + l
        east_t = jnp.where(lane == at, turn(u_ref[l], at + 1, 1), east_t)
    even = is_even("lon")
    one_ref[:rows] = jnp.where(even, east, west)
    two_ref[:rows] = jnp.where(even, west, east)
    one_ref[rows:] = jnp.where(even, east_t, west_t)
    two_ref[rows:] = jnp.where(even, west_t, east_t)
    t_0_ref[...] = turn(west_t, -1, 1)
    for c in range(2):
        for l in range(depth):
            at = c * depth + l
            rows_ref[0, at : at + 1] = t_ref[c, l, rows - 1 : rows]
            rows_ref[1, at : at + 1] = t_ref[c, l, 0:1]
    for l in range(depth):
        at = 2 * depth + l
        rows_ref[0, at : at + 1] = v_rows[l, HALO - 1 : HALO]
    rows_ref[1, 2 * depth :] = jnp.zeros((depth, cols), F32)

def own_lookup(tab, row_ref, lane_ref, used_ref, cut, fields):
    total = {f: None for f in fields}
    for k in range(used_ref.shape[0]):
        lane = lane_ref[k, cut]
        row = row_ref[k, cut]
        acc = {}
        for r in range(tab.shape[1]):
            here = row == r
            for f in fields:
                source = jnp.broadcast_to(tab[f, r : r + 1, :], lane.shape)
                value = jnp.take_along_axis(source, lane, axis=1)
                acc[f] = value if r == 0 else jnp.where(here, value, acc[f])
        used = used_ref[k, cut]
        for f in fields:
            total[f] = acc[f] * used if k == 0 else total[f] + acc[f] * used
    return total


def rim_of(east, west, by_east, by_west):
    lane = lanes(east.shape)
    outer = jnp.where(lane >= 128 - HALO, turn(west, by_west, 1), 0.0)
    return jnp.where(lane < HALO, turn(east, by_east, 1), outer)


def from_lon(one_ref, two_ref, cut):
    even = is_even("lon")
    one, two = one_ref[cut], two_ref[cut]
    return jnp.where(even, one, two), jnp.where(even, two, one)


def state_rims(east, west):
    return [rim_of(east, west, -g * HALO, 128 - (g + 1) * HALO) for g in range(4)]


def side_lookup(side, sides):
    (east, west), (east_2, west_2) = sides
    lane = lanes(east.shape)
    quarter = lane >> 5

    def gathered(by):
        parts = (turn(west_2, -32 - by, 1), turn(east, -by, 1), turn(west, 32 - by, 1), turn(east_2, 64 - by, 1))
        low = jnp.where(quarter == 0, parts[0], parts[1])
        return jnp.where(quarter < 2, low, jnp.where(quarter == 2, parts[2], parts[3]))

    owner = gathered(0).astype(jnp.int32)
    slot = gathered(32).astype(jnp.int32)
    used = gathered(64)
    slot = jnp.where((quarter & 1) == 0, slot + 64, slot)
    acc = [None] * 3
    for r in range(side.shape[1]):
        here = owner == r
        for f in range(3):
            source = jnp.broadcast_to(side[f, r : r + 1, :], slot.shape)
            value = jnp.take_along_axis(source, slot, axis=1)
            acc[f] = value if r == 0 else jnp.where(here, value, acc[f])
    rims = ([], [])
    for f in range(3):
        v = acc[f] * used
        v = v + turn(v, -16, 1)
        v = v + turn(v, -8, 1)
        rims[0].append(rim_of(v, v, -32, 56))
        rims[1].append(rim_of(v, v, -96, 120))
    return rims


def rim_lookup_kernel(
    table_ref, two_ref, one_ref, pick_row_ref, pick_lane_ref, used_ref, rows_ref, level_ref, height_ref,
    transport_ref, after_ref, first_ref, second_ref, flux_ref, rim_ref, tab, side, pack,
):
    n_lon = table_ref.shape[0]
    half = n_lon // 2
    rows, cols = height_ref.shape
    low = lanes((half, 128)) < 64
    for pair in range(2):
        part = table_ref[:, 0, pair * 128 : (pair + 1) * 128]
        lo, hi = part[:half], part[half:]
        tab[2 * pair] = jnp.where(low, lo, turn(hi, 64, 1))
        tab[2 * pair + 1] = jnp.where(low, turn(lo, 64, 1), hi)
    for f in range(3):
        side[f] = table_ref[:, 0, LISTS + f * 128 : LISTS + (f + 1) * 128]
    lane = lanes((HALO, cols))
    cuts = (slice(rows - HALO, rows), slice(0, HALO))
    sides = [from_lon(one_ref, two_ref, cut) for cut in cuts]
    side_rims = side_lookup(side, sides)
    for s, cut in enumerate(cuts):
        found = own_lookup(tab, pick_row_ref, pick_lane_ref, used_ref, cut, (1, 2, 3))
        for f in range(3):
            flux_ref[s, f] = found[f + 1]
            rim_ref[s, f] = side_rims[s][f]
        rims = state_rims(*sides[s]) + side_rims[s]
        own = [
            height_ref[cut], transport_ref[0, cut], transport_ref[1, cut], level_ref[cut].astype(F32),
            found[1], found[2], found[3],
        ]
        packed = jnp.zeros((HALO, cols), F32)
        for i in range(FIELDS):
            pack[s, i * HALO : (i + 1) * HALO] = own[i]
            start = 2 * HALO * i
            here = (lane >= start) & (lane < start + 2 * HALO)
            packed = jnp.where(here, turn(rims[i], start + HALO, 1), packed)
        pack[s, ROW_RIM:ROW_T] = packed
        pack[s, ROW_T:] = rows_ref[s]
    even = is_even("lat")
    north_going, south_going = pack[0], pack[1]
    first_ref[...] = jnp.where(even, north_going, south_going)
    second_ref[...] = jnp.where(even, south_going, north_going)


def sources(flux_ref, level_ref, cut):
    wet = (level_ref[cut] > 0).astype(F32)
    return heat_gain * flux_ref[0, cut] * wet, -salt_gain * flux_ref[1, cut] * wet


def lookup_kernel(
    edge_flux_ref, edge_rim_ref, tab, side, two_ref, one_ref, pick_row_ref, pick_lane_ref, used_ref,
    level_ref, x_ref, unit_ref, flux_ref, rim_ref, t_out, fixed, sems,
):
    rows = used_ref.shape[1]
    depth = x_ref.shape[1]
    cuts = [slice(at, at + HALO) for at in range(0, rows, HALO)]
    sides = [from_lon(one_ref, two_ref, cut) for cut in cuts]
    for at in range(1, len(cuts) - 1, 2):
        side_rims = side_lookup(side, sides[at : at + 2])
        for i in range(2):
            cut = cuts[at + i]
            found = own_lookup(tab, pick_row_ref, pick_lane_ref, used_ref, cut, (0, 1, 2, 3))
            for f in range(4):
                flux_ref[f, cut] = found[f]
            for g, rim in enumerate(state_rims(*sides[at + i]) + side_rims[i]):
                rim_ref[g, cut] = rim
    mid = slice(HALO, rows - HALO)
    source = sources(flux_ref, level_ref, mid)
    copies = []
    for c in range(2):
        for l in range(depth):
            fixed[c, l] = x_ref[c, l, mid] + unit_ref[l, mid] * source[c]
        copies.append(pltpu.make_async_copy(fixed.at[c], t_out.at[c, :, mid], sems.at[c]))
        copies[c].start()
    for s, at in ((0, len(cuts) - 1), (1, 0)):
        cut = cuts[at]
        flux_ref[0, cut] = own_lookup(tab, pick_row_ref, pick_lane_ref, used_ref, cut, (0,))[0]
        for f in range(3):
            flux_ref[f + 1, cut] = edge_flux_ref[s, f]
        for g, rim in enumerate(state_rims(*sides[at]) + [edge_rim_ref[s, f] for f in range(3)]):
            rim_ref[g, cut] = rim
    for copy in copies:
        copy.wait()


def split(x):
    hi = x.astype(jnp.bfloat16)
    return hi, (x - hi.astype(F32)).astype(jnp.bfloat16)


def tracer_kernel(
    two_ref, one_ref, t_0_ref, level_ref, diff_ref, t_ref, u_ref, v_hbm, x_ref, unit_ref, inv_rows_ref, gain_ref,
    parts, rims, net_x, v_ref, sem,
):
    depth, rows, cols = t_ref.shape[1:]
    copy = pltpu.make_async_copy(v_hbm.at[1], v_ref, sem)
    copy.start()
    shape = (rows, cols)
    east, west = from_lon(one_ref, two_ref, slice(0, rows))
    t_e, t_w = from_lon(one_ref, two_ref, slice(rows, 2 * rows))
    level = level_ref[...]
    level_f = level.astype(F32)
    lane = lanes(shape)
    row = rows_of(shape)
    first = LEVELS * HALO
    last = cols - 1
    level_e = jnp.where(lane == last, turn(east, last - first, 1), turn(level_f, -1, 1))
    level_n = turn(level_f, -1, 0)
    face_e = jnp.minimum(level_f, level_e)
    face_n = jnp.where(row == rows - 1, 0.0, jnp.minimum(level_f, level_n))
    t_0 = t_0_ref[...]
    u_w = jnp.where(lane < depth, turn(t_w, -2 * depth, 1), turn(t_w, -depth, 1))
    layer = jnp.where(lane < depth, lane, lane - depth).astype(F32)
    level_w = west[:, first + HALO - 1 : first + HALO]
    face_w = jnp.broadcast_to(jnp.minimum(level_f[:, 0:1], level_w), shape)
    west_flux = jnp.where((layer < face_w) & (lane < 2 * depth), u_w * ((t_w + t_0) * 0.5), 0.0)
    both = []
    for x in (turn(t_e, -1, 1), west_flux):
        hi, lo = split(x)
        both.append(jnp.where(lane < 64, hi.astype(F32), turn(lo.astype(F32), 64, 1)))
    plane = lane & 63
    for f in range(2 * depth):
        at = slice(f * rows, (f + 1) * rows)
        here = plane == f
        parts[at, 0:128] = jnp.where(here, both[0], 0.0).astype(jnp.bfloat16)
        parts[at, 128:256] = jnp.where(here, both[1], 0.0).astype(jnp.bfloat16)
    k = lax.broadcasted_iota(jnp.int32, (2 * cols, cols), 0)
    into = jnp.where(k < cols, last, 0) == lanes((2 * cols, cols))
    rims[...] = jnp.dot(parts[...], into.astype(F32).astype(jnp.bfloat16), preferred_element_type=F32)
    for l in range(depth):
        mask_e = face_e > l
        u_l = u_ref[l] * 0.5
        for c in range(2):
            f = c * depth + l
            at = slice(f * rows, (f + 1) * rows)
            t = t_ref[c, l]
            t_east = jnp.where(lane == last, rims[at], turn(t, -1, 1))
            flux_e = jnp.where(mask_e, u_l * (t + t_east), 0.0)
            net_x[at] = flux_e - jnp.where(lane == 0, rims[at], turn(flux_e, 1, 1))
    copy.wait()
    diff = diff_ref[...]
    above = jnp.zeros(shape, F32)
    inv = None
    right = [None, None, None]
    for l in range(depth):
        below = jnp.where(level > l + 1, diff, 0.0) if l < depth - 1 else jnp.zeros(shape, F32)
        pivot = 1.0 + above + below
        if l > 0:
            pivot = pivot - above * above * inv
        inv = 1.0 / pivot
        inv_rows_ref[0, l : l + 1] = inv[rows - 1 : rows]
        inv_rows_ref[1, l : l + 1] = inv[0:1]
        gain_ref[l] = below * inv
        mask_n = face_n > l
        v_l = v_ref[l] * 0.5
        for c in range(2):
            f = c * depth + l
            at = slice(f * rows, (f + 1) * rows)
            t = t_ref[c, l]
            flux_n = jnp.where(mask_n, v_l * (t + turn(t, -1, 0)), 0.0)
            flux_s = turn(flux_n, 1, 0)
            forced = t - adv_rate * (net_x[at] + (flux_n - flux_s))
            right[c] = forced * inv if l == 0 else (forced + above * right[c]) * inv
            x_ref[c, l] = right[c]
        right[2] = inv if l == 0 else above * right[2] * inv
        unit_ref[l] = right[2]
        above = below
    for l in range(depth - 2, -1, -1):
        gain = gain_ref[l]
        for c in range(2):
            right[c] = x_ref[c, l] + gain * right[c]
            x_ref[c, l] = right[c]
        right[2] = unit_ref[l] + gain * right[2]
        unit_ref[l] = right[2]


def step_kernel(
    first_ref, second_ref, height_ref, transport_ref, level_ref, diff_ref, flux_ref, rim_ref, rows_ref, inv_rows_ref,
    x_ref, unit_ref, t_middle, t_out, height_out, transport_out, north_ref, shift, fixed, result, sems,
):
    top = is_top()
    level = level_ref[...]
    level_f = level.astype(F32)
    rows, cols = level.shape
    depth = x_ref.shape[1]
    lo, hi = slice(0, HALO), slice(rows - HALO, rows)
    copies = []

    def send(value, out):
        copies.append(pltpu.make_async_copy(value, out, sems.at[len(copies)]))
        copies[-1].start()

    even = is_even("lat")
    a, b = first_ref[...], second_ref[...]
    south = jnp.where(even, b, a)
    north = jnp.where(even, a, b)
    mirrored = jnp.take_along_axis(north, 127 - lanes(north.shape), axis=1)
    north = jnp.where(top, mirrored, north)
    north_ref[...] = north

    first = LEVELS * HALO
    level_n = jnp.where(top, north[first + HALO - 1 : first + HALO], north[first : first + 1])
    level_s = south[first + HALO - 1 : first + HALO]
    sides = ((north, level_n, rows - 1, -adv_rate), (south, level_s, 0, adv_rate))
    chains = []
    for s, (message, level_out, at, gain) in enumerate(sides):
        level_in = level_f[at : at + 1]
        face = jnp.minimum(level_in, level_out)
        speed = rows_ref[0, 2 * depth :] if s == 0 else message[ROW_T + 2 * depth :]
        for c in range(2):
            planes = slice(c * depth, (c + 1) * depth)
            outside = message[ROW_T + c * depth : ROW_T + (c + 1) * depth]
            flux = speed * ((outside + rows_ref[s, planes]) * 0.5)
            deep = rows_of(flux.shape).astype(F32) < face
            shift[s, planes] = jnp.where(deep, gain * flux, 0.0)
            chains.append((s, c, level_in, diff_ref[at : at + 1]))
    right = [None] * 4
    for l in range(depth):
        for i, (s, c, level_in, diff_in) in enumerate(chains):
            at = c * depth + l
            inv = inv_rows_ref[s, l : l + 1]
            value = shift[s, at : at + 1]
            if l > 0:
                value = value + jnp.where(level_in > l, diff_in, 0.0) * right[i]
            right[i] = value * inv
            shift[s, at : at + 1] = right[i]
    for l in range(depth - 2, -1, -1):
        for i, (s, c, level_in, diff_in) in enumerate(chains):
            at = c * depth + l
            inv = inv_rows_ref[s, l : l + 1]
            below = jnp.where(level_in > l + 1, diff_in, 0.0) * inv
            right[i] = shift[s, at : at + 1] + below * right[i]
            shift[s, at : at + 1] = right[i]
    own = (
        height_ref[...], transport_ref[0], transport_ref[1], level_f,
        flux_ref[1], flux_ref[2], flux_ref[3],
    )
    ext = []
    lane = lanes((HALO, cols))
    side = (lane < HALO) | (lane >= cols - HALO)
    for i in range(FIELDS):
        at = slice(i * HALO, (i + 1) * HALO)
        whole = jnp.concatenate([south[at], own[i], north[at]], axis=0)
        start = jnp.where(top, cols - 2 * HALO * (FIELDS - i) - HALO, cols - 2 * HALO * i - HALO)
        north_rim = jnp.where(side, pltpu.roll(north[ROW_RIM:ROW_T], start, 1), 0.0)
        south_rim = jnp.where(side, turn(south[ROW_RIM:ROW_T], -(2 * HALO * i + HALO), 1), 0.0)
        rim = jnp.concatenate([south_rim, rim_ref[i], north_rim], axis=0)
        ext.append(jnp.concatenate([whole, rim], axis=1))


    def coefficients(f):
        wet = (f[LEVELS] > 0.0).astype(F32)
        return (
            wet,
            wave_grad * (f[LEVELS] / depth),
            fresh_gain * f[FRESH] * wet,
            wind_gain * f[WIND_E] * wet,
            wind_gain * f[WIND_N] * wet,
        )

    mine = [x for x in ext]
    fold = [x[HALO + rows :] for x in ext]
    wet, grad, fresh, wind_e, wind_n = coefficients(mine)
    p_wet, p_grad, p_fresh, p_wind_e, p_wind_n = coefficients(fold)
    h, e, n = mine[HEIGHT], mine[EAST], mine[NORTH]
    p_h, p_e, p_n = fold[HEIGHT], fold[EAST], fold[NORTH]
    row_h = rows_of(h.shape)
    last = HALO + rows - 1
    across = (row_h == last) & top
    p_last = rows_of(p_h.shape) == HALO - 1
    for step in range(SUBSTEPS):
        if step == 3:
            row = rows_of((HALO, cols))
            for s, cut, at_row in ((0, hi, HALO - 1), (1, lo, 0)):
                source = sources(flux_ref, level_ref, cut)
                for c in range(2):
                    for l in range(depth):
                        at = c * depth + l
                        add = jnp.broadcast_to(shift[s, at : at + 1], (HALO, cols))
                        x = x_ref[c, l, cut] + unit_ref[l, cut] * source[c]
                        fixed[s, c, l] = x + jnp.where(row == at_row, add, 0.0)
                send(fixed.at[s], t_out.at[:, :, cut])
        h = (h - wave_div * ((e - turn(e, 1, 1)) + (n - turn(n, 1, 0)))) * wet + fresh
        p_h = (p_h - wave_div * ((p_e - turn(p_e, -1, 1)) + (p_n - turn(p_n, 1, 0)))) * p_wet + p_fresh
        h_n = jnp.where(across, jnp.broadcast_to(p_h[HALO - 1 :], h.shape), turn(h, -1, 0))
        p_h_n = jnp.where(p_last, jnp.broadcast_to(h[last : last + 1], p_h.shape), turn(p_h, -1, 0))
        e = (e - grad * (turn(h, -1, 1) - h)) * wet + wind_e
        n = (n - grad * (h_n - h)) * wet + wind_n
        p_e = (p_e - p_grad * (turn(p_h, 1, 1) - p_h)) * p_wet + p_wind_e
        p_n = (p_n - p_grad * (p_h_n - p_h)) * p_wet + p_wind_n
    inside = slice(HALO, HALO + rows)
    result[0] = h[inside, :cols]
    result[1] = e[inside, :cols]
    result[2] = n[inside, :cols]
    send(result.at[0], height_out)
    send(result.at[1:3], transport_out)

    for copy in copies:
        copy.wait()


def vmem(count):
    return [pl.BlockSpec(memory_space=pltpu.VMEM)] * count


def params(mib=24):
    return pltpu.CompilerParams(vmem_limit_bytes=mib * 1024 * 1024)


def work(mb):
    return pl.CostEstimate(flops=mb * 1000000, bytes_accessed=mb * 1000000, transcendentals=0)


def in_hbm(x):
    return pltpu.with_memory_space_constraint(x, pltpu.HBM)


def shape_of(*shape):
    return jax.ShapeDtypeStruct(shape, F32)


def lat_pairs(n_lat, n_lon):
    def at(i, j):
        return i * n_lon + j

    first, second = [], []
    for j in range(n_lon):
        for i in range(0, n_lat, 2):
            first += [(at(i, j), at(i + 1, j)), (at(i + 1, j), at(i, j))]
        for i in range(1, n_lat - 1, 2):
            second += [(at(i, j), at(i + 1, j)), (at(i + 1, j), at(i, j))]
        second.append((at(n_lat - 1, j), at(n_lat - 1, n_lon - 1 - j)))
    return first, second


def lon_pairs(n_lon):
    first, second = [], []
    for j in range(0, n_lon, 2):
        first += [(j, j + 1), (j + 1, j)]
        k, m = j + 1, (j + 2) % n_lon
        second += [(k, m), (m, k)]
    return first, second


def per_device(
    tracers,
    velocity,
    diffusivity,
    ocean_levels,
    surface_height,
    transport,
    atm_flux,
    send_rows,
    src_owner,
    src_slot,
    xgrid_weights,
    xgrid_count,
):
    n_lat, n_lon = lax.axis_size("lat"), lax.axis_size("lon")
    depth, rows, cols = tracers.shape[1:]
    slots = send_rows.shape[3]
    block = (rows, cols)
    picked, t_near, u_near, v_rows = pl.pallas_call(
        pick_kernel,
        out_shape=(
            shape_of(n_lon, 1, 10 * slots),
            shape_of(2, depth, *block),
            shape_of(depth, *block),
            shape_of(depth, HALO, cols),
        ),
        in_specs=[pl.BlockSpec(memory_space=pltpu.HBM)] * 4,
        out_specs=[pl.BlockSpec(memory_space=pltpu.HBM)] + vmem(3),
        scratch_shapes=[
            pltpu.VMEM(atm_flux.shape, F32),
            pltpu.VMEM(send_rows.shape, jnp.int32),
            pltpu.VMEM((n_lon, 1, 10 * slots), F32),
            pltpu.SemaphoreType.DMA((6,)),
        ],
        compiler_params=params(24),
        cost_estimate=work(40),
        name="pick",
    )(in_hbm(atm_flux), in_hbm(send_rows), in_hbm(tracers), in_hbm(velocity))
    table = lax.all_to_all(picked, "lon", split_axis=0, concat_axis=0, tiled=True)

    lat_rows = ROW_T + 3 * depth
    two, one, t_0, edge_rows, pick_row, pick_lane, used = pl.pallas_call(
        edge_kernel,
        out_shape=(
            shape_of(2 * rows, cols),
            shape_of(2 * rows, cols),
            shape_of(*block),
            shape_of(2, 3 * depth, cols),
            jax.ShapeDtypeStruct((4, *block), jnp.int32),
            jax.ShapeDtypeStruct((4, *block), jnp.int32),
            shape_of(4, *block),
        ),
        in_specs=[pl.BlockSpec(memory_space=pl.ANY)] + vmem(10),
        out_specs=vmem(7),
        compiler_params=params(),
        cost_estimate=work(2),
        name="edges",
    )(
        picked, v_rows, t_near, u_near, ocean_levels, surface_height, transport, src_owner, src_slot,
        xgrid_weights, xgrid_count,
    )
    pairs = lon_pairs(n_lon)
    two = lax.ppermute(two, "lon", pairs[1])
    one = lax.ppermute(one, "lon", pairs[0])

    solved, unit, inv_rows = pl.pallas_call(
        tracer_kernel,
        out_shape=(shape_of(2, depth, *block), shape_of(depth, *block), shape_of(2, depth, cols)),
        in_specs=vmem(7) + [pl.BlockSpec(memory_space=pltpu.HBM)],
        out_specs=vmem(3),
        scratch_shapes=[
            pltpu.VMEM((depth, *block), F32),
            pltpu.VMEM((2 * depth * rows, 2 * cols), jnp.bfloat16),
            pltpu.VMEM((2 * depth * rows, cols), F32),
            pltpu.VMEM((2 * depth * rows, cols), F32),
            pltpu.VMEM((depth, *block), F32),
            pltpu.SemaphoreType.DMA,
        ],
        compiler_params=params(),
        cost_estimate=work(8),
        name="tracers",
    )(two, one, t_0, ocean_levels, diffusivity, t_near, u_near, in_hbm(velocity))

    first, second, edge_flux, edge_rim, tab, side = pl.pallas_call(
        rim_lookup_kernel,
        out_shape=(
            shape_of(lat_rows, cols),
            shape_of(lat_rows, cols),
            shape_of(2, 3, HALO, cols),
            shape_of(2, 3, HALO, cols),
            shape_of(4, n_lon // 2, 128),
            shape_of(3, n_lon, 128),
        ),
        in_specs=vmem(10) + [pl.BlockSpec(memory_space=pl.ANY)],
        out_specs=vmem(6),
        scratch_shapes=[pltpu.VMEM((2, lat_rows, cols), F32)],
        compiler_params=params(),
        cost_estimate=work(8),
        name="rim_lookup",
    )(
        table, two, one, pick_row, pick_lane, used, edge_rows, ocean_levels, surface_height, transport,
        inv_rows,
    )
    pairs = lat_pairs(n_lat, n_lon)
    first = lax.ppermute(first, ("lat", "lon"), pairs[0])
    second = lax.ppermute(second, ("lat", "lon"), pairs[1])

    flux, rim, t_middle = pl.pallas_call(
        lookup_kernel,
        out_shape=(shape_of(4, *block), shape_of(FIELDS, *block), shape_of(2, depth, *block)),
        in_specs=vmem(12),
        out_specs=vmem(2) + [pl.BlockSpec(memory_space=pltpu.HBM)],
        scratch_shapes=[pltpu.VMEM((2, depth, rows - 2 * HALO, cols), F32), pltpu.SemaphoreType.DMA((2,))],
        compiler_params=params(),
        cost_estimate=work(8),
        name="lookup",
    )(
        edge_flux, edge_rim, tab, side, two, one, pick_row, pick_lane, used, ocean_levels, solved, unit,
    )

    return pl.pallas_call(
        step_kernel,
        out_shape=(shape_of(2, depth, rows, cols), shape_of(rows, cols), shape_of(2, rows, cols)),
        in_specs=vmem(12) + [pl.BlockSpec(memory_space=pltpu.HBM)],
        out_specs=(pl.BlockSpec(memory_space=pltpu.HBM),) * 3,
        input_output_aliases={12: 0},
        scratch_shapes=[
            pltpu.VMEM((lat_rows, cols), F32),
            pltpu.VMEM((2, 2 * depth, cols), F32),
            pltpu.VMEM((2, 2, depth, HALO, cols), F32),
            pltpu.VMEM((3, rows, cols), F32),
            pltpu.SemaphoreType.DMA((4,)),
        ],
        compiler_params=params(),
        name="step",
    )(
        first, second, surface_height, transport, ocean_levels, diffusivity, flux, rim, edge_rows, inv_rows,
        solved, unit, t_middle,
    )


def solution(mesh):
    return jax.shard_map(
        per_device,
        mesh=mesh,
        in_specs=(
            P(None, None, "lat", "lon"),
            P(None, None, "lat", "lon"),
            P("lat", "lon"),
            P("lat", "lon"),
            P("lat", "lon"),
            P(None, "lat", "lon"),
            P("lat", None, "lon"),
            P("lat", "lon", None, None),
            P(None, "lat", "lon"),
            P(None, "lat", "lon"),
            P(None, "lat", "lon"),
            P("lat", "lon"),
        ),
        out_specs=(P(None, None, "lat", "lon"), P("lat", "lon"), P(None, "lat", "lon")),
        check_vma=False,
    )
```

```python
import jax
import jax.numpy as jnp
from jax import lax
from jax.experimental import pallas as pl
from jax.experimental.pallas import tpu as pltpu
from jax.sharding import PartitionSpec as P

SUBSTEPS = 6
HALO = 8
FIELDS = 7
HEIGHT, EAST, NORTH, LEVELS, FRESH, WIND_E, WIND_N = range(FIELDS)
ROW_RIM = FIELDS * HALO
ROW_T = ROW_RIM + HALO
LISTS = 256
OWNER, SLOT, USED = 32, 64, 96

adv_rate = 0.1
heat_gain = 0.5
salt_gain = 0.5
wave_div = 0.5
wave_grad = 0.8
fresh_gain = 0.2
wind_gain = 0.2

F32 = jnp.float32


def lanes(shape):
    return lax.broadcasted_iota(jnp.int32, shape, len(shape) - 1)


def rows_of(shape):
    return lax.broadcasted_iota(jnp.int32, shape, len(shape) - 2)


def turn(x, by, axis):
    size = x.shape[axis]
    by = by % size
    return x if by == 0 else pltpu.roll(x, by, axis)


def is_even(axis):
    return lax.rem(lax.axis_index(axis), 2) == 0


def is_top():
    return lax.axis_index("lat") == lax.axis_size("lat") - 1


def pick_kernel(
    atm_hbm, rows_hbm, t_hbm, v_hbm, out_hbm, t_ref, u_ref, v_rows, atm_ref, rows_ref, out_ref, sems,
):
    last = t_ref.shape[2] - HALO
    copies = [
        pltpu.make_async_copy(atm_hbm, atm_ref, sems.at[0]),
        pltpu.make_async_copy(rows_hbm, rows_ref, sems.at[1]),
        pltpu.make_async_copy(t_hbm, t_ref, sems.at[2]),
        pltpu.make_async_copy(v_hbm.at[0], u_ref, sems.at[3]),
        pltpu.make_async_copy(v_hbm.at[1, :, last:], v_rows, sems.at[4]),
    ]
    for copy in copies:
        copy.start()
    for copy in copies[:2]:
        copy.wait()
    rows = rows_ref[0, 0]
    both = jnp.concatenate([rows, rows], axis=1)
    lane = both & 127
    part = both >> 7
    low = lanes(both.shape) < 64
    values = []
    for f in range(4):
        acc = None
        for k in range(atm_ref.shape[2] // 128):
            row = jnp.broadcast_to(atm_ref[0, f : f + 1, k * 128 : (k + 1) * 128], both.shape)
            value = jnp.take_along_axis(row, lane, axis=1)
            acc = value if k == 0 else jnp.where(part == k, value, acc)
        values.append(acc)
    out_ref[:, 0, 0:128] = jnp.where(low, values[0], values[1])
    out_ref[:, 0, 128:256] = jnp.where(low, values[2], values[3])
    for f in range(1, 4):
        at = 128 + f * 128
        out_ref[:, 0, at : at + 128] = jnp.where(low, turn(values[f], -1, 0), turn(values[f], 1, 0))
    copies.append(pltpu.make_async_copy(out_ref, out_hbm, sems.at[5]))
    copies[-1].start()
    for copy in copies[2:]:
        copy.wait()


def edge_kernel(
    picked_ref, v_rows, t_ref, u_ref, level_ref, height_ref, transport_ref, owner_ref, slot_ref, weight_ref, count_ref,
    two_ref, one_ref, t_0_ref, rows_ref, pick_row_ref, pick_lane_ref, used_ref,
):
    depth, rows, cols = t_ref.shape[1:]
    shape = (rows, cols)
    lane = lanes(shape)
    level = level_ref[...]
    half = lax.axis_size("lon") // 2
    count = count_ref[...]
    for k in range(owner_ref.shape[0]):
        owner = owner_ref[k]
        high = owner >= half
        pick_row_ref[k] = jnp.where(high, owner - half, owner)
        pick_lane_ref[k] = jnp.where(high, slot_ref[k] + 64, slot_ref[k])
        used_ref[k] = jnp.where(count > k, weight_ref[k], 0.0)
    fields = [height_ref[...], transport_ref[0], transport_ref[1], level.astype(F32)]
    fields += [owner_ref[k].astype(F32) for k in range(4)]
    fields += [slot_ref[k].astype(F32) for k in range(4)]
    fields += [used_ref[k] for k in range(4)]
    west = jnp.zeros(shape, F32)
    east = jnp.zeros(shape, F32)
    for g, field in enumerate(fields):
        here = (lane >= g * HALO) & (lane < (g + 1) * HALO)
        west = jnp.where(here, turn(field, g * HALO, 1), west)
        east = jnp.where(here, turn(field, (g + 1) * HALO, 1), east)
    west_t = jnp.zeros(shape, F32)
    east_t = jnp.zeros(shape, F32)
    for c in range(2):
        for l in range(depth):
            f = c * depth + l
            moved = turn(t_ref[c, l], f + 1, 1)
            west_t = jnp.where(lane == f + 1, moved, west_t)
            east_t = jnp.where(lane == f, moved, east_t)
    for l in range(depth):
        at = 2 * depth + l
        east_t = jnp.where(lane == at, turn(u_ref[l], at + 1, 1), east_t)
    even = is_even("lon")
    one_ref[:rows] = jnp.where(even, east, west)
    two_ref[:rows] = jnp.where(even, west, east)
    one_ref[rows:] = jnp.where(even, east_t, west_t)
    two_ref[rows:] = jnp.where(even, west_t, east_t)
    t_0_ref[...] = turn(west_t, -1, 1)
    for c in range(2):
        for l in range(depth):
            at = c * depth + l
            rows_ref[0, at : at + 1] = t_ref[c, l, rows - 1 : rows]
            rows_ref[1, at : at + 1] = t_ref[c, l, 0:1]
    for l in range(depth):
        at = 2 * depth + l
        rows_ref[0, at : at + 1] = v_rows[l, HALO - 1 : HALO]
    rows_ref[1, 2 * depth :] = jnp.zeros((depth, cols), F32)

def own_lookup(tab, row_ref, lane_ref, used_ref, cut, fields):
    total = {f: None for f in fields}
    for k in range(used_ref.shape[0]):
        lane = lane_ref[k, cut]
        row = row_ref[k, cut]
        acc = {}
        for r in range(tab.shape[1]):
            here = row == r
            for f in fields:
                source = jnp.broadcast_to(tab[f, r : r + 1, :], lane.shape)
                value = jnp.take_along_axis(source, lane, axis=1)
                acc[f] = value if r == 0 else jnp.where(here, value, acc[f])
        used = used_ref[k, cut]
        for f in fields:
            total[f] = acc[f] * used if k == 0 else total[f] + acc[f] * used
    return total


def rim_of(east, west, by_east, by_west):
    lane = lanes(east.shape)
    outer = jnp.where(lane >= 128 - HALO, turn(west, by_west, 1), 0.0)
    return jnp.where(lane < HALO, turn(east, by_east, 1), outer)


def from_lon(one_ref, two_ref, cut):
    even = is_even("lon")
    one, two = one_ref[cut], two_ref[cut]
    return jnp.where(even, one, two), jnp.where(even, two, one)


def state_rims(east, west):
    return [rim_of(east, west, -g * HALO, 128 - (g + 1) * HALO) for g in range(4)]


def side_lookup(side, sides):
    (east, west), (east_2, west_2) = sides
    lane = lanes(east.shape)
    quarter = lane >> 5

    def gathered(by):
        parts = (turn(west_2, -32 - by, 1), turn(east, -by, 1), turn(west, 32 - by, 1), turn(east_2, 64 - by, 1))
        low = jnp.where(quarter == 0, parts[0], parts[1])
        return jnp.where(quarter < 2, low, jnp.where(quarter == 2, parts[2], parts[3]))

    owner = gathered(0).astype(jnp.int32)
    slot = gathered(32).astype(jnp.int32)
    used = gathered(64)
    slot = jnp.where((quarter & 1) == 0, slot + 64, slot)
    acc = [None] * 3
    for r in range(side.shape[1]):
        here = owner == r
        for f in range(3):
            source = jnp.broadcast_to(side[f, r : r + 1, :], slot.shape)
            value = jnp.take_along_axis(source, slot, axis=1)
            acc[f] = value if r == 0 else jnp.where(here, value, acc[f])
    rims = ([], [])
    for f in range(3):
        v = acc[f] * used
        v = v + turn(v, -16, 1)
        v = v + turn(v, -8, 1)
        rims[0].append(rim_of(v, v, -32, 56))
        rims[1].append(rim_of(v, v, -96, 120))
    return rims


def rim_lookup_kernel(
    table_ref, two_ref, one_ref, pick_row_ref, pick_lane_ref, used_ref, rows_ref, level_ref, height_ref,
    transport_ref, second_ref, first_ref, flux_ref, rim_ref, tab, side, pack,
):
    n_lon = table_ref.shape[0]
    half = n_lon // 2
    rows, cols = height_ref.shape
    low = lanes((half, 128)) < 64
    for pair in range(2):
        part = table_ref[:, 0, pair * 128 : (pair + 1) * 128]
        lo, hi = part[:half], part[half:]
        tab[2 * pair] = jnp.where(low, lo, turn(hi, 64, 1))
        tab[2 * pair + 1] = jnp.where(low, turn(lo, 64, 1), hi)
    for f in range(3):
        side[f] = table_ref[:, 0, LISTS + f * 128 : LISTS + (f + 1) * 128]
    lane = lanes((HALO, cols))
    cuts = (slice(rows - HALO, rows), slice(0, HALO))
    sides = [from_lon(one_ref, two_ref, cut) for cut in cuts]
    side_rims = side_lookup(side, sides)
    for s, cut in enumerate(cuts):
        found = own_lookup(tab, pick_row_ref, pick_lane_ref, used_ref, cut, (1, 2, 3))
        for f in range(3):
            flux_ref[s, f] = found[f + 1]
            rim_ref[s, f] = side_rims[s][f]
        rims = state_rims(*sides[s]) + side_rims[s]
        own = [
            height_ref[cut], transport_ref[0, cut], transport_ref[1, cut], level_ref[cut].astype(F32),
            found[1], found[2], found[3],
        ]
        packed = jnp.zeros((HALO, cols), F32)
        for i in range(FIELDS):
            pack[s, i * HALO : (i + 1) * HALO] = own[i]
            start = 2 * HALO * i
            here = (lane >= start) & (lane < start + 2 * HALO)
            packed = jnp.where(here, turn(rims[i], start + HALO, 1), packed)
        pack[s, ROW_RIM:ROW_T] = packed
        pack[s, ROW_T:] = rows_ref[s]
    even = is_even("lat")
    north_going, south_going = pack[0], pack[1]
    second_ref[...] = jnp.where(even, south_going, north_going)
    first_ref[...] = jnp.where(even, north_going, south_going)


def lookup_kernel(
    edge_flux_ref, edge_rim_ref, tab, side, two_ref, one_ref, pick_row_ref, pick_lane_ref, used_ref,
    flux_ref, rim_ref,
):
    rows = used_ref.shape[1]
    cuts = [slice(at, at + HALO) for at in range(0, rows, HALO)]
    sides = [from_lon(one_ref, two_ref, cut) for cut in cuts]
    for at in range(1, len(cuts) - 1, 2):
        side_rims = side_lookup(side, sides[at : at + 2])
        for i in range(2):
            cut = cuts[at + i]
            found = own_lookup(tab, pick_row_ref, pick_lane_ref, used_ref, cut, (0, 1, 2, 3))
            for f in range(4):
                flux_ref[f, cut] = found[f]
            for g, rim in enumerate(state_rims(*sides[at + i]) + side_rims[i]):
                rim_ref[g, cut] = rim
    for s, at in ((0, len(cuts) - 1), (1, 0)):
        cut = cuts[at]
        flux_ref[0, cut] = own_lookup(tab, pick_row_ref, pick_lane_ref, used_ref, cut, (0,))[0]
        for f in range(3):
            flux_ref[f + 1, cut] = edge_flux_ref[s, f]
        for g, rim in enumerate(state_rims(*sides[at]) + [edge_rim_ref[s, f] for f in range(3)]):
            rim_ref[g, cut] = rim


def split(x):
    hi = x.astype(jnp.bfloat16)
    return hi, (x - hi.astype(F32)).astype(jnp.bfloat16)


def tracer_kernel(
    two_ref, one_ref, t_0_ref, level_ref, diff_ref, t_ref, u_ref, v_hbm, x_ref, unit_ref, inv_rows_ref, gain_ref,
    parts, rims, net_x, v_ref, sem,
):
    depth, rows, cols = t_ref.shape[1:]
    copy = pltpu.make_async_copy(v_hbm.at[1], v_ref, sem)
    copy.start()
    shape = (rows, cols)
    east, west = from_lon(one_ref, two_ref, slice(0, rows))
    t_e, t_w = from_lon(one_ref, two_ref, slice(rows, 2 * rows))
    level = level_ref[...]
    level_f = level.astype(F32)
    lane = lanes(shape)
    row = rows_of(shape)
    first = LEVELS * HALO
    last = cols - 1
    level_e = jnp.where(lane == last, turn(east, last - first, 1), turn(level_f, -1, 1))
    level_n = turn(level_f, -1, 0)
    face_e = jnp.minimum(level_f, level_e)
    face_n = jnp.where(row == rows - 1, 0.0, jnp.minimum(level_f, level_n))
    t_0 = t_0_ref[...]
    u_w = jnp.where(lane < depth, turn(t_w, -2 * depth, 1), turn(t_w, -depth, 1))
    layer = jnp.where(lane < depth, lane, lane - depth).astype(F32)
    level_w = west[:, first + HALO - 1 : first + HALO]
    face_w = jnp.broadcast_to(jnp.minimum(level_f[:, 0:1], level_w), shape)
    west_flux = jnp.where((layer < face_w) & (lane < 2 * depth), u_w * ((t_w + t_0) * 0.5), 0.0)
    both = []
    for x in (turn(t_e, -1, 1), west_flux):
        hi, lo = split(x)
        both.append(jnp.where(lane < 64, hi.astype(F32), turn(lo.astype(F32), 64, 1)))
    plane = lane & 63
    for f in range(2 * depth):
        at = slice(f * rows, (f + 1) * rows)
        here = plane == f
        parts[at, 0:128] = jnp.where(here, both[0], 0.0).astype(jnp.bfloat16)
        parts[at, 128:256] = jnp.where(here, both[1], 0.0).astype(jnp.bfloat16)
    k = lax.broadcasted_iota(jnp.int32, (2 * cols, cols), 0)
    into = jnp.where(k < cols, last, 0) == lanes((2 * cols, cols))
    rims[...] = jnp.dot(parts[...], into.astype(F32).astype(jnp.bfloat16), preferred_element_type=F32)
    for l in range(depth):
        mask_e = face_e > l
        u_l = u_ref[l] * 0.5
        for c in range(2):
            f = c * depth + l
            at = slice(f * rows, (f + 1) * rows)
            t = t_ref[c, l]
            t_east = jnp.where(lane == last, rims[at], turn(t, -1, 1))
            flux_e = jnp.where(mask_e, u_l * (t + t_east), 0.0)
            net_x[at] = flux_e - jnp.where(lane == 0, rims[at], turn(flux_e, 1, 1))
    copy.wait()
    diff = diff_ref[...]
    above = jnp.zeros(shape, F32)
    inv = None
    right = [None, None, None]
    for l in range(depth):
        below = jnp.where(level > l + 1, diff, 0.0) if l < depth - 1 else jnp.zeros(shape, F32)
        pivot = 1.0 + above + below
        if l > 0:
            pivot = pivot - above * above * inv
        inv = 1.0 / pivot
        inv_rows_ref[0, l : l + 1] = inv[rows - 1 : rows]
        inv_rows_ref[1, l : l + 1] = inv[0:1]
        gain_ref[l] = below * inv
        mask_n = face_n > l
        v_l = v_ref[l] * 0.5
        for c in range(2):
            f = c * depth + l
            at = slice(f * rows, (f + 1) * rows)
            t = t_ref[c, l]
            flux_n = jnp.where(mask_n, v_l * (t + turn(t, -1, 0)), 0.0)
            flux_s = turn(flux_n, 1, 0)
            forced = t - adv_rate * (net_x[at] + (flux_n - flux_s))
            right[c] = forced * inv if l == 0 else (forced + above * right[c]) * inv
            x_ref[c, l] = right[c]
        right[2] = inv if l == 0 else above * right[2] * inv
        unit_ref[l] = right[2]
        above = below
    for l in range(depth - 2, -1, -1):
        gain = gain_ref[l]
        for c in range(2):
            right[c] = x_ref[c, l] + gain * right[c]
            x_ref[c, l] = right[c]
        right[2] = unit_ref[l] + gain * right[2]
        unit_ref[l] = right[2]


def step_kernel(
    second_ref, first_ref, height_ref, transport_ref, level_ref, diff_ref, flux_ref, rim_ref, rows_ref, inv_rows_ref,
    x_ref, unit_ref, t_out, height_out, transport_out, north_ref, shift, fixed, result, sems,
):
    top = is_top()
    level = level_ref[...]
    level_f = level.astype(F32)
    rows, cols = level.shape
    depth = x_ref.shape[1]
    wet_0 = (level > 0).astype(F32)
    source = (heat_gain * flux_ref[0] * wet_0, -salt_gain * flux_ref[1] * wet_0)
    lo, hi = slice(0, HALO), slice(rows - HALO, rows)
    mid = slice(HALO, rows - HALO)
    copies = []

    def send(value, out):
        copies.append(pltpu.make_async_copy(value, out, sems.at[len(copies)]))
        copies[-1].start()

    for c in range(2):
        for l in range(depth):
            fixed[c, l, mid] = x_ref[c, l, mid] + unit_ref[l, mid] * source[c][mid]
        send(fixed.at[c, :, mid], t_out.at[c, :, mid])
    even = is_even("lat")
    a, b = first_ref[...], second_ref[...]
    south = jnp.where(even, b, a)
    north = jnp.where(even, a, b)
    mirrored = jnp.take_along_axis(north, 127 - lanes(north.shape), axis=1)
    north = jnp.where(top, mirrored, north)
    north_ref[...] = north

    first = LEVELS * HALO
    level_n = jnp.where(top, north[first + HALO - 1 : first + HALO], north[first : first + 1])
    level_s = south[first + HALO - 1 : first + HALO]
    sides = ((north, level_n, rows - 1, -adv_rate), (south, level_s, 0, adv_rate))
    chains = []
    for s, (message, level_out, at, gain) in enumerate(sides):
        level_in = level_f[at : at + 1]
        face = jnp.minimum(level_in, level_out)
        speed = rows_ref[0, 2 * depth :] if s == 0 else message[ROW_T + 2 * depth :]
        for c in range(2):
            planes = slice(c * depth, (c + 1) * depth)
            outside = message[ROW_T + c * depth : ROW_T + (c + 1) * depth]
            flux = speed * ((outside + rows_ref[s, planes]) * 0.5)
            deep = rows_of(flux.shape).astype(F32) < face
            shift[s, planes] = jnp.where(deep, gain * flux, 0.0)
            chains.append((s, c, level_in, diff_ref[at : at + 1]))
    right = [None] * 4
    for l in range(depth):
        for i, (s, c, level_in, diff_in) in enumerate(chains):
            at = c * depth + l
            inv = inv_rows_ref[s, l : l + 1]
            value = shift[s, at : at + 1]
            if l > 0:
                value = value + jnp.where(level_in > l, diff_in, 0.0) * right[i]
            right[i] = value * inv
            shift[s, at : at + 1] = right[i]
    for l in range(depth - 2, -1, -1):
        for i, (s, c, level_in, diff_in) in enumerate(chains):
            at = c * depth + l
            inv = inv_rows_ref[s, l : l + 1]
            below = jnp.where(level_in > l + 1, diff_in, 0.0) * inv
            right[i] = shift[s, at : at + 1] + below * right[i]
            shift[s, at : at + 1] = right[i]
    own = (
        height_ref[...], transport_ref[0], transport_ref[1], level_f,
        flux_ref[1], flux_ref[2], flux_ref[3],
    )
    ext = []
    lane = lanes((HALO, cols))
    side = (lane < HALO) | (lane >= cols - HALO)
    for i in range(FIELDS):
        at = slice(i * HALO, (i + 1) * HALO)
        whole = jnp.concatenate([south[at], own[i], north[at]], axis=0)
        start = jnp.where(top, cols - 2 * HALO * (FIELDS - i) - HALO, cols - 2 * HALO * i - HALO)
        north_rim = jnp.where(side, pltpu.roll(north[ROW_RIM:ROW_T], start, 1), 0.0)
        south_rim = jnp.where(side, turn(south[ROW_RIM:ROW_T], -(2 * HALO * i + HALO), 1), 0.0)
        rim = jnp.concatenate([south_rim, rim_ref[i], north_rim], axis=0)
        ext.append(jnp.concatenate([whole, rim], axis=1))


    def coefficients(f):
        wet = (f[LEVELS] > 0.0).astype(F32)
        return (
            wet,
            wave_grad * (f[LEVELS] / depth),
            fresh_gain * f[FRESH] * wet,
            wind_gain * f[WIND_E] * wet,
            wind_gain * f[WIND_N] * wet,
        )

    mine = [x for x in ext]
    fold = [x[HALO + rows :] for x in ext]
    wet, grad, fresh, wind_e, wind_n = coefficients(mine)
    p_wet, p_grad, p_fresh, p_wind_e, p_wind_n = coefficients(fold)
    h, e, n = mine[HEIGHT], mine[EAST], mine[NORTH]
    p_h, p_e, p_n = fold[HEIGHT], fold[EAST], fold[NORTH]
    e_w, grad_w, wet_w, wind_w = (turn(x, 1, 1) for x in (e, grad, wet, wind_e))
    p_e_w, p_grad_w, p_wet_w, p_wind_w = (turn(x, -1, 1) for x in (p_e, p_grad, p_wet, p_wind_e))
    row_h = rows_of(h.shape)
    last = HALO + rows - 1
    across = (row_h == last) & top
    p_last = rows_of(p_h.shape) == HALO - 1
    for step in range(SUBSTEPS):
        if step == 4:
            row = rows_of((HALO, cols))
            for s, cut, at_row in ((0, hi, HALO - 1), (1, lo, 0)):
                for c in range(2):
                    for l in range(depth):
                        at = c * depth + l
                        add = jnp.broadcast_to(shift[s, at : at + 1], (HALO, cols))
                        x = x_ref[c, l, cut] + unit_ref[l, cut] * source[c][cut]
                        fixed[c, l, cut] = x + jnp.where(row == at_row, add, 0.0)
                send(fixed.at[:, :, cut], t_out.at[:, :, cut])
        h = (h - wave_div * ((e - e_w) + (n - turn(n, 1, 0)))) * wet + fresh
        p_h = (p_h - wave_div * ((p_e - p_e_w) + (p_n - turn(p_n, 1, 0)))) * p_wet + p_fresh
        h_n = jnp.where(across, jnp.broadcast_to(p_h[HALO - 1 :], h.shape), turn(h, -1, 0))
        p_h_n = jnp.where(p_last, jnp.broadcast_to(h[last : last + 1], p_h.shape), turn(p_h, -1, 0))
        e = (e - grad * (turn(h, -1, 1) - h)) * wet + wind_e
        n = (n - grad * (h_n - h)) * wet + wind_n
        p_e = (p_e - p_grad * (turn(p_h, 1, 1) - p_h)) * p_wet + p_wind_e
        p_n = (p_n - p_grad * (p_h_n - p_h)) * p_wet + p_wind_n
        e_w = (e_w - grad_w * (h - turn(h, 1, 1))) * wet_w + wind_w
        p_e_w = (p_e_w - p_grad_w * (p_h - turn(p_h, -1, 1))) * p_wet_w + p_wind_w
    inside = slice(HALO, HALO + rows)
    result[0] = h[inside, :cols]
    result[1] = e[inside, :cols]
    result[2] = n[inside, :cols]
    send(result.at[0], height_out)
    send(result.at[1:3], transport_out)

    for copy in copies:
        copy.wait()


def vmem(count):
    return [pl.BlockSpec(memory_space=pltpu.VMEM)] * count


def params(mib=24):
    return pltpu.CompilerParams(vmem_limit_bytes=mib * 1024 * 1024)


def work(mb):
    return pl.CostEstimate(flops=mb * 1000000, bytes_accessed=mb * 1000000, transcendentals=0)


def in_hbm(x):
    return pltpu.with_memory_space_constraint(x, pltpu.HBM)


def shape_of(*shape):
    return jax.ShapeDtypeStruct(shape, F32)


def lat_pairs(n_lat, n_lon):
    def at(i, j):
        return i * n_lon + j

    first, second = [], []
    for j in range(n_lon):
        for i in range(0, n_lat, 2):
            first += [(at(i, j), at(i + 1, j)), (at(i + 1, j), at(i, j))]
        for i in range(1, n_lat - 1, 2):
            second += [(at(i, j), at(i + 1, j)), (at(i + 1, j), at(i, j))]
        second.append((at(n_lat - 1, j), at(n_lat - 1, n_lon - 1 - j)))
    return first, second


def lon_pairs(n_lon):
    first, second = [], []
    for j in range(0, n_lon, 2):
        first += [(j, j + 1), (j + 1, j)]
        k, m = j + 1, (j + 2) % n_lon
        second += [(k, m), (m, k)]
    return first, second


def per_device(
    tracers,
    velocity,
    diffusivity,
    ocean_levels,
    surface_height,
    transport,
    atm_flux,
    send_rows,
    src_owner,
    src_slot,
    xgrid_weights,
    xgrid_count,
):
    n_lat, n_lon = lax.axis_size("lat"), lax.axis_size("lon")
    depth, rows, cols = tracers.shape[1:]
    slots = send_rows.shape[3]
    block = (rows, cols)
    picked, t_near, u_near, v_rows = pl.pallas_call(
        pick_kernel,
        out_shape=(
            shape_of(n_lon, 1, 10 * slots),
            shape_of(2, depth, *block),
            shape_of(depth, *block),
            shape_of(depth, HALO, cols),
        ),
        in_specs=[pl.BlockSpec(memory_space=pltpu.HBM)] * 4,
        out_specs=[pl.BlockSpec(memory_space=pltpu.HBM)] + vmem(3),
        scratch_shapes=[
            pltpu.VMEM(atm_flux.shape, F32),
            pltpu.VMEM(send_rows.shape, jnp.int32),
            pltpu.VMEM((n_lon, 1, 10 * slots), F32),
            pltpu.SemaphoreType.DMA((6,)),
        ],
        compiler_params=params(24),
        cost_estimate=work(40),
        name="pick",
    )(in_hbm(atm_flux), in_hbm(send_rows), in_hbm(tracers), in_hbm(velocity))
    table = lax.all_to_all(picked, "lon", split_axis=0, concat_axis=0, tiled=True)

    lat_rows = ROW_T + 3 * depth
    two, one, t_0, edge_rows, pick_row, pick_lane, used = pl.pallas_call(
        edge_kernel,
        out_shape=(
            shape_of(2 * rows, cols),
            shape_of(2 * rows, cols),
            shape_of(*block),
            shape_of(2, 3 * depth, cols),
            jax.ShapeDtypeStruct((4, *block), jnp.int32),
            jax.ShapeDtypeStruct((4, *block), jnp.int32),
            shape_of(4, *block),
        ),
        in_specs=[pl.BlockSpec(memory_space=pl.ANY)] + vmem(10),
        out_specs=vmem(7),
        compiler_params=params(),
        cost_estimate=work(2),
        name="edges",
    )(
        picked, v_rows, t_near, u_near, ocean_levels, surface_height, transport, src_owner, src_slot,
        xgrid_weights, xgrid_count,
    )
    pairs = lon_pairs(n_lon)
    two = lax.ppermute(two, "lon", pairs[1])
    one = lax.ppermute(one, "lon", pairs[0])

    solved, unit, inv_rows = pl.pallas_call(
        tracer_kernel,
        out_shape=(shape_of(2, depth, *block), shape_of(depth, *block), shape_of(2, depth, cols)),
        in_specs=vmem(7) + [pl.BlockSpec(memory_space=pltpu.HBM)],
        out_specs=vmem(3),
        scratch_shapes=[
            pltpu.VMEM((depth, *block), F32),
            pltpu.VMEM((2 * depth * rows, 2 * cols), jnp.bfloat16),
            pltpu.VMEM((2 * depth * rows, cols), F32),
            pltpu.VMEM((2 * depth * rows, cols), F32),
            pltpu.VMEM((depth, *block), F32),
            pltpu.SemaphoreType.DMA,
        ],
        compiler_params=params(),
        cost_estimate=work(8),
        name="tracers",
    )(two, one, t_0, ocean_levels, diffusivity, t_near, u_near, in_hbm(velocity))

    second, first, edge_flux, edge_rim, tab, side = pl.pallas_call(
        rim_lookup_kernel,
        out_shape=(
            shape_of(lat_rows, cols),
            shape_of(lat_rows, cols),
            shape_of(2, 3, HALO, cols),
            shape_of(2, 3, HALO, cols),
            shape_of(4, n_lon // 2, 128),
            shape_of(3, n_lon, 128),
        ),
        in_specs=vmem(10),
        out_specs=vmem(6),
        scratch_shapes=[pltpu.VMEM((2, lat_rows, cols), F32)],
        compiler_params=params(),
        cost_estimate=work(8),
        name="rim_lookup",
    )(
        table, two, one, pick_row, pick_lane, used, edge_rows, ocean_levels, surface_height, transport,
    )
    pairs = lat_pairs(n_lat, n_lon)
    second = lax.ppermute(second, ("lat", "lon"), pairs[1])
    first = lax.ppermute(first, ("lat", "lon"), pairs[0])

    flux, rim = pl.pallas_call(
        lookup_kernel,
        out_shape=(shape_of(4, *block), shape_of(FIELDS, *block)),
        in_specs=vmem(9),
        out_specs=vmem(2),
        compiler_params=params(),
        cost_estimate=work(8),
        name="lookup",
    )(edge_flux, edge_rim, tab, side, two, one, pick_row, pick_lane, used)

    return pl.pallas_call(
        step_kernel,
        out_shape=(shape_of(2, depth, rows, cols), shape_of(rows, cols), shape_of(2, rows, cols)),
        in_specs=vmem(12),
        out_specs=(pl.BlockSpec(memory_space=pl.ANY),) * 3,
        scratch_shapes=[
            pltpu.VMEM((lat_rows, cols), F32),
            pltpu.VMEM((2, 2 * depth, cols), F32),
            pltpu.VMEM((2, depth, rows, cols), F32),
            pltpu.VMEM((3, rows, cols), F32),
            pltpu.SemaphoreType.DMA((6,)),
        ],
        compiler_params=params(),
        name="step",
    )(
        second, first, surface_height, transport, ocean_levels, diffusivity, flux, rim, edge_rows, inv_rows,
        solved, unit,
    )


def solution(mesh):
    return jax.shard_map(
        per_device,
        mesh=mesh,
        in_specs=(
            P(None, None, "lat", "lon"),
            P(None, None, "lat", "lon"),
            P("lat", "lon"),
            P("lat", "lon"),
            P("lat", "lon"),
            P(None, "lat", "lon"),
            P("lat", None, "lon"),
            P("lat", "lon", None, None),
            P(None, "lat", "lon"),
            P(None, "lat", "lon"),
            P(None, "lat", "lon"),
            P("lat", "lon"),
        ),
        out_specs=(P(None, None, "lat", "lon"), P("lat", "lon"), P(None, "lat", "lon")),
        check_vma=False,
    )
```

```python
import jax
import jax.numpy as jnp
from jax import lax
from jax.experimental import pallas as pl
from jax.experimental.pallas import tpu as pltpu
from jax.sharding import PartitionSpec as P

SUBSTEPS = 6
HALO = 8
FIELDS = 7
HEIGHT, EAST, NORTH, LEVELS, FRESH, WIND_E, WIND_N = range(FIELDS)
ROW_RIM = FIELDS * HALO
ROW_T = ROW_RIM + HALO
LISTS = 256
OWNER, SLOT, USED = 32, 64, 96

adv_rate = 0.1
heat_gain = 0.5
salt_gain = 0.5
wave_div = 0.5
wave_grad = 0.8
fresh_gain = 0.2
wind_gain = 0.2

F32 = jnp.float32


def lanes(shape):
    return lax.broadcasted_iota(jnp.int32, shape, len(shape) - 1)


def rows_of(shape):
    return lax.broadcasted_iota(jnp.int32, shape, len(shape) - 2)


def turn(x, by, axis):
    size = x.shape[axis]
    by = by % size
    return x if by == 0 else pltpu.roll(x, by, axis)


def is_even(axis):
    return lax.rem(lax.axis_index(axis), 2) == 0


def is_top():
    return lax.axis_index("lat") == lax.axis_size("lat") - 1


def pick_kernel(
    atm_hbm, rows_hbm, t_hbm, v_hbm, out_hbm, t_ref, u_ref, v_rows, atm_ref, rows_ref, out_ref, sems,
):
    last = t_ref.shape[2] - HALO
    copies = [
        pltpu.make_async_copy(atm_hbm, atm_ref, sems.at[0]),
        pltpu.make_async_copy(rows_hbm, rows_ref, sems.at[1]),
        pltpu.make_async_copy(t_hbm, t_ref, sems.at[2]),
        pltpu.make_async_copy(v_hbm.at[0], u_ref, sems.at[3]),
        pltpu.make_async_copy(v_hbm.at[1, :, last:], v_rows, sems.at[4]),
    ]
    for copy in copies:
        copy.start()
    for copy in copies[:2]:
        copy.wait()
    rows = rows_ref[0, 0]
    both = jnp.concatenate([rows, rows], axis=1)
    lane = both & 127
    part = both >> 7
    low = lanes(both.shape) < 64
    values = []
    for f in range(4):
        acc = None
        for k in range(atm_ref.shape[2] // 128):
            row = jnp.broadcast_to(atm_ref[0, f : f + 1, k * 128 : (k + 1) * 128], both.shape)
            value = jnp.take_along_axis(row, lane, axis=1)
            acc = value if k == 0 else jnp.where(part == k, value, acc)
        values.append(acc)
    out_ref[:, 0, 0:128] = jnp.where(low, values[0], values[1])
    out_ref[:, 0, 128:256] = jnp.where(low, values[2], values[3])
    for f in range(1, 4):
        at = 128 + f * 128
        out_ref[:, 0, at : at + 128] = jnp.where(low, turn(values[f], -1, 0), turn(values[f], 1, 0))
    copies.append(pltpu.make_async_copy(out_ref, out_hbm, sems.at[5]))
    copies[-1].start()
    for copy in copies[2:]:
        copy.wait()


def edge_kernel(
    picked_ref, v_rows, t_ref, u_ref, level_ref, height_ref, transport_ref, owner_ref, slot_ref, weight_ref, count_ref,
    two_ref, one_ref, t_0_ref, rows_ref, pick_row_ref, pick_lane_ref, used_ref,
):
    depth, rows, cols = t_ref.shape[1:]
    shape = (rows, cols)
    lane = lanes(shape)
    level = level_ref[...]
    half = lax.axis_size("lon") // 2
    count = count_ref[...]
    for k in range(owner_ref.shape[0]):
        owner = owner_ref[k]
        high = owner >= half
        pick_row_ref[k] = jnp.where(high, owner - half, owner)
        pick_lane_ref[k] = jnp.where(high, slot_ref[k] + 64, slot_ref[k])
        used_ref[k] = jnp.where(count > k, weight_ref[k], 0.0)
    fields = [height_ref[...], transport_ref[0], transport_ref[1], level.astype(F32)]
    fields += [owner_ref[k].astype(F32) for k in range(4)]
    fields += [slot_ref[k].astype(F32) for k in range(4)]
    fields += [used_ref[k] for k in range(4)]
    west = jnp.zeros(shape, F32)
    east = jnp.zeros(shape, F32)
    for g, field in enumerate(fields):
        here = (lane >= g * HALO) & (lane < (g + 1) * HALO)
        west = jnp.where(here, turn(field, g * HALO, 1), west)
        east = jnp.where(here, turn(field, (g + 1) * HALO, 1), east)
    west_t = jnp.zeros(shape, F32)
    east_t = jnp.zeros(shape, F32)
    for c in range(2):
        for l in range(depth):
            f = c * depth + l
            moved = turn(t_ref[c, l], f + 1, 1)
            west_t = jnp.where(lane == f + 1, moved, west_t)
            east_t = jnp.where(lane == f, moved, east_t)
    for l in range(depth):
        at = 2 * depth + l
        east_t = jnp.where(lane == at, turn(u_ref[l], at + 1, 1), east_t)
    even = is_even("lon")
    one_ref[:rows] = jnp.where(even, east, west)
    two_ref[:rows] = jnp.where(even, west, east)
    one_ref[rows:] = jnp.where(even, east_t, west_t)
    two_ref[rows:] = jnp.where(even, west_t, east_t)
    t_0_ref[...] = turn(west_t, -1, 1)
    for c in range(2):
        for l in range(depth):
            at = c * depth + l
            rows_ref[0, at : at + 1] = t_ref[c, l, rows - 1 : rows]
            rows_ref[1, at : at + 1] = t_ref[c, l, 0:1]
    for l in range(depth):
        at = 2 * depth + l
        rows_ref[0, at : at + 1] = v_rows[l, HALO - 1 : HALO]
    rows_ref[1, 2 * depth :] = jnp.zeros((depth, cols), F32)

def own_lookup(tab, row_ref, lane_ref, used_ref, cut, fields):
    total = {f: None for f in fields}
    for k in range(used_ref.shape[0]):
        lane = lane_ref[k, cut]
        row = row_ref[k, cut]
        acc = {}
        for r in range(tab.shape[1]):
            here = row == r
            for f in fields:
                source = jnp.broadcast_to(tab[f, r : r + 1, :], lane.shape)
                value = jnp.take_along_axis(source, lane, axis=1)
                acc[f] = value if r == 0 else jnp.where(here, value, acc[f])
        used = used_ref[k, cut]
        for f in fields:
            total[f] = acc[f] * used if k == 0 else total[f] + acc[f] * used
    return total


def rim_of(east, west, by_east, by_west):
    lane = lanes(east.shape)
    outer = jnp.where(lane >= 128 - HALO, turn(west, by_west, 1), 0.0)
    return jnp.where(lane < HALO, turn(east, by_east, 1), outer)


def from_lon(one_ref, two_ref, cut):
    even = is_even("lon")
    one, two = one_ref[cut], two_ref[cut]
    return jnp.where(even, one, two), jnp.where(even, two, one)


def state_rims(east, west):
    return [rim_of(east, west, -g * HALO, 128 - (g + 1) * HALO) for g in range(4)]


def side_lookup(side, sides):
    (east, west), (east_2, west_2) = sides
    lane = lanes(east.shape)
    quarter = lane >> 5

    def gathered(by):
        parts = (turn(west_2, -32 - by, 1), turn(east, -by, 1), turn(west, 32 - by, 1), turn(east_2, 64 - by, 1))
        low = jnp.where(quarter == 0, parts[0], parts[1])
        return jnp.where(quarter < 2, low, jnp.where(quarter == 2, parts[2], parts[3]))

    owner = gathered(0).astype(jnp.int32)
    slot = gathered(32).astype(jnp.int32)
    used = gathered(64)
    slot = jnp.where((quarter & 1) == 0, slot + 64, slot)
    acc = [None] * 3
    for r in range(side.shape[1]):
        here = owner == r
        for f in range(3):
            source = jnp.broadcast_to(side[f, r : r + 1, :], slot.shape)
            value = jnp.take_along_axis(source, slot, axis=1)
            acc[f] = value if r == 0 else jnp.where(here, value, acc[f])
    rims = ([], [])
    for f in range(3):
        v = acc[f] * used
        v = v + turn(v, -16, 1)
        v = v + turn(v, -8, 1)
        rims[0].append(rim_of(v, v, -32, 56))
        rims[1].append(rim_of(v, v, -96, 120))
    return rims


def rim_lookup_kernel(
    table_ref, two_ref, one_ref, pick_row_ref, pick_lane_ref, used_ref, rows_ref, level_ref, height_ref,
    transport_ref, second_ref, first_ref, flux_ref, rim_ref, tab, side, pack,
):
    n_lon = table_ref.shape[0]
    half = n_lon // 2
    rows, cols = height_ref.shape
    low = lanes((half, 128)) < 64
    for pair in range(2):
        part = table_ref[:, 0, pair * 128 : (pair + 1) * 128]
        lo, hi = part[:half], part[half:]
        tab[2 * pair] = jnp.where(low, lo, turn(hi, 64, 1))
        tab[2 * pair + 1] = jnp.where(low, turn(lo, 64, 1), hi)
    for f in range(3):
        side[f] = table_ref[:, 0, LISTS + f * 128 : LISTS + (f + 1) * 128]
    lane = lanes((HALO, cols))
    cuts = (slice(rows - HALO, rows), slice(0, HALO))
    sides = [from_lon(one_ref, two_ref, cut) for cut in cuts]
    side_rims = side_lookup(side, sides)
    for s, cut in enumerate(cuts):
        found = own_lookup(tab, pick_row_ref, pick_lane_ref, used_ref, cut, (1, 2, 3))
        for f in range(3):
            flux_ref[s, f] = found[f + 1]
            rim_ref[s, f] = side_rims[s][f]
        rims = state_rims(*sides[s]) + side_rims[s]
        own = [
            height_ref[cut], transport_ref[0, cut], transport_ref[1, cut], level_ref[cut].astype(F32),
            found[1], found[2], found[3],
        ]
        packed = jnp.zeros((HALO, cols), F32)
        for i in range(FIELDS):
            pack[s, i * HALO : (i + 1) * HALO] = own[i]
            start = 2 * HALO * i
            here = (lane >= start) & (lane < start + 2 * HALO)
            packed = jnp.where(here, turn(rims[i], start + HALO, 1), packed)
        pack[s, ROW_RIM:ROW_T] = packed
        pack[s, ROW_T:] = rows_ref[s]
    even = is_even("lat")
    north_going, south_going = pack[0], pack[1]
    second_ref[...] = jnp.where(even, south_going, north_going)
    first_ref[...] = jnp.where(even, north_going, south_going)


def lookup_kernel(
    edge_flux_ref, edge_rim_ref, tab, side, two_ref, one_ref, pick_row_ref, pick_lane_ref, used_ref,
    flux_ref, rim_ref,
):
    rows = used_ref.shape[1]
    cuts = [slice(at, at + HALO) for at in range(0, rows, HALO)]
    sides = [from_lon(one_ref, two_ref, cut) for cut in cuts]
    for at in range(1, len(cuts) - 1, 2):
        side_rims = side_lookup(side, sides[at : at + 2])
        for i in range(2):
            cut = cuts[at + i]
            found = own_lookup(tab, pick_row_ref, pick_lane_ref, used_ref, cut, (0, 1, 2, 3))
            for f in range(4):
                flux_ref[f, cut] = found[f]
            for g, rim in enumerate(state_rims(*sides[at + i]) + side_rims[i]):
                rim_ref[g, cut] = rim
    for s, at in ((0, len(cuts) - 1), (1, 0)):
        cut = cuts[at]
        flux_ref[0, cut] = own_lookup(tab, pick_row_ref, pick_lane_ref, used_ref, cut, (0,))[0]
        for f in range(3):
            flux_ref[f + 1, cut] = edge_flux_ref[s, f]
        for g, rim in enumerate(state_rims(*sides[at]) + [edge_rim_ref[s, f] for f in range(3)]):
            rim_ref[g, cut] = rim


def split(x):
    hi = x.astype(jnp.bfloat16)
    return hi, (x - hi.astype(F32)).astype(jnp.bfloat16)


def tracer_kernel(
    two_ref, one_ref, t_0_ref, level_ref, diff_ref, t_ref, u_ref, v_hbm, x_ref, unit_ref, inv_rows_ref, gain_ref,
    parts, rims, net_x, v_ref, sem,
):
    depth, rows, cols = t_ref.shape[1:]
    copy = pltpu.make_async_copy(v_hbm.at[1], v_ref, sem)
    copy.start()
    shape = (rows, cols)
    east, west = from_lon(one_ref, two_ref, slice(0, rows))
    t_e, t_w = from_lon(one_ref, two_ref, slice(rows, 2 * rows))
    level = level_ref[...]
    level_f = level.astype(F32)
    lane = lanes(shape)
    row = rows_of(shape)
    first = LEVELS * HALO
    last = cols - 1
    level_e = jnp.where(lane == last, turn(east, last - first, 1), turn(level_f, -1, 1))
    level_n = turn(level_f, -1, 0)
    face_e = jnp.minimum(level_f, level_e)
    face_n = jnp.where(row == rows - 1, 0.0, jnp.minimum(level_f, level_n))
    t_0 = t_0_ref[...]
    u_w = jnp.where(lane < depth, turn(t_w, -2 * depth, 1), turn(t_w, -depth, 1))
    layer = jnp.where(lane < depth, lane, lane - depth).astype(F32)
    level_w = west[:, first + HALO - 1 : first + HALO]
    face_w = jnp.broadcast_to(jnp.minimum(level_f[:, 0:1], level_w), shape)
    west_flux = jnp.where((layer < face_w) & (lane < 2 * depth), u_w * ((t_w + t_0) * 0.5), 0.0)
    both = []
    for x in (turn(t_e, -1, 1), west_flux):
        hi, lo = split(x)
        both.append(jnp.where(lane < 64, hi.astype(F32), turn(lo.astype(F32), 64, 1)))
    plane = lane & 63
    for f in range(2 * depth):
        at = slice(f * rows, (f + 1) * rows)
        here = plane == f
        parts[at, 0:128] = jnp.where(here, both[0], 0.0).astype(jnp.bfloat16)
        parts[at, 128:256] = jnp.where(here, both[1], 0.0).astype(jnp.bfloat16)
    k = lax.broadcasted_iota(jnp.int32, (2 * cols, cols), 0)
    into = jnp.where(k < cols, last, 0) == lanes((2 * cols, cols))
    rims[...] = jnp.dot(parts[...], into.astype(F32).astype(jnp.bfloat16), preferred_element_type=F32)
    for l in range(depth):
        mask_e = face_e > l
        u_l = u_ref[l] * 0.5
        for c in range(2):
            f = c * depth + l
            at = slice(f * rows, (f + 1) * rows)
            t = t_ref[c, l]
            t_east = jnp.where(lane == last, rims[at], turn(t, -1, 1))
            flux_e = jnp.where(mask_e, u_l * (t + t_east), 0.0)
            net_x[at] = flux_e - jnp.where(lane == 0, rims[at], turn(flux_e, 1, 1))
    copy.wait()
    diff = diff_ref[...]
    above = jnp.zeros(shape, F32)
    inv = None
    right = [None, None, None]
    for l in range(depth):
        below = jnp.where(level > l + 1, diff, 0.0) if l < depth - 1 else jnp.zeros(shape, F32)
        pivot = 1.0 + above + below
        if l > 0:
            pivot = pivot - above * above * inv
        inv = 1.0 / pivot
        inv_rows_ref[0, l : l + 1] = inv[rows - 1 : rows]
        inv_rows_ref[1, l : l + 1] = inv[0:1]
        gain_ref[l] = below * inv
        mask_n = face_n > l
        v_l = v_ref[l] * 0.5
        for c in range(2):
            f = c * depth + l
            at = slice(f * rows, (f + 1) * rows)
            t = t_ref[c, l]
            flux_n = jnp.where(mask_n, v_l * (t + turn(t, -1, 0)), 0.0)
            flux_s = turn(flux_n, 1, 0)
            forced = t - adv_rate * (net_x[at] + (flux_n - flux_s))
            right[c] = forced * inv if l == 0 else (forced + above * right[c]) * inv
            x_ref[c, l] = right[c]
        right[2] = inv if l == 0 else above * right[2] * inv
        unit_ref[l] = right[2]
        above = below
    for l in range(depth - 2, -1, -1):
        gain = gain_ref[l]
        for c in range(2):
            right[c] = x_ref[c, l] + gain * right[c]
            x_ref[c, l] = right[c]
        right[2] = unit_ref[l] + gain * right[2]
        unit_ref[l] = right[2]


def step_kernel(
    second_ref, first_ref, height_ref, transport_ref, level_ref, diff_ref, flux_ref, rim_ref, rows_ref, inv_rows_ref,
    x_ref, unit_ref, t_out, height_out, transport_out, shift, fixed, result, sems,
):
    top = is_top()
    level = level_ref[...]
    level_f = level.astype(F32)
    rows, cols = level.shape
    depth = x_ref.shape[1]
    wet_0 = (level > 0).astype(F32)
    source = (heat_gain * flux_ref[0] * wet_0, -salt_gain * flux_ref[1] * wet_0)
    lo, hi = slice(0, HALO), slice(rows - HALO, rows)
    mid = slice(HALO, rows - HALO)
    copies = []

    def send(value, out):
        copies.append(pltpu.make_async_copy(value, out, sems.at[len(copies)]))
        copies[-1].start()

    for c in range(2):
        for l in range(depth):
            fixed[c, l, mid] = x_ref[c, l, mid] + unit_ref[l, mid] * source[c][mid]
        send(fixed.at[c, :, mid], t_out.at[c, :, mid])
    even = is_even("lat")
    a, b = first_ref[...], second_ref[...]
    south = jnp.where(even, b, a)
    north = jnp.where(even, a, b)
    used = ROW_T + 2 * depth
    mirrored = jnp.take_along_axis(north[:used], 127 - lanes((used, cols)), axis=1)
    north = jnp.where(top, mirrored, north[:used])

    first = LEVELS * HALO
    level_n = jnp.where(top, north[first + HALO - 1 : first + HALO], north[first : first + 1])
    level_s = south[first + HALO - 1 : first + HALO]
    sides = ((north, level_n, rows - 1, -adv_rate), (south, level_s, 0, adv_rate))
    chains = []
    for s, (message, level_out, at, gain) in enumerate(sides):
        level_in = level_f[at : at + 1]
        face = jnp.minimum(level_in, level_out)
        speed = rows_ref[0, 2 * depth :] if s == 0 else message[ROW_T + 2 * depth :]
        for c in range(2):
            planes = slice(c * depth, (c + 1) * depth)
            outside = message[ROW_T + c * depth : ROW_T + (c + 1) * depth]
            flux = speed * ((outside + rows_ref[s, planes]) * 0.5)
            deep = rows_of(flux.shape).astype(F32) < face
            shift[s, planes] = jnp.where(deep, gain * flux, 0.0)
            chains.append((s, c, level_in, diff_ref[at : at + 1]))
    right = [None] * 4
    for l in range(depth):
        for i, (s, c, level_in, diff_in) in enumerate(chains):
            at = c * depth + l
            inv = inv_rows_ref[s, l : l + 1]
            value = shift[s, at : at + 1]
            if l > 0:
                value = value + jnp.where(level_in > l, diff_in, 0.0) * right[i]
            right[i] = value * inv
            shift[s, at : at + 1] = right[i]
    for l in range(depth - 2, -1, -1):
        for i, (s, c, level_in, diff_in) in enumerate(chains):
            at = c * depth + l
            inv = inv_rows_ref[s, l : l + 1]
            below = jnp.where(level_in > l + 1, diff_in, 0.0) * inv
            right[i] = shift[s, at : at + 1] + below * right[i]
            shift[s, at : at + 1] = right[i]
    own = (
        height_ref[...], transport_ref[0], transport_ref[1], level_f,
        flux_ref[1], flux_ref[2], flux_ref[3],
    )
    ext = []
    lane = lanes((HALO, cols))
    side = (lane < HALO) | (lane >= cols - HALO)
    for i in range(FIELDS):
        at = slice(i * HALO, (i + 1) * HALO)
        whole = jnp.concatenate([south[at], own[i], north[at]], axis=0)
        start = jnp.where(top, cols - 2 * HALO * (FIELDS - i) - HALO, cols - 2 * HALO * i - HALO)
        north_rim = jnp.where(side, pltpu.roll(north[ROW_RIM:ROW_T], start, 1), 0.0)
        south_rim = jnp.where(side, turn(south[ROW_RIM:ROW_T], -(2 * HALO * i + HALO), 1), 0.0)
        rim = jnp.concatenate([south_rim, rim_ref[i], north_rim], axis=0)
        ext.append(jnp.concatenate([whole, rim], axis=1))


    def coefficients(f):
        wet = (f[LEVELS] > 0.0).astype(F32)
        return (
            wet,
            wave_grad * (f[LEVELS] / depth),
            fresh_gain * f[FRESH] * wet,
            wind_gain * f[WIND_E] * wet,
            wind_gain * f[WIND_N] * wet,
        )

    mine = [x for x in ext]
    fold = [x[HALO + rows :] for x in ext]
    wet, grad, fresh, wind_e, wind_n = coefficients(mine)
    p_wet, p_grad, p_fresh, p_wind_e, p_wind_n = coefficients(fold)
    h, e, n = mine[HEIGHT], mine[EAST], mine[NORTH]
    p_h, p_e, p_n = fold[HEIGHT], fold[EAST], fold[NORTH]
    e_w, grad_w, wet_w, wind_w = (turn(x, 1, 1) for x in (e, grad, wet, wind_e))
    p_e_w, p_grad_w, p_wet_w, p_wind_w = (turn(x, -1, 1) for x in (p_e, p_grad, p_wet, p_wind_e))
    row_h = rows_of(h.shape)
    last = HALO + rows - 1
    across = (row_h == last) & top
    p_last = rows_of(p_h.shape) == HALO - 1
    for step in range(SUBSTEPS):
        if step == 4:
            row = rows_of((HALO, cols))
            for s, cut, at_row in ((0, hi, HALO - 1), (1, lo, 0)):
                for c in range(2):
                    for l in range(depth):
                        at = c * depth + l
                        add = jnp.broadcast_to(shift[s, at : at + 1], (HALO, cols))
                        x = x_ref[c, l, cut] + unit_ref[l, cut] * source[c][cut]
                        fixed[c, l, cut] = x + jnp.where(row == at_row, add, 0.0)
                send(fixed.at[:, :, cut], t_out.at[:, :, cut])
        h = (h - wave_div * ((e - e_w) + (n - turn(n, 1, 0)))) * wet + fresh
        p_h = (p_h - wave_div * ((p_e - p_e_w) + (p_n - turn(p_n, 1, 0)))) * p_wet + p_fresh
        h_n = jnp.where(across, jnp.broadcast_to(p_h[HALO - 1 :], h.shape), turn(h, -1, 0))
        p_h_n = jnp.where(p_last, jnp.broadcast_to(h[last : last + 1], p_h.shape), turn(p_h, -1, 0))
        e = (e - grad * (turn(h, -1, 1) - h)) * wet + wind_e
        n = (n - grad * (h_n - h)) * wet + wind_n
        p_e = (p_e - p_grad * (turn(p_h, 1, 1) - p_h)) * p_wet + p_wind_e
        p_n = (p_n - p_grad * (p_h_n - p_h)) * p_wet + p_wind_n
        e_w = (e_w - grad_w * (h - turn(h, 1, 1))) * wet_w + wind_w
        p_e_w = (p_e_w - p_grad_w * (p_h - turn(p_h, -1, 1))) * p_wet_w + p_wind_w
    inside = slice(HALO, HALO + rows)
    result[0] = h[inside, :cols]
    result[1] = e[inside, :cols]
    result[2] = n[inside, :cols]
    send(result.at[0], height_out)
    send(result.at[1:3], transport_out)

    for copy in copies:
        copy.wait()


def vmem(count):
    return [pl.BlockSpec(memory_space=pltpu.VMEM)] * count


def params(mib=24):
    return pltpu.CompilerParams(vmem_limit_bytes=mib * 1024 * 1024)


def work(mb):
    return pl.CostEstimate(flops=mb * 1000000, bytes_accessed=mb * 1000000, transcendentals=0)


def in_hbm(x):
    return pltpu.with_memory_space_constraint(x, pltpu.HBM)


def shape_of(*shape):
    return jax.ShapeDtypeStruct(shape, F32)


def lat_pairs(n_lat, n_lon):
    def at(i, j):
        return i * n_lon + j

    first, second = [], []
    for j in range(n_lon):
        for i in range(0, n_lat, 2):
            first += [(at(i, j), at(i + 1, j)), (at(i + 1, j), at(i, j))]
        for i in range(1, n_lat - 1, 2):
            second += [(at(i, j), at(i + 1, j)), (at(i + 1, j), at(i, j))]
        second.append((at(n_lat - 1, j), at(n_lat - 1, n_lon - 1 - j)))
    return first, second


def lon_pairs(n_lon):
    first, second = [], []
    for j in range(0, n_lon, 2):
        first += [(j, j + 1), (j + 1, j)]
        k, m = j + 1, (j + 2) % n_lon
        second += [(k, m), (m, k)]
    return first, second


def per_device(
    tracers,
    velocity,
    diffusivity,
    ocean_levels,
    surface_height,
    transport,
    atm_flux,
    send_rows,
    src_owner,
    src_slot,
    xgrid_weights,
    xgrid_count,
):
    n_lat, n_lon = lax.axis_size("lat"), lax.axis_size("lon")
    depth, rows, cols = tracers.shape[1:]
    slots = send_rows.shape[3]
    block = (rows, cols)
    picked, t_near, u_near, v_rows = pl.pallas_call(
        pick_kernel,
        out_shape=(
            shape_of(n_lon, 1, 10 * slots),
            shape_of(2, depth, *block),
            shape_of(depth, *block),
            shape_of(depth, HALO, cols),
        ),
        in_specs=[pl.BlockSpec(memory_space=pltpu.HBM)] * 4,
        out_specs=[pl.BlockSpec(memory_space=pltpu.HBM)] + vmem(3),
        scratch_shapes=[
            pltpu.VMEM(atm_flux.shape, F32),
            pltpu.VMEM(send_rows.shape, jnp.int32),
            pltpu.VMEM((n_lon, 1, 10 * slots), F32),
            pltpu.SemaphoreType.DMA((6,)),
        ],
        compiler_params=params(24),
        cost_estimate=work(40),
        name="pick",
    )(in_hbm(atm_flux), in_hbm(send_rows), in_hbm(tracers), in_hbm(velocity))
    table = lax.all_to_all(picked, "lon", split_axis=0, concat_axis=0, tiled=True)

    lat_rows = ROW_T + 3 * depth
    two, one, t_0, edge_rows, pick_row, pick_lane, used = pl.pallas_call(
        edge_kernel,
        out_shape=(
            shape_of(2 * rows, cols),
            shape_of(2 * rows, cols),
            shape_of(*block),
            shape_of(2, 3 * depth, cols),
            jax.ShapeDtypeStruct((4, *block), jnp.int32),
            jax.ShapeDtypeStruct((4, *block), jnp.int32),
            shape_of(4, *block),
        ),
        in_specs=[pl.BlockSpec(memory_space=pl.ANY)] + vmem(10),
        out_specs=vmem(7),
        compiler_params=params(),
        cost_estimate=work(2),
        name="edges",
    )(
        picked, v_rows, t_near, u_near, ocean_levels, surface_height, transport, src_owner, src_slot,
        xgrid_weights, xgrid_count,
    )
    pairs = lon_pairs(n_lon)
    two = lax.ppermute(two, "lon", pairs[1])
    one = lax.ppermute(one, "lon", pairs[0])

    solved, unit, inv_rows = pl.pallas_call(
        tracer_kernel,
        out_shape=(shape_of(2, depth, *block), shape_of(depth, *block), shape_of(2, depth, cols)),
        in_specs=vmem(7) + [pl.BlockSpec(memory_space=pltpu.HBM)],
        out_specs=vmem(3),
        scratch_shapes=[
            pltpu.VMEM((depth, *block), F32),
            pltpu.VMEM((2 * depth * rows, 2 * cols), jnp.bfloat16),
            pltpu.VMEM((2 * depth * rows, cols), F32),
            pltpu.VMEM((2 * depth * rows, cols), F32),
            pltpu.VMEM((depth, *block), F32),
            pltpu.SemaphoreType.DMA,
        ],
        compiler_params=params(),
        cost_estimate=work(8),
        name="tracers",
    )(two, one, t_0, ocean_levels, diffusivity, t_near, u_near, in_hbm(velocity))

    second, first, edge_flux, edge_rim, tab, side = pl.pallas_call(
        rim_lookup_kernel,
        out_shape=(
            shape_of(lat_rows, cols),
            shape_of(lat_rows, cols),
            shape_of(2, 3, HALO, cols),
            shape_of(2, 3, HALO, cols),
            shape_of(4, n_lon // 2, 128),
            shape_of(3, n_lon, 128),
        ),
        in_specs=vmem(10),
        out_specs=vmem(6),
        scratch_shapes=[pltpu.VMEM((2, lat_rows, cols), F32)],
        compiler_params=params(),
        cost_estimate=work(8),
        name="rim_lookup",
    )(
        table, two, one, pick_row, pick_lane, used, edge_rows, ocean_levels, surface_height, transport,
    )
    pairs = lat_pairs(n_lat, n_lon)
    second = lax.ppermute(second, ("lat", "lon"), pairs[1])
    first = lax.ppermute(first, ("lat", "lon"), pairs[0])

    flux, rim = pl.pallas_call(
        lookup_kernel,
        out_shape=(shape_of(4, *block), shape_of(FIELDS, *block)),
        in_specs=vmem(9),
        out_specs=vmem(2),
        compiler_params=params(),
        cost_estimate=work(8),
        name="lookup",
    )(edge_flux, edge_rim, tab, side, two, one, pick_row, pick_lane, used)

    return pl.pallas_call(
        step_kernel,
        out_shape=(shape_of(2, depth, rows, cols), shape_of(rows, cols), shape_of(2, rows, cols)),
        in_specs=vmem(12),
        out_specs=(pl.BlockSpec(memory_space=pl.ANY),) * 3,
        scratch_shapes=[
            pltpu.VMEM((2, 2 * depth, cols), F32),
            pltpu.VMEM((2, depth, rows, cols), F32),
            pltpu.VMEM((3, rows, cols), F32),
            pltpu.SemaphoreType.DMA((6,)),
        ],
        compiler_params=params(),
        name="step",
    )(
        second, first, surface_height, transport, ocean_levels, diffusivity, flux, rim, edge_rows, inv_rows,
        solved, unit,
    )


def solution(mesh):
    return jax.shard_map(
        per_device,
        mesh=mesh,
        in_specs=(
            P(None, None, "lat", "lon"),
            P(None, None, "lat", "lon"),
            P("lat", "lon"),
            P("lat", "lon"),
            P("lat", "lon"),
            P(None, "lat", "lon"),
            P("lat", None, "lon"),
            P("lat", "lon", None, None),
            P(None, "lat", "lon"),
            P(None, "lat", "lon"),
            P(None, "lat", "lon"),
            P("lat", "lon"),
        ),
        out_specs=(P(None, None, "lat", "lon"), P("lat", "lon"), P(None, "lat", "lon")),
        check_vma=False,
    )
```
